32 devices in a mesh: scen: 4 (over y, core), fac: 8 (over z, x).
Axes of the slice: x: 2, y: 2, z: 4, core: 2. Of those that a mesh axis runs over, the one named last changes fastest.
Arguments:
- shocks: bfloat16 [2, 1024, 256], P(None, 'scen'), may hold values from -6 to 6
- loadings: bfloat16 [256, 2048], P(None, 'fac'), may hold values from -0.375 to 0.375
- vol: float32 [2048], P('fac'), may hold values from 0.1 to 0.5
- jump_counts: int32 [2, 1024, 2048], P(None, 'scen', 'fac'), may hold values from 0 to 3
- jump_noise: bfloat16 [2, 1024, 2048], P(None, 'scen', 'fac'), may hold values from -6 to 6
- jump_mean: float32 [2048], P('fac'), may hold values from -0.15 to 0.1
- jump_vol: float32 [2048], P('fac'), may hold values from 0.05 to 0.3
- dependencies: int32 [2048, 2], P('fac'), may hold values from 0 to 15, as said below
- block_slot: int32 [16], replicated, may hold values from 0 to 15, each once
- trade_weights: bfloat16 [2048, 2, 128], P('fac'), may hold values from -0.375 to 0.375
- netting: int32 [2048], P('fac'), may hold values from 0 to 511
Outputs:
- exposure: float32 [2, 512, 1024], P(None, 'fac', 'scen')
- expected: float32 [2, 512], P(None, 'fac')
The draws below stay inside these ranges and needn't reach their ends.
Inputs may be any that keep to these rules, and one draw needn't show every extreme that they name: `dependencies`: each trade names 2 different blocks.
All inputs are finite; a program needn't handle non-finite values.
Results may differ from the reference program's by a relative error of at most 0.0056.
Values may be sent and summed in bfloat16 or wider, within the bound.
No kernel may reach another device: no remote copies, remote signals or barrier semaphores. Data moves between devices by JAX's collectives and lax.ppermute only.
A program may use at most 192 MiB of HBM per device.

```python
import math
import jax
import jax.numpy as jnp
from jax import lax

SHOCKS = 256
BLOCK = 128
DEPS = 2
DATES = 2
SCENARIOS = 1024
FACTORS = 2048
NBLOCKS = 16
TRADES = 2048
NSETS = 512


def draw_dependencies(key, part):
    key = jax.random.fold_in(key, 11)
    heat_key, score_key = jax.random.split(key)
    heat = jax.random.randint(heat_key, (NBLOCKS,), 0, 4)
    scores = jax.random.randint(score_key, (TRADES, NBLOCKS), 0, 65536) + heat[None, :] * 16384
    scores = scores * NBLOCKS + jnp.arange(NBLOCKS, dtype=jnp.int32)[None, :]
    return lax.top_k(scores, DEPS)[1].astype(jnp.int32)


def plant(values, stream_key, low, high):
    place = [jax.random.randint(jax.random.fold_in(stream_key, axis), (), 0, length) for axis, length in enumerate(values.shape)]
    widest = values.shape.index(max(values.shape))
    beside = place[:widest] + [(place[widest] + 1) % values.shape[widest]] + place[widest + 1:]
    return values.at[tuple(place)].set(low).at[tuple(beside)].set(high)


def block_levels(key, dims, pieces, least, high):
    def one(axis_at, shards_of):
        heights = jax.random.uniform(jax.random.fold_in(jax.random.fold_in(key, 6), axis_at), (shards_of,), jnp.float32, least / len(pieces), high / len(pieces))
        return jnp.repeat(jnp.exp(heights), dims[axis_at] // shards_of).reshape((-1,) + (1,) * (len(dims) - axis_at - 1))

    factor_of = one(*pieces[0])
    for cut in pieces[1:]:
        factor_of = factor_of * one(*cut)
    return factor_of


def gaussian(rng, shape, width, most, cuts=(), kind=jnp.bfloat16):
    values = width * jax.random.normal(rng, shape, jnp.float32)
    if cuts:
        values = values * block_levels(rng, shape, cuts, -0.22, 0.18)
    return jnp.clip(values, -most, most).astype(kind)


def setup_inputs(seed: int = 0) -> dict:
    arg_keys = jax.random.split(jax.random.key(seed), 12)
    shocks = gaussian(arg_keys[0], (DATES, SCENARIOS, SHOCKS), 1.0, 6.0, ((1, 4),))
    loadings = gaussian(arg_keys[1], (SHOCKS, FACTORS), SHOCKS ** -0.5, 0.375, ((1, 8),))
    vol = jnp.clip(jnp.exp(math.log(0.5) - 1.609438 * jax.random.uniform(arg_keys[2], (FACTORS,), jnp.float32) ** block_levels(arg_keys[2], (FACTORS,), ((0, 8),), -0.2, 0.2)), 0.1, 0.5)
    jump_counts = plant(jax.random.randint(arg_keys[3], (DATES, SCENARIOS, FACTORS), 0, 4), jax.random.fold_in(arg_keys[3], 1), 0, 3).astype(jnp.int32)
    jump_noise = gaussian(arg_keys[4], (DATES, SCENARIOS, FACTORS), 1.0, 6.0, ((1, 4), (2, 8)))
    jump_mean = jnp.clip(-0.15 + 0.25 * jax.random.uniform(arg_keys[5], (FACTORS,), jnp.float32) ** block_levels(arg_keys[5], (FACTORS,), ((0, 8),), -0.2, 0.2), -0.15, 0.1)
    jump_vol = jnp.clip(jnp.exp(math.log(0.3) - 1.7917595 * jax.random.uniform(arg_keys[6], (FACTORS,), jnp.float32) ** block_levels(arg_keys[6], (FACTORS,), ((0, 8),), -0.2, 0.2)), 0.05, 0.3)
    dependencies = draw_dependencies(jax.random.fold_in(arg_keys[11], 71), 0)
    block_slot = jax.random.permutation(arg_keys[8], NBLOCKS).astype(jnp.int32)
    trade_weights = gaussian(arg_keys[9], (TRADES, DEPS, BLOCK), (DEPS * BLOCK) ** -0.5, 0.375, ((0, 8),))
    netting = plant(jax.random.randint(arg_keys[10], (TRADES,), 0, NSETS), jax.random.fold_in(arg_keys[10], 1), 0, NSETS - 1).astype(jnp.int32)
    return dict(shocks=shocks, loadings=loadings, vol=vol, jump_counts=jump_counts, jump_noise=jump_noise, jump_mean=jump_mean, jump_vol=jump_vol, dependencies=dependencies, block_slot=block_slot, trade_weights=trade_weights, netting=netting)


def price_trades(blocks, slots, weights):

    def one(part):
        total = jnp.zeros((part.shape[0], slots.shape[0]), jnp.float32)
        for k in range(DEPS):
            chosen = part[:, slots[:, k], :].astype(jnp.float32)
            total = total + jnp.einsum('stj,tj->st', chosen, weights[:, k, :].astype(jnp.float32))
        return total
    grouped = blocks.reshape(SCENARIOS // 32, 32, NBLOCKS, BLOCK)
    return lax.map(one, grouped).reshape(SCENARIOS, TRADES)

def reference(shocks, loadings, vol, jump_counts, jump_noise, jump_mean, jump_vol, dependencies, block_slot, trade_weights, netting):
    level = jnp.zeros((SCENARIOS, FACTORS), jnp.float32)
    slots = block_slot[dependencies]
    exposures = []
    expects = []
    for date in range(DATES):
        diffuse = jnp.dot(shocks[date], loadings, preferred_element_type=jnp.float32)
        counts = jump_counts[date].astype(jnp.float32)
        level = level + vol * diffuse - 0.5 * vol * vol + counts * jump_mean + jnp.sqrt(counts) * jump_vol * jump_noise[date].astype(jnp.float32)
        prices = (jnp.exp(level) - 1.0).astype(jnp.bfloat16)
        values = price_trades(prices.reshape(SCENARIOS, NBLOCKS, BLOCK), slots, trade_weights)
        nets = jax.ops.segment_sum(values.T, netting, num_segments=NSETS)
        exposure = jnp.maximum(nets, 0.0)
        exposures.append(exposure)
        expects.append(lax.optimization_barrier(jnp.sum(exposure, axis=1)) / SCENARIOS)
    return (jnp.stack(exposures), jnp.stack(expects))
```

```python
import functools

import jax
import jax.numpy as jnp
from jax import lax
from jax.experimental import pallas as pl
from jax.experimental.pallas import tpu as pltpu
from jax.sharding import PartitionSpec as P

BLOCK = 128
SET_DEV = 64
DATES = 2
SIDE_FLIP = 1
PRICE_FLIP = 2
TAGS = 16
CHUNK = 64

VMEM = pl.BlockSpec(memory_space=pltpu.VMEM)
HBM = pl.BlockSpec(memory_space=pltpu.HBM)
SMEM = pl.BlockSpec(memory_space=pltpu.SMEM)
PARAMS = pltpu.CompilerParams(vmem_limit_bytes=16 * 1024 * 1024)
FETCH_PARAMS = pltpu.CompilerParams(vmem_limit_bytes=60 * 1024 * 1024)
NT = (((1,), (1,)), ((), ()))


def f32_dot(a, b, dims):
    return lax.dot_general(a, b, dims, preferred_element_type=jnp.float32)


def fetch(pairs, sems):
    copies = [pltpu.make_async_copy(src, dst, sems.at[i]) for i, (src, dst) in enumerate(pairs)]
    for copy in copies:
        copy.start()
    for copy in copies:
        copy.wait()


def pack_kernel(part, weights_hbm, deps_hbm, netting_hbm, packet_ref, weights_ref, deps_ref, netting_ref, sems):
    fetch([(weights_hbm, weights_ref), (deps_hbm, deps_ref), (netting_hbm, netting_ref)], sems)
    scen = lax.axis_index("scen")
    row = lax.broadcasted_iota(jnp.int32, (part, BLOCK), 0)
    column = lax.broadcasted_iota(jnp.int32, (part, BLOCK), 1)
    pick = (column == scen * part + row).astype(jnp.float32).astype(jnp.bfloat16)
    for k in range(2):
        share = f32_dot(pick, weights_ref[:, k, :], NT)
        packet_ref[k * part : (k + 1) * part, :] = share.astype(jnp.bfloat16)
    netting = netting_ref[...]
    tags = jnp.concatenate(
        [
            deps_ref[...],
            netting // SET_DEV,
            netting % SET_DEV,
            jnp.zeros((TAGS - 4, netting.shape[1]), jnp.int32),
        ],
        axis=0,
    )
    packet_ref[2 * part :, :] = tags.astype(jnp.float32).astype(jnp.bfloat16)


def price_kernel(*refs):
    count = 7
    out_ref, sems = refs[count], refs[-1]
    refs_in = refs[count + 1 : -1]
    fetch(list(zip(refs[:count], refs_in)), sems)
    shocks_ref, loadings_ref, vol_ref, counts_ref, noise_ref, mean_ref, dev_ref = refs_in
    rows = shocks_ref.shape[1]
    vol = vol_ref[...]
    drift = 0.5 * vol * vol
    mean = mean_ref[...]
    dev = dev_ref[...]
    loadings = loadings_ref[...]

    def step(i, carry):
        at = pl.ds(pl.multiple_of(i * CHUNK, CHUNK), CHUNK)
        level = jnp.zeros((CHUNK, vol.shape[1]), jnp.float32)
        for date in range(DATES):
            diffuse = jnp.dot(shocks_ref[date, at, :], loadings, preferred_element_type=jnp.float32)
            counts = counts_ref[date, at, :].astype(jnp.float32)
            noise = noise_ref[date, at, :].astype(jnp.float32)
            level = level + vol * diffuse - drift + counts * mean + jnp.sqrt(counts) * dev * noise
            out_ref[date, at, :] = (jnp.exp(level) - 1.0).astype(jnp.bfloat16)
        return carry

    lax.fori_loop(0, rows // CHUNK, step, 0)


def combine_kernel(part, held, flips, *refs):
    slot_ref, packet_refs = refs[0], refs[1:-4]
    own_ref, other_ref, chosen_ref, marks_ref = refs[-4:]
    fac = lax.axis_index("fac")
    names = []
    for flip in (0, PRICE_FLIP, SIDE_FLIP, SIDE_FLIP ^ PRICE_FLIP):
        for h in range(held):
            slot = (fac ^ flip) * held + h

            def find(b, name):
                return jnp.where(slot_ref[b] == slot, b, name)

            names.append(lax.fori_loop(0, slot_ref.shape[0], find, 0, unroll=True).astype(jnp.float32))
    trades = packet_refs[0].shape[1]
    place = lax.broadcasted_iota(jnp.int32, (SET_DEV, trades), 0).astype(jnp.float32)
    for source, packet_ref in enumerate(packet_refs):
        at = slice(source * trades, (source + 1) * trades)
        tags = packet_ref[2 * part :, :].astype(jnp.float32)
        weights = [packet_ref[k * part : (k + 1) * part, :].astype(jnp.float32) for k in range(2)]
        for b, name in enumerate(names):
            picked = jnp.where(tags[0:1] == name, weights[0], 0.0)
            picked = jnp.where(tags[1:2] == name, weights[1], picked)
            chosen_ref[b * part : (b + 1) * part, at] = picked.astype(jnp.bfloat16)
        for i, flip in enumerate(flips):
            owner = (fac ^ flip).astype(jnp.float32)
            local = jnp.where(tags[2:3] == owner, tags[3:4], -1.0)
            mark = jnp.where(local == place, 1.0, 0.0)
            marks_ref[i * SET_DEV : (i + 1) * SET_DEV, at] = mark.astype(jnp.bfloat16)
    sums = f32_dot(chosen_ref[...], marks_ref[...], NT)
    half = own_ref.shape[0]
    own_ref[...] = sums[:half]
    other_ref[...] = sums[half:].astype(jnp.bfloat16)


def merge_kernel(own_ref, other_ref, share_ref):
    pair = 2 * SET_DEV
    for at in range(0, own_ref.shape[1], pair):
        other = pltpu.roll(other_ref[:, at : at + pair].astype(jnp.float32), SET_DEV, 1)
        share_ref[:, at : at + pair] = (own_ref[:, at : at + pair] + other).astype(jnp.bfloat16)


def value_kernel(part, held, scen_count, *refs):
    share_refs, price_refs = refs[:scen_count], refs[scen_count : scen_count + 2]
    out_refs, whole_ref = refs[scen_count + 2 : -1], refs[-1]
    scen = lax.axis_index("scen")
    for i, share_ref in enumerate(share_refs):
        column = (scen ^ i) * part
        for b in range(2 * held):
            at = pl.ds(pl.multiple_of(b * BLOCK + column, part), part)
            whole_ref[at, :] = share_ref[b * part : (b + 1) * part, :].astype(jnp.float32)
    width = held * BLOCK
    total = None
    for i, price_ref in enumerate(price_refs):
        whole = whole_ref[i * width : (i + 1) * width, :].T.astype(jnp.bfloat16)
        term = f32_dot(whole, price_ref[...], NT)
        total = term if total is None else total + term
    for p, out_ref in enumerate(out_refs):
        out_ref[...] = total[p * SET_DEV : (p + 1) * SET_DEV].astype(out_ref.dtype)


def expose_kernel(rows, *refs):
    part_refs, exposure_ref, totals_ref = refs[:-2], refs[-2], refs[-1]
    for date in range(DATES):
        at = slice(date * rows, (date + 1) * rows)
        nets = part_refs[0][:, at]
        for ref in part_refs[1:]:
            nets = nets + ref[:, at].astype(jnp.float32)
        exposure = jnp.maximum(nets, 0.0)
        exposure_ref[date] = exposure
        totals_ref[date] = jnp.sum(exposure, axis=1)


def from_partner(x, axis, flip):
    count = lax.axis_size(axis)
    return lax.ppermute(x, axis, [(i, i ^ flip) for i in range(count)])


def body(
    shocks,
    loadings,
    vol,
    jump_counts,
    jump_noise,
    jump_mean,
    jump_vol,
    dependencies,
    block_slot,
    trade_weights,
    netting,
):
    fac_count = lax.axis_size("fac")
    scen_count = lax.axis_size("scen")
    rows = shocks.shape[1]
    width = loadings.shape[1]
    held = width // BLOCK
    trades = trade_weights.shape[0]
    part = BLOCK // scen_count
    column_flips = [i for i in range(fac_count) if not i & SIDE_FLIP]
    owner_flips = [i for i in range(fac_count) if not i & PRICE_FLIP]

    inputs = (trade_weights, dependencies.T, netting[None])
    packet = pl.pallas_call(
        functools.partial(pack_kernel, part),
        out_shape=jax.ShapeDtypeStruct((2 * part + TAGS, trades), jnp.bfloat16),
        in_specs=[HBM] * len(inputs),
        out_specs=VMEM,
        scratch_shapes=[pltpu.VMEM(x.shape, x.dtype) for x in inputs]
        + [pltpu.SemaphoreType.DMA((len(inputs),))],
        compiler_params=FETCH_PARAMS,
        name="pack",
    )(*inputs)
    packets = [packet] + [from_partner(packet, "fac", i) for i in column_flips[1:]]

    packet, shocks = lax.optimization_barrier((packet, shocks))
    inputs = (shocks, loadings, vol[None], jump_counts, jump_noise, jump_mean[None], jump_vol[None])
    prices = pl.pallas_call(
        price_kernel,
        out_shape=jax.ShapeDtypeStruct((DATES, rows, width), jnp.bfloat16),
        in_specs=[HBM] * len(inputs),
        out_specs=VMEM,
        scratch_shapes=[pltpu.VMEM(x.shape, x.dtype) for x in inputs]
        + [pltpu.SemaphoreType.DMA((len(inputs),))],
        compiler_params=FETCH_PARAMS,
        name="price",
    )(*inputs)
    prices = prices.reshape(DATES * rows, width)
    share_shape = (2 * held * part, len(owner_flips) * SET_DEV)
    column_trades = len(column_flips) * trades
    own, other = pl.pallas_call(
        functools.partial(combine_kernel, part, held, owner_flips),
        out_shape=[
            jax.ShapeDtypeStruct(share_shape, jnp.float32),
            jax.ShapeDtypeStruct(share_shape, jnp.bfloat16),
        ],
        in_specs=[SMEM] + [VMEM] * len(packets),
        out_specs=[VMEM] * 2,
        scratch_shapes=[
            pltpu.VMEM((2 * share_shape[0], column_trades), jnp.bfloat16),
            pltpu.VMEM((share_shape[1], column_trades), jnp.bfloat16),
        ],
        compiler_params=PARAMS,
        name="combine",
    )(block_slot, *packets)
    prices, other = lax.optimization_barrier((prices, other))
    pair_prices = [prices, from_partner(prices, "fac", PRICE_FLIP)]
    share = pl.pallas_call(
        merge_kernel,
        out_shape=jax.ShapeDtypeStruct(share_shape, jnp.bfloat16),
        in_specs=[VMEM] * 2,
        out_specs=VMEM,
        compiler_params=PARAMS,
        name="merge",
    )(own, from_partner(other, "fac", SIDE_FLIP))
    shares = [share] + [from_partner(share, "scen", i) for i in range(1, scen_count)]

    parts = pl.pallas_call(
        functools.partial(value_kernel, part, held, scen_count),
        out_shape=[
            jax.ShapeDtypeStruct((SET_DEV, DATES * rows), jnp.bfloat16 if flip else jnp.float32)
            for flip in owner_flips
        ],
        in_specs=[VMEM] * (scen_count + 2),
        out_specs=[VMEM] * len(owner_flips),
        scratch_shapes=[pltpu.VMEM((2 * width, share_shape[1]), jnp.float32)],
        compiler_params=PARAMS,
        name="value",
    )(*shares, *pair_prices)
    parts = [parts[0]] + [from_partner(x, "fac", i) for x, i in zip(parts[1:], owner_flips[1:])]

    exposure, totals = pl.pallas_call(
        functools.partial(expose_kernel, rows),
        out_shape=[
            jax.ShapeDtypeStruct((DATES, SET_DEV, rows), jnp.float32),
            jax.ShapeDtypeStruct((DATES, SET_DEV), jnp.float32),
        ],
        in_specs=[VMEM] * len(parts),
        out_specs=[VMEM] * 2,
        compiler_params=PARAMS,
        name="expose",
    )(*parts)
    sums = [totals] + [from_partner(totals, "scen", i) for i in range(1, scen_count)]
    while len(sums) > 1:
        sums = [sums[i] + sums[i + 1] for i in range(0, len(sums), 2)]
    return (exposure, sums[0] / (rows * scen_count))


def solution(mesh):
    placed = (
        P(None, "scen", None),
        P(None, "fac"),
        P("fac"),
        P(None, "scen", "fac"),
        P(None, "scen", "fac"),
        P("fac"),
        P("fac"),
        P("fac", None),
        P(),
        P("fac", None, None),
        P("fac"),
    )
    return jax.shard_map(
        body,
        mesh=mesh,
        in_specs=placed,
        out_specs=(P(None, "fac", "scen"), P(None, "fac")),
        check_vma=False,
    )
```

```python
import functools

import jax
import jax.numpy as jnp
from jax import lax
from jax.experimental import pallas as pl
from jax.experimental.pallas import tpu as pltpu
from jax.sharding import PartitionSpec as P

BLOCK = 128
SET_DEV = 64
DATES = 2
SIDE_FLIP = 1
PRICE_FLIP = 2
TAGS = 16
CHUNK = 64

VMEM = pl.BlockSpec(memory_space=pltpu.VMEM)
HBM = pl.BlockSpec(memory_space=pltpu.HBM)
SMEM = pl.BlockSpec(memory_space=pltpu.SMEM)
PARAMS = pltpu.CompilerParams(vmem_limit_bytes=16 * 1024 * 1024)
FETCH_PARAMS = pltpu.CompilerParams(vmem_limit_bytes=60 * 1024 * 1024)
NT = (((1,), (1,)), ((), ()))


def f32_dot(a, b, dims):
    return lax.dot_general(a, b, dims, preferred_element_type=jnp.float32)


def fetch(pairs, sems):
    copies = [pltpu.make_async_copy(src, dst, sems.at[i]) for i, (src, dst) in enumerate(pairs)]
    for copy in copies:
        copy.start()
    for copy in copies:
        copy.wait()


def pack_kernel(part, weights_hbm, deps_hbm, netting_hbm, packet_ref, weights_ref, deps_ref, netting_ref, sems):
    fetch([(weights_hbm, weights_ref), (deps_hbm, deps_ref), (netting_hbm, netting_ref)], sems)
    scen = lax.axis_index("scen")
    row = lax.broadcasted_iota(jnp.int32, (part, BLOCK), 0)
    column = lax.broadcasted_iota(jnp.int32, (part, BLOCK), 1)
    pick = (column == scen * part + row).astype(jnp.float32).astype(jnp.bfloat16)
    for k in range(2):
        share = f32_dot(pick, weights_ref[:, k, :], NT)
        packet_ref[k * part : (k + 1) * part, :] = share.astype(jnp.bfloat16)
    netting = netting_ref[...]
    tags = jnp.concatenate(
        [
            deps_ref[...],
            netting // SET_DEV,
            netting % SET_DEV,
            jnp.zeros((TAGS - 4, netting.shape[1]), jnp.int32),
        ],
        axis=0,
    )
    packet_ref[2 * part :, :] = tags.astype(jnp.float32).astype(jnp.bfloat16)


def price_kernel(*refs):
    sources, out_hbm, held_refs, out_ref = refs[:7], refs[7], refs[8:15], refs[15]
    sems, chunk_sems, out_sems = refs[16:]
    loadings_ref, vol_ref, mean_ref, dev_ref, shocks_ref, counts_ref, noise_ref = held_refs
    rows = shocks_ref.shape[1]
    fixed = [
        pltpu.make_async_copy(src, dst, sems.at[i])
        for i, (src, dst) in enumerate(zip(sources[:4], held_refs[:4]))
    ]
    chunks = [
        [
            pltpu.make_async_copy(src.at[:, pl.ds(at, CHUNK)], dst.at[:, pl.ds(at, CHUNK)], chunk_sems.at[i, j])
            for j, (src, dst) in enumerate(zip(sources[4:], held_refs[4:]))
        ]
        for i, at in enumerate(range(0, rows, CHUNK))
    ]
    results = [
        pltpu.make_async_copy(out_ref.at[:, pl.ds(at, CHUNK)], out_hbm.at[:, pl.ds(at, CHUNK)], out_sems.at[i])
        for i, at in enumerate(range(0, rows, CHUNK))
    ]
    for copy in fixed + sum(chunks, []):
        copy.start()
    for copy in fixed:
        copy.wait()
    vol = vol_ref[...]
    drift = 0.5 * vol * vol
    mean = mean_ref[...]
    dev = dev_ref[...]
    loadings = loadings_ref[...]
    for i, copies in enumerate(chunks):
        for copy in copies:
            copy.wait()
        at = slice(i * CHUNK, (i + 1) * CHUNK)
        level = jnp.zeros((CHUNK, vol.shape[1]), jnp.float32)
        for date in range(DATES):
            diffuse = jnp.dot(shocks_ref[date, at, :], loadings, preferred_element_type=jnp.float32)
            counts = counts_ref[date, at, :].astype(jnp.float32)
            noise = noise_ref[date, at, :].astype(jnp.float32)
            level = level + vol * diffuse - drift + counts * mean + jnp.sqrt(counts) * dev * noise
            out_ref[date, at, :] = (jnp.exp(level) - 1.0).astype(jnp.bfloat16)
        results[i].start()
    for copy in results:
        copy.wait()


def combine_kernel(part, held, flips, *refs):
    slot_ref, packet_refs = refs[0], refs[1:-4]
    own_ref, other_ref, chosen_ref, marks_ref = refs[-4:]
    fac = lax.axis_index("fac")
    names = []
    for flip in (0, PRICE_FLIP, SIDE_FLIP, SIDE_FLIP ^ PRICE_FLIP):
        for h in range(held):
            slot = (fac ^ flip) * held + h

            def find(b, name):
                return jnp.where(slot_ref[b] == slot, b, name)

            names.append(lax.fori_loop(0, slot_ref.shape[0], find, 0, unroll=True).astype(jnp.float32))
    trades = packet_refs[0].shape[1]
    place = lax.broadcasted_iota(jnp.int32, (SET_DEV, trades), 0).astype(jnp.float32)
    for source, packet_ref in enumerate(packet_refs):
        at = slice(source * trades, (source + 1) * trades)
        tags = packet_ref[2 * part :, :].astype(jnp.float32)
        weights = [packet_ref[k * part : (k + 1) * part, :].astype(jnp.float32) for k in range(2)]
        for b, name in enumerate(names):
            picked = jnp.where(tags[0:1] == name, weights[0], 0.0)
            picked = jnp.where(tags[1:2] == name, weights[1], picked)
            chosen_ref[b * part : (b + 1) * part, at] = picked.astype(jnp.bfloat16)
        for i, flip in enumerate(flips):
            owner = (fac ^ flip).astype(jnp.float32)
            local = jnp.where(tags[2:3] == owner, tags[3:4], -1.0)
            mark = jnp.where(local == place, 1.0, 0.0)
            marks_ref[i * SET_DEV : (i + 1) * SET_DEV, at] = mark.astype(jnp.bfloat16)
    sums = f32_dot(chosen_ref[...], marks_ref[...], NT)
    half = own_ref.shape[0]
    own_ref[...] = sums[:half]
    other_ref[...] = sums[half:].astype(jnp.bfloat16)


def merge_kernel(own_ref, other_ref, share_ref):
    pair = 2 * SET_DEV
    for at in range(0, own_ref.shape[1], pair):
        other = pltpu.roll(other_ref[:, at : at + pair].astype(jnp.float32), SET_DEV, 1)
        share_ref[:, at : at + pair] = (own_ref[:, at : at + pair] + other).astype(jnp.bfloat16)


def value_kernel(part, held, scen_count, *refs):
    share_refs, price_refs = refs[:scen_count], refs[scen_count : scen_count + 2]
    out_refs, whole_ref = refs[scen_count + 2 : -1], refs[-1]
    scen = lax.axis_index("scen")
    for i, share_ref in enumerate(share_refs):
        column = (scen ^ i) * part
        for b in range(2 * held):
            at = pl.ds(pl.multiple_of(b * BLOCK + column, part), part)
            whole_ref[at, :] = share_ref[b * part : (b + 1) * part, :].astype(jnp.float32)
    width = held * BLOCK
    total = None
    for i, price_ref in enumerate(price_refs):
        whole = whole_ref[i * width : (i + 1) * width, :].T.astype(jnp.bfloat16)
        term = f32_dot(whole, price_ref[...], NT)
        total = term if total is None else total + term
    for p, out_ref in enumerate(out_refs):
        out_ref[...] = total[p * SET_DEV : (p + 1) * SET_DEV].astype(out_ref.dtype)


def exposure_of(part_refs, date, rows):
    at = slice(date * rows, (date + 1) * rows)
    nets = part_refs[0][:, at]
    for ref in part_refs[1:]:
        nets = nets + ref[:, at].astype(jnp.float32)
    return jnp.maximum(nets, 0.0)


def totals_kernel(rows, *refs):
    for date in range(DATES):
        refs[-1][date] = jnp.sum(exposure_of(refs[:-1], date, rows), axis=1)


def expose_kernel(rows, *refs):
    for date in range(DATES):
        refs[-1][date] = exposure_of(refs[:-1], date, rows)


def from_partner(x, axis, flip):
    count = lax.axis_size(axis)
    return lax.ppermute(x, axis, [(i, i ^ flip) for i in range(count)])


def body(
    shocks,
    loadings,
    vol,
    jump_counts,
    jump_noise,
    jump_mean,
    jump_vol,
    dependencies,
    block_slot,
    trade_weights,
    netting,
):
    fac_count = lax.axis_size("fac")
    scen_count = lax.axis_size("scen")
    rows = shocks.shape[1]
    width = loadings.shape[1]
    held = width // BLOCK
    trades = trade_weights.shape[0]
    part = BLOCK // scen_count
    column_flips = [i for i in range(fac_count) if not i & SIDE_FLIP]
    owner_flips = [i for i in range(fac_count) if not i & PRICE_FLIP]

    inputs = (trade_weights, dependencies.T, netting[None])
    packet = pl.pallas_call(
        functools.partial(pack_kernel, part),
        out_shape=jax.ShapeDtypeStruct((2 * part + TAGS, trades), jnp.bfloat16),
        in_specs=[HBM] * len(inputs),
        out_specs=VMEM,
        scratch_shapes=[pltpu.VMEM(x.shape, x.dtype) for x in inputs]
        + [pltpu.SemaphoreType.DMA((len(inputs),))],
        compiler_params=FETCH_PARAMS,
        name="pack",
    )(*inputs)
    packets = [packet] + [from_partner(packet, "fac", i) for i in column_flips[1:]]

    packet, shocks = lax.optimization_barrier((packet, shocks))
    inputs = (loadings, vol[None], jump_mean[None], jump_vol[None], shocks, jump_counts, jump_noise)
    prices_shape = jax.ShapeDtypeStruct((DATES, rows, width), jnp.bfloat16)
    prices = pl.pallas_call(
        price_kernel,
        out_shape=prices_shape,
        in_specs=[HBM] * len(inputs),
        out_specs=HBM,
        scratch_shapes=[pltpu.VMEM(x.shape, x.dtype) for x in inputs + (prices_shape,)]
        + [
            pltpu.SemaphoreType.DMA((4,)),
            pltpu.SemaphoreType.DMA((rows // CHUNK, 3)),
            pltpu.SemaphoreType.DMA((rows // CHUNK,)),
        ],
        compiler_params=FETCH_PARAMS,
        name="price",
    )(*inputs)
    prices = prices.reshape(DATES * rows, width)
    share_shape = (2 * held * part, len(owner_flips) * SET_DEV)
    column_trades = len(column_flips) * trades
    own, other = pl.pallas_call(
        functools.partial(combine_kernel, part, held, owner_flips),
        out_shape=[
            jax.ShapeDtypeStruct(share_shape, jnp.float32),
            jax.ShapeDtypeStruct(share_shape, jnp.bfloat16),
        ],
        in_specs=[SMEM] + [VMEM] * len(packets),
        out_specs=[VMEM] * 2,
        scratch_shapes=[
            pltpu.VMEM((2 * share_shape[0], column_trades), jnp.bfloat16),
            pltpu.VMEM((share_shape[1], column_trades), jnp.bfloat16),
        ],
        compiler_params=PARAMS,
        name="combine",
    )(block_slot, *packets)
    prices, other = lax.optimization_barrier((prices, other))
    pair_prices = [prices, from_partner(prices, "fac", PRICE_FLIP)]
    share = pl.pallas_call(
        merge_kernel,
        out_shape=jax.ShapeDtypeStruct(share_shape, jnp.bfloat16),
        in_specs=[VMEM] * 2,
        out_specs=VMEM,
        compiler_params=PARAMS,
        cost_estimate=pl.CostEstimate(flops=10**10, bytes_accessed=0, transcendentals=0),
        name="merge",
    )(own, from_partner(other, "fac", SIDE_FLIP))
    shares = [share] + [from_partner(share, "scen", i) for i in range(1, scen_count)]

    parts = pl.pallas_call(
        functools.partial(value_kernel, part, held, scen_count),
        out_shape=[
            jax.ShapeDtypeStruct((SET_DEV, DATES * rows), jnp.bfloat16 if flip else jnp.float32)
            for flip in owner_flips
        ],
        in_specs=[VMEM] * (scen_count + 2),
        out_specs=[VMEM] * len(owner_flips),
        scratch_shapes=[pltpu.VMEM((2 * width, share_shape[1]), jnp.float32)],
        compiler_params=PARAMS,
        name="value",
    )(*shares, *pair_prices)
    sends = list(zip(parts[1:], owner_flips[1:]))
    parts = [parts[0]] + [from_partner(x, "fac", i) for x, i in sends[::-1]]

    totals = pl.pallas_call(
        functools.partial(totals_kernel, rows),
        out_shape=jax.ShapeDtypeStruct((DATES, SET_DEV), jnp.float32),
        in_specs=[VMEM] * len(parts),
        out_specs=VMEM,
        compiler_params=PARAMS,
        name="totals",
    )(*parts)
    exposure = pl.pallas_call(
        functools.partial(expose_kernel, rows),
        out_shape=jax.ShapeDtypeStruct((DATES, SET_DEV, rows), jnp.float32),
        in_specs=[VMEM] * len(parts),
        out_specs=VMEM,
        compiler_params=PARAMS,
        name="expose",
    )(*parts)
    sums = [totals] + [from_partner(totals, "scen", i) for i in range(1, scen_count)]
    while len(sums) > 1:
        sums = [sums[i] + sums[i + 1] for i in range(0, len(sums), 2)]
    return (exposure, sums[0] / (rows * scen_count))


def solution(mesh):
    placed = (
        P(None, "scen", None),
        P(None, "fac"),
        P("fac"),
        P(None, "scen", "fac"),
        P(None, "scen", "fac"),
        P("fac"),
        P("fac"),
        P("fac", None),
        P(),
        P("fac", None, None),
        P("fac"),
    )
    return jax.shard_map(
        body,
        mesh=mesh,
        in_specs=placed,
        out_specs=(P(None, "fac", "scen"), P(None, "fac")),
        check_vma=False,
    )
```

```python
import functools

import jax
import jax.numpy as jnp
from jax import lax
from jax.experimental import pallas as pl
from jax.experimental.pallas import tpu as pltpu
from jax.sharding import PartitionSpec as P

BLOCK = 128
SET_DEV = 64
DATES = 2
SIDE_FLIP = 1
PRICE_FLIP = 2
TAGS = 16
CHUNK = 64

VMEM = pl.BlockSpec(memory_space=pltpu.VMEM)
HBM = pl.BlockSpec(memory_space=pltpu.HBM)
SMEM = pl.BlockSpec(memory_space=pltpu.SMEM)
PARAMS = pltpu.CompilerParams(vmem_limit_bytes=16 * 1024 * 1024)
FETCH_PARAMS = pltpu.CompilerParams(vmem_limit_bytes=60 * 1024 * 1024)
NT = (((1,), (1,)), ((), ()))


def f32_dot(a, b, dims):
    return lax.dot_general(a, b, dims, preferred_element_type=jnp.float32)


def pack_kernel(part, weights_ref, trades_ref, packet_ref):
    scen = lax.axis_index("scen")
    row = lax.broadcasted_iota(jnp.int32, (part, BLOCK), 0)
    column = lax.broadcasted_iota(jnp.int32, (part, BLOCK), 1)
    pick = (column == scen * part + row).astype(jnp.float32).astype(jnp.bfloat16)
    for k in range(2):
        share = f32_dot(pick, weights_ref[:, k, :], NT)
        packet_ref[k * part : (k + 1) * part, :] = share.astype(jnp.bfloat16)
    netting = trades_ref[2:3, :]
    tags = jnp.concatenate(
        [
            trades_ref[:2, :],
            netting // SET_DEV,
            netting % SET_DEV,
            jnp.zeros((TAGS - 4, netting.shape[1]), jnp.int32),
        ],
        axis=0,
    )
    packet_ref[2 * part :, :] = tags.astype(jnp.float32).astype(jnp.bfloat16)


def price_kernel(*refs):
    sources, out_hbm, held_refs, out_ref = refs[:7], refs[7], refs[8:15], refs[15]
    sems, chunk_sems, out_sems = refs[16:]
    loadings_ref, vol_ref, mean_ref, dev_ref, shocks_ref, counts_ref, noise_ref = held_refs
    rows = shocks_ref.shape[1]
    fixed = [
        pltpu.make_async_copy(src, dst, sems.at[i])
        for i, (src, dst) in enumerate(zip(sources[:4], held_refs[:4]))
    ]
    chunks = [
        [
            pltpu.make_async_copy(src.at[:, pl.ds(at, CHUNK)], dst.at[:, pl.ds(at, CHUNK)], chunk_sems.at[i, j])
            for j, (src, dst) in enumerate(zip(sources[4:], held_refs[4:]))
        ]
        for i, at in enumerate(range(0, rows, CHUNK))
    ]
    results = [
        pltpu.make_async_copy(out_ref.at[:, pl.ds(at, CHUNK)], out_hbm.at[:, pl.ds(at, CHUNK)], out_sems.at[i])
        for i, at in enumerate(range(0, rows, CHUNK))
    ]
    for copy in fixed + sum(chunks, []):
        copy.start()
    for copy in fixed:
        copy.wait()
    vol = vol_ref[...]
    drift = 0.5 * vol * vol
    mean = mean_ref[...]
    dev = dev_ref[...]
    loadings = loadings_ref[...]
    for i, copies in enumerate(chunks):
        for copy in copies:
            copy.wait()
        at = slice(i * CHUNK, (i + 1) * CHUNK)
        level = jnp.zeros((CHUNK, vol.shape[1]), jnp.float32)
        for date in range(DATES):
            diffuse = jnp.dot(shocks_ref[date, at, :], loadings, preferred_element_type=jnp.float32)
            counts = counts_ref[date, at, :].astype(jnp.float32)
            noise = noise_ref[date, at, :].astype(jnp.float32)
            level = level + vol * diffuse - drift + counts * mean + jnp.sqrt(counts) * dev * noise
            out_ref[date, at, :] = (jnp.exp(level) - 1.0).astype(jnp.bfloat16)
        results[i].start()
    for copy in results:
        copy.wait()


def combine_kernel(part, held, flips, *refs):
    slot_ref, packet_refs = refs[0], refs[1:-4]
    own_ref, other_ref, chosen_ref, marks_ref = refs[-4:]
    fac = lax.axis_index("fac")
    names = []
    for flip in (0, PRICE_FLIP, SIDE_FLIP, SIDE_FLIP ^ PRICE_FLIP):
        for h in range(held):
            slot = (fac ^ flip) * held + h

            def find(b, name):
                return jnp.where(slot_ref[b] == slot, b, name)

            names.append(lax.fori_loop(0, slot_ref.shape[0], find, 0, unroll=True).astype(jnp.float32))
    trades = packet_refs[0].shape[1]
    place = lax.broadcasted_iota(jnp.int32, (SET_DEV, trades), 0).astype(jnp.float32)
    for source, packet_ref in enumerate(packet_refs):
        at = slice(source * trades, (source + 1) * trades)
        tags = packet_ref[2 * part :, :].astype(jnp.float32)
        weights = [packet_ref[k * part : (k + 1) * part, :].astype(jnp.float32) for k in range(2)]
        for b, name in enumerate(names):
            picked = jnp.where(tags[0:1] == name, weights[0], 0.0)
            picked = jnp.where(tags[1:2] == name, weights[1], picked)
            chosen_ref[b * part : (b + 1) * part, at] = picked.astype(jnp.bfloat16)
        for i, flip in enumerate(flips):
            owner = (fac ^ flip).astype(jnp.float32)
            local = jnp.where(tags[2:3] == owner, tags[3:4], -1.0)
            mark = jnp.where(local == place, 1.0, 0.0)
            marks_ref[i * SET_DEV : (i + 1) * SET_DEV, at] = mark.astype(jnp.bfloat16)
    sums = f32_dot(chosen_ref[...], marks_ref[...], NT)
    half = own_ref.shape[0]
    own_ref[...] = sums[:half]
    other_ref[...] = sums[half:].astype(jnp.bfloat16)


def merge_kernel(own_ref, other_ref, share_ref):
    pair = 2 * SET_DEV
    for at in range(0, own_ref.shape[1], pair):
        other = pltpu.roll(other_ref[:, at : at + pair].astype(jnp.float32), SET_DEV, 1)
        share_ref[:, at : at + pair] = (own_ref[:, at : at + pair] + other).astype(jnp.bfloat16)


def value_kernel(part, held, scen_count, *refs):
    share_refs, price_refs = refs[:scen_count], refs[scen_count : scen_count + 2]
    out_refs, whole_ref = refs[scen_count + 2 : -1], refs[-1]
    scen = lax.axis_index("scen")
    for i, share_ref in enumerate(share_refs):
        column = (scen ^ i) * part
        for b in range(2 * held):
            at = pl.ds(pl.multiple_of(b * BLOCK + column, part), part)
            whole_ref[at, :] = share_ref[b * part : (b + 1) * part, :].astype(jnp.float32)
    width = held * BLOCK
    total = None
    for i, price_ref in enumerate(price_refs):
        whole = whole_ref[i * width : (i + 1) * width, :].T.astype(jnp.bfloat16)
        term = f32_dot(whole, price_ref[...], NT)
        total = term if total is None else total + term
    for p, out_ref in enumerate(out_refs):
        out_ref[...] = total[p * SET_DEV : (p + 1) * SET_DEV].astype(out_ref.dtype)


def exposure_of(part_refs, date, rows):
    at = slice(date * rows, (date + 1) * rows)
    nets = part_refs[0][:, at]
    for ref in part_refs[1:]:
        nets = nets + ref[:, at].astype(jnp.float32)
    return jnp.maximum(nets, 0.0)


def totals_kernel(rows, *refs):
    for date in range(DATES):
        refs[-1][date] = jnp.sum(exposure_of(refs[:-1], date, rows), axis=1)


def expose_kernel(rows, *refs):
    for date in range(DATES):
        refs[-1][date] = exposure_of(refs[:-1], date, rows)


def from_partner(x, axis, flip):
    count = lax.axis_size(axis)
    return lax.ppermute(x, axis, [(i, i ^ flip) for i in range(count)])


def body(
    shocks,
    loadings,
    vol,
    jump_counts,
    jump_noise,
    jump_mean,
    jump_vol,
    dependencies,
    block_slot,
    trade_weights,
    netting,
):
    fac_count = lax.axis_size("fac")
    scen_count = lax.axis_size("scen")
    rows = shocks.shape[1]
    width = loadings.shape[1]
    held = width // BLOCK
    trades = trade_weights.shape[0]
    part = BLOCK // scen_count
    column_flips = [i for i in range(fac_count) if not i & SIDE_FLIP]
    owner_flips = [i for i in range(fac_count) if not i & PRICE_FLIP]

    packet = pl.pallas_call(
        functools.partial(pack_kernel, part),
        out_shape=jax.ShapeDtypeStruct((2 * part + TAGS, trades), jnp.bfloat16),
        in_specs=[VMEM] * 2,
        out_specs=VMEM,
        compiler_params=PARAMS,
        name="pack",
    )(trade_weights, jnp.concatenate([dependencies.T, netting[None]]))
    packets = [packet] + [from_partner(packet, "fac", i) for i in column_flips[1:]]

    packet, shocks = lax.optimization_barrier((packet, shocks))
    inputs = (loadings, vol[None], jump_mean[None], jump_vol[None], shocks, jump_counts, jump_noise)
    prices_shape = jax.ShapeDtypeStruct((DATES, rows, width), jnp.bfloat16)
    prices = pl.pallas_call(
        price_kernel,
        out_shape=prices_shape,
        in_specs=[HBM] * len(inputs),
        out_specs=HBM,
        scratch_shapes=[pltpu.VMEM(x.shape, x.dtype) for x in inputs + (prices_shape,)]
        + [
            pltpu.SemaphoreType.DMA((4,)),
            pltpu.SemaphoreType.DMA((rows // CHUNK, 3)),
            pltpu.SemaphoreType.DMA((rows // CHUNK,)),
        ],
        compiler_params=FETCH_PARAMS,
        name="price",
    )(*inputs)
    prices = prices.reshape(DATES * rows, width)
    share_shape = (2 * held * part, len(owner_flips) * SET_DEV)
    column_trades = len(column_flips) * trades
    own, other = pl.pallas_call(
        functools.partial(combine_kernel, part, held, owner_flips),
        out_shape=[
            jax.ShapeDtypeStruct(share_shape, jnp.float32),
            jax.ShapeDtypeStruct(share_shape, jnp.bfloat16),
        ],
        in_specs=[SMEM] + [VMEM] * len(packets),
        out_specs=[VMEM] * 2,
        scratch_shapes=[
            pltpu.VMEM((2 * share_shape[0], column_trades), jnp.bfloat16),
            pltpu.VMEM((share_shape[1], column_trades), jnp.bfloat16),
        ],
        compiler_params=PARAMS,
        name="combine",
    )(block_slot, *packets)
    prices, other = lax.optimization_barrier((prices, other))
    pair_prices = [prices, from_partner(prices, "fac", PRICE_FLIP)]
    share = pl.pallas_call(
        merge_kernel,
        out_shape=jax.ShapeDtypeStruct(share_shape, jnp.bfloat16),
        in_specs=[VMEM] * 2,
        out_specs=VMEM,
        compiler_params=PARAMS,
        cost_estimate=pl.CostEstimate(flops=10**10, bytes_accessed=0, transcendentals=0),
        name="merge",
    )(own, from_partner(other, "fac", SIDE_FLIP))
    shares = [share] + [from_partner(share, "scen", i) for i in range(1, scen_count)]

    parts = pl.pallas_call(
        functools.partial(value_kernel, part, held, scen_count),
        out_shape=[
            jax.ShapeDtypeStruct((SET_DEV, DATES * rows), jnp.bfloat16 if flip else jnp.float32)
            for flip in owner_flips
        ],
        in_specs=[VMEM] * (scen_count + 2),
        out_specs=[VMEM] * len(owner_flips),
        scratch_shapes=[pltpu.VMEM((2 * width, share_shape[1]), jnp.float32)],
        compiler_params=PARAMS,
        name="value",
    )(*shares, *pair_prices)
    sends = list(zip(parts[1:], owner_flips[1:]))
    sends = sends[1:] + sends[:1]
    parts = [parts[0]] + [from_partner(x, "fac", i) for x, i in sends]

    totals = pl.pallas_call(
        functools.partial(totals_kernel, rows),
        out_shape=jax.ShapeDtypeStruct((DATES, SET_DEV), jnp.float32),
        in_specs=[VMEM] * len(parts),
        out_specs=VMEM,
        compiler_params=PARAMS,
        name="totals",
    )(*parts)
    exposure = pl.pallas_call(
        functools.partial(expose_kernel, rows),
        out_shape=jax.ShapeDtypeStruct((DATES, SET_DEV, rows), jnp.float32),
        in_specs=[VMEM] * len(parts),
        out_specs=VMEM,
        compiler_params=PARAMS,
        name="expose",
    )(*parts)
    sums = [totals] + [from_partner(totals, "scen", i) for i in range(1, scen_count)]
    while len(sums) > 1:
        sums = [sums[i] + sums[i + 1] for i in range(0, len(sums), 2)]
    return (exposure, sums[0] / (rows * scen_count))


def solution(mesh):
    placed = (
        P(None, "scen", None),
        P(None, "fac"),
        P("fac"),
        P(None, "scen", "fac"),
        P(None, "scen", "fac"),
        P("fac"),
        P("fac"),
        P("fac", None),
        P(),
        P("fac", None, None),
        P("fac"),
    )
    return jax.shard_map(
        body,
        mesh=mesh,
        in_specs=placed,
        out_specs=(P(None, "fac", "scen"), P(None, "fac")),
        check_vma=False,
    )
```

```python
import functools

import jax
import jax.numpy as jnp
from jax import lax
from jax.experimental import pallas as pl
from jax.experimental.pallas import tpu as pltpu
from jax.sharding import PartitionSpec as P

BLOCK = 128
SET_DEV = 64
DATES = 2
SIDE_FLIP = 1
PRICE_FLIP = 2
TAGS = 16
CHUNK = 64

VMEM = pl.BlockSpec(memory_space=pltpu.VMEM)
HBM = pl.BlockSpec(memory_space=pltpu.HBM)
SMEM = pl.BlockSpec(memory_space=pltpu.SMEM)
PARAMS = pltpu.CompilerParams(vmem_limit_bytes=16 * 1024 * 1024)
FETCH_PARAMS = pltpu.CompilerParams(vmem_limit_bytes=60 * 1024 * 1024)
NT = (((1,), (1,)), ((), ()))


def f32_dot(a, b, dims):
    return lax.dot_general(a, b, dims, preferred_element_type=jnp.float32)


def pack_kernel(part, weights_ref, trades_ref, packet_ref):
    scen = lax.axis_index("scen")
    row = lax.broadcasted_iota(jnp.int32, (part, BLOCK), 0)
    column = lax.broadcasted_iota(jnp.int32, (part, BLOCK), 1)
    pick = (column == scen * part + row).astype(jnp.float32).astype(jnp.bfloat16)
    for k in range(2):
        share = f32_dot(pick, weights_ref[:, k, :], NT)
        packet_ref[k * part : (k + 1) * part, :] = share.astype(jnp.bfloat16)
    netting = trades_ref[2:3, :]
    tags = jnp.concatenate(
        [
            trades_ref[:2, :],
            netting // SET_DEV,
            netting % SET_DEV,
            jnp.zeros((TAGS - 4, netting.shape[1]), jnp.int32),
        ],
        axis=0,
    )
    packet_ref[2 * part :, :] = tags.astype(jnp.float32).astype(jnp.bfloat16)


def price_kernel(*refs):
    sources, out_hbm, held_refs, out_ref = refs[:7], refs[7], refs[8:15], refs[15]
    sems, chunk_sems, out_sems = refs[16:]
    loadings_ref, vol_ref, mean_ref, dev_ref, shocks_ref, counts_ref, noise_ref = held_refs
    rows = shocks_ref.shape[1]
    fixed = [
        pltpu.make_async_copy(src, dst, sems.at[i])
        for i, (src, dst) in enumerate(zip(sources[:4], held_refs[:4]))
    ]
    chunks = [
        [
            pltpu.make_async_copy(src.at[:, pl.ds(at, CHUNK)], dst.at[:, pl.ds(at, CHUNK)], chunk_sems.at[i, j])
            for j, (src, dst) in enumerate(zip(sources[4:], held_refs[4:]))
        ]
        for i, at in enumerate(range(0, rows, CHUNK))
    ]
    results = [
        pltpu.make_async_copy(out_ref.at[:, pl.ds(at, CHUNK)], out_hbm.at[:, pl.ds(at, CHUNK)], out_sems.at[i])
        for i, at in enumerate(range(0, rows, CHUNK))
    ]
    for copy in fixed + sum(chunks, []):
        copy.start()
    for copy in fixed:
        copy.wait()
    vol = vol_ref[...]
    drift = 0.5 * vol * vol
    mean = mean_ref[...]
    dev = dev_ref[...]
    loadings = loadings_ref[...]
    for i, copies in enumerate(chunks):
        for copy in copies:
            copy.wait()
        at = slice(i * CHUNK, (i + 1) * CHUNK)
        level = jnp.zeros((CHUNK, vol.shape[1]), jnp.float32)
        for date in range(DATES):
            diffuse = jnp.dot(shocks_ref[date, at, :], loadings, preferred_element_type=jnp.float32)
            counts = counts_ref[date, at, :].astype(jnp.float32)
            noise = noise_ref[date, at, :].astype(jnp.float32)
            level = level + vol * diffuse - drift + counts * mean + jnp.sqrt(counts) * dev * noise
            out_ref[date, at, :] = (jnp.exp(level) - 1.0).astype(jnp.bfloat16)
        results[i].start()
    for copy in results:
        copy.wait()


def combine_kernel(part, held, flips, *refs):
    slot_ref, packet_refs = refs[0], refs[1:-4]
    own_ref, other_ref, chosen_ref, marks_ref = refs[-4:]
    fac = lax.axis_index("fac")
    names = []
    for flip in (0, PRICE_FLIP, SIDE_FLIP, SIDE_FLIP ^ PRICE_FLIP):
        for h in range(held):
            slot = (fac ^ flip) * held + h

            def find(b, name):
                return jnp.where(slot_ref[b] == slot, b, name)

            names.append(lax.fori_loop(0, slot_ref.shape[0], find, 0, unroll=True).astype(jnp.float32))
    trades = packet_refs[0].shape[1]
    place = lax.broadcasted_iota(jnp.int32, (SET_DEV, trades), 0).astype(jnp.float32)
    for source, packet_ref in enumerate(packet_refs):
        at = slice(source * trades, (source + 1) * trades)
        tags = packet_ref[2 * part :, :].astype(jnp.float32)
        weights = [packet_ref[k * part : (k + 1) * part, :].astype(jnp.float32) for k in range(2)]
        for b, name in enumerate(names):
            picked = jnp.where(tags[0:1] == name, weights[0], 0.0)
            picked = jnp.where(tags[1:2] == name, weights[1], picked)
            chosen_ref[b * part : (b + 1) * part, at] = picked.astype(jnp.bfloat16)
        for i, flip in enumerate(flips):
            owner = (fac ^ flip).astype(jnp.float32)
            local = jnp.where(tags[2:3] == owner, tags[3:4], -1.0)
            mark = jnp.where(local == place, 1.0, 0.0)
            marks_ref[i * SET_DEV : (i + 1) * SET_DEV, at] = mark.astype(jnp.bfloat16)
    sums = f32_dot(chosen_ref[...], marks_ref[...], NT)
    half = own_ref.shape[0]
    own_ref[...] = sums[:half]
    other_ref[...] = sums[half:].astype(jnp.bfloat16)


def merge_kernel(own_ref, other_ref, share_ref):
    pair = 2 * SET_DEV
    for at in range(0, own_ref.shape[1], pair):
        other = pltpu.roll(other_ref[:, at : at + pair].astype(jnp.float32), SET_DEV, 1)
        share_ref[:, at : at + pair] = (own_ref[:, at : at + pair] + other).astype(jnp.bfloat16)


def value_kernel(part, held, scen_count, *refs):
    share_refs, price_refs = refs[:scen_count], refs[scen_count : scen_count + 2]
    out_refs, whole_ref = refs[scen_count + 2 : -1], refs[-1]
    scen = lax.axis_index("scen")
    for i, share_ref in enumerate(share_refs):
        column = (scen ^ i) * part
        for b in range(2 * held):
            at = pl.ds(pl.multiple_of(b * BLOCK + column, part), part)
            whole_ref[at, :] = share_ref[b * part : (b + 1) * part, :].astype(jnp.float32)
    width = held * BLOCK
    total = None
    for i, price_ref in enumerate(price_refs):
        whole = whole_ref[i * width : (i + 1) * width, :].T.astype(jnp.bfloat16)
        term = f32_dot(whole, price_ref[...], NT)
        total = term if total is None else total + term
    for p, out_ref in enumerate(out_refs):
        out_ref[...] = total[p * SET_DEV : (p + 1) * SET_DEV].astype(out_ref.dtype)


def exposure_of(part_refs, date, rows):
    at = slice(date * rows, (date + 1) * rows)
    nets = part_refs[0][:, at]
    for ref in part_refs[1:]:
        nets = nets + ref[:, at].astype(jnp.float32)
    return jnp.maximum(nets, 0.0)


def totals_kernel(rows, *refs):
    for date in range(DATES):
        refs[-1][date] = jnp.sum(exposure_of(refs[:-1], date, rows), axis=1)


def expose_kernel(rows, *refs):
    for date in range(DATES):
        refs[-1][date] = exposure_of(refs[:-1], date, rows)


def from_partner(x, axis, flip):
    count = lax.axis_size(axis)
    return lax.ppermute(x, axis, [(i, i ^ flip) for i in range(count)])


def body(
    shocks,
    loadings,
    vol,
    jump_counts,
    jump_noise,
    jump_mean,
    jump_vol,
    dependencies,
    block_slot,
    trade_weights,
    netting,
):
    fac_count = lax.axis_size("fac")
    scen_count = lax.axis_size("scen")
    rows = shocks.shape[1]
    width = loadings.shape[1]
    held = width // BLOCK
    trades = trade_weights.shape[0]
    part = BLOCK // scen_count
    column_flips = [i for i in range(fac_count) if not i & SIDE_FLIP]
    owner_flips = [i for i in range(fac_count) if (i // PRICE_FLIP) % 4 in (0, 3)]

    packet = pl.pallas_call(
        functools.partial(pack_kernel, part),
        out_shape=jax.ShapeDtypeStruct((2 * part + TAGS, trades), jnp.bfloat16),
        in_specs=[VMEM] * 2,
        out_specs=VMEM,
        compiler_params=PARAMS,
        name="pack",
    )(trade_weights, jnp.concatenate([dependencies.T, netting[None]]))
    order = column_flips[1:2] + column_flips[:1:-1]
    packets = [packet] + [from_partner(packet, "fac", i) for i in order]

    packet, shocks = lax.optimization_barrier((packet, shocks))
    inputs = (loadings, vol[None], jump_mean[None], jump_vol[None], shocks, jump_counts, jump_noise)
    prices_shape = jax.ShapeDtypeStruct((DATES, rows, width), jnp.bfloat16)
    prices = pl.pallas_call(
        price_kernel,
        out_shape=prices_shape,
        in_specs=[HBM] * len(inputs),
        out_specs=HBM,
        scratch_shapes=[pltpu.VMEM(x.shape, x.dtype) for x in inputs + (prices_shape,)]
        + [
            pltpu.SemaphoreType.DMA((4,)),
            pltpu.SemaphoreType.DMA((rows // CHUNK, 3)),
            pltpu.SemaphoreType.DMA((rows // CHUNK,)),
        ],
        compiler_params=FETCH_PARAMS,
        name="price",
    )(*inputs)
    prices = prices.reshape(DATES * rows, width)
    share_shape = (2 * held * part, len(owner_flips) * SET_DEV)
    column_trades = len(column_flips) * trades
    own, other = pl.pallas_call(
        functools.partial(combine_kernel, part, held, owner_flips),
        out_shape=[
            jax.ShapeDtypeStruct(share_shape, jnp.float32),
            jax.ShapeDtypeStruct(share_shape, jnp.bfloat16),
        ],
        in_specs=[SMEM] + [VMEM] * len(packets),
        out_specs=[VMEM] * 2,
        scratch_shapes=[
            pltpu.VMEM((2 * share_shape[0], column_trades), jnp.bfloat16),
            pltpu.VMEM((share_shape[1], column_trades), jnp.bfloat16),
        ],
        compiler_params=PARAMS,
        name="combine",
    )(block_slot, *packets)
    prices, other = lax.optimization_barrier((prices, other))
    pair_prices = [prices, from_partner(prices, "fac", PRICE_FLIP)]
    share = pl.pallas_call(
        merge_kernel,
        out_shape=jax.ShapeDtypeStruct(share_shape, jnp.bfloat16),
        in_specs=[VMEM] * 2,
        out_specs=VMEM,
        compiler_params=PARAMS,
        cost_estimate=pl.CostEstimate(flops=10**10, bytes_accessed=0, transcendentals=0),
        name="merge",
    )(own, from_partner(other, "fac", SIDE_FLIP))
    shares = [share]
    for i in range(2, scen_count, 2):
        shares.append(from_partner(share, "scen", i))
    shares = sum([[x, from_partner(x, "scen", 1)] for x in shares], [])

    parts = pl.pallas_call(
        functools.partial(value_kernel, part, held, scen_count),
        out_shape=[
            jax.ShapeDtypeStruct((SET_DEV, DATES * rows), jnp.bfloat16 if flip else jnp.float32)
            for flip in owner_flips
        ],
        in_specs=[VMEM] * (scen_count + 2),
        out_specs=[VMEM] * len(owner_flips),
        scratch_shapes=[pltpu.VMEM((2 * width, share_shape[1]), jnp.float32)],
        compiler_params=PARAMS,
        name="value",
    )(*shares, *pair_prices)
    sends = list(zip(parts[1:], owner_flips[1:]))
    sends = sends[1:] + sends[:1]
    parts = [parts[0]] + [from_partner(x, "fac", i) for x, i in sends]

    totals = pl.pallas_call(
        functools.partial(totals_kernel, rows),
        out_shape=jax.ShapeDtypeStruct((DATES, SET_DEV), jnp.float32),
        in_specs=[VMEM] * len(parts),
        out_specs=VMEM,
        compiler_params=PARAMS,
        name="totals",
    )(*parts)
    exposure = pl.pallas_call(
        functools.partial(expose_kernel, rows),
        out_shape=jax.ShapeDtypeStruct((DATES, SET_DEV, rows), jnp.float32),
        in_specs=[VMEM] * len(parts),
        out_specs=VMEM,
        compiler_params=PARAMS,
        name="expose",
    )(*parts)
    sums = [totals] + [from_partner(totals, "scen", i) for i in range(1, scen_count)]
    while len(sums) > 1:
        sums = [sums[i] + sums[i + 1] for i in range(0, len(sums), 2)]
    return (exposure, sums[0] / (rows * scen_count))


def solution(mesh):
    placed = (
        P(None, "scen", None),
        P(None, "fac"),
        P("fac"),
        P(None, "scen", "fac"),
        P(None, "scen", "fac"),
        P("fac"),
        P("fac"),
        P("fac", None),
        P(),
        P("fac", None, None),
        P("fac"),
    )
    return jax.shard_map(
        body,
        mesh=mesh,
        in_specs=placed,
        out_specs=(P(None, "fac", "scen"), P(None, "fac")),
        check_vma=False,
    )
```

```python
import functools

import jax
import jax.numpy as jnp
from jax import lax
from jax.experimental import pallas as pl
from jax.experimental.pallas import tpu as pltpu
from jax.sharding import PartitionSpec as P

BLOCK = 128
SET_DEV = 64
DATES = 2
SIDE_FLIP = 1
PRICE_FLIP = 2
TAGS = 16
CHUNK = 64

VMEM = pl.BlockSpec(memory_space=pltpu.VMEM)
HBM = pl.BlockSpec(memory_space=pltpu.HBM)
SMEM = pl.BlockSpec(memory_space=pltpu.SMEM)
PARAMS = pltpu.CompilerParams(vmem_limit_bytes=16 * 1024 * 1024)
FETCH_PARAMS = pltpu.CompilerParams(vmem_limit_bytes=60 * 1024 * 1024)
NT = (((1,), (1,)), ((), ()))


def f32_dot(a, b, dims):
    return lax.dot_general(a, b, dims, preferred_element_type=jnp.float32)


def pack_kernel(part, weights_ref, trades_ref, packet_ref):
    scen = lax.axis_index("scen")
    row = lax.broadcasted_iota(jnp.int32, (part, BLOCK), 0)
    column = lax.broadcasted_iota(jnp.int32, (part, BLOCK), 1)
    pick = (column == scen * part + row).astype(jnp.float32).astype(jnp.bfloat16)
    for k in range(2):
        share = f32_dot(pick, weights_ref[:, k, :], NT)
        packet_ref[k * part : (k + 1) * part, :] = share.astype(jnp.bfloat16)
    netting = trades_ref[2:3, :]
    tags = jnp.concatenate(
        [
            trades_ref[:2, :],
            netting // SET_DEV,
            netting % SET_DEV,
            jnp.zeros((TAGS - 4, netting.shape[1]), jnp.int32),
        ],
        axis=0,
    )
    packet_ref[2 * part :, :] = tags.astype(jnp.float32).astype(jnp.bfloat16)


def price_kernel(*refs):
    sources, out_hbm, held_refs, out_ref = refs[:7], refs[7], refs[8:15], refs[15]
    sems, chunk_sems, out_sems = refs[16:]
    loadings_ref, vol_ref, mean_ref, dev_ref, shocks_ref, counts_ref, noise_ref = held_refs
    rows = shocks_ref.shape[1]
    fixed = [
        pltpu.make_async_copy(src, dst, sems.at[i])
        for i, (src, dst) in enumerate(zip(sources[:4], held_refs[:4]))
    ]
    chunks = [
        [
            pltpu.make_async_copy(src.at[:, pl.ds(at, CHUNK)], dst.at[:, pl.ds(at, CHUNK)], chunk_sems.at[i, j])
            for j, (src, dst) in enumerate(zip(sources[4:], held_refs[4:]))
        ]
        for i, at in enumerate(range(0, rows, CHUNK))
    ]
    results = [
        pltpu.make_async_copy(out_ref.at[:, pl.ds(at, CHUNK)], out_hbm.at[:, pl.ds(at, CHUNK)], out_sems.at[i])
        for i, at in enumerate(range(0, rows, CHUNK))
    ]
    for copy in fixed + sum(chunks, []):
        copy.start()
    for copy in fixed:
        copy.wait()
    vol = vol_ref[...]
    drift = 0.5 * vol * vol
    mean = mean_ref[...]
    dev = dev_ref[...]
    loadings = loadings_ref[...]
    for i, copies in enumerate(chunks):
        for copy in copies:
            copy.wait()
        at = slice(i * CHUNK, (i + 1) * CHUNK)
        level = jnp.zeros((CHUNK, vol.shape[1]), jnp.float32)
        for date in range(DATES):
            diffuse = jnp.dot(shocks_ref[date, at, :], loadings, preferred_element_type=jnp.float32)
            counts = counts_ref[date, at, :].astype(jnp.float32)
            noise = noise_ref[date, at, :].astype(jnp.float32)
            level = level + vol * diffuse - drift + counts * mean + jnp.sqrt(counts) * dev * noise
            out_ref[date, at, :] = (jnp.exp(level) - 1.0).astype(jnp.bfloat16)
        results[i].start()
    for copy in results:
        copy.wait()


def combine_kernel(part, held, flips, *refs):
    slot_ref, packet_refs = refs[0], refs[1:-5]
    own_ref, narrow_ref, other_ref, chosen_ref, marks_ref = refs[-5:]
    fac = lax.axis_index("fac")
    names = []
    for flip in (0, PRICE_FLIP, SIDE_FLIP, SIDE_FLIP ^ PRICE_FLIP):
        for h in range(held):
            slot = (fac ^ flip) * held + h

            def find(b, name):
                return jnp.where(slot_ref[b] == slot, b, name)

            names.append(lax.fori_loop(0, slot_ref.shape[0], find, 0, unroll=True).astype(jnp.float32))
    trades = packet_refs[0].shape[1]
    place = lax.broadcasted_iota(jnp.int32, (SET_DEV, trades), 0).astype(jnp.float32)
    for source, packet_ref in enumerate(packet_refs):
        at = slice(source * trades, (source + 1) * trades)
        tags = packet_ref[2 * part :, :].astype(jnp.float32)
        weights = [packet_ref[k * part : (k + 1) * part, :].astype(jnp.float32) for k in range(2)]
        for b, name in enumerate(names):
            picked = jnp.where(tags[0:1] == name, weights[0], 0.0)
            picked = jnp.where(tags[1:2] == name, weights[1], picked)
            chosen_ref[b * part : (b + 1) * part, at] = picked.astype(jnp.bfloat16)
        for i, flip in enumerate(flips):
            owner = (fac ^ flip).astype(jnp.float32)
            local = jnp.where(tags[2:3] == owner, tags[3:4], -1.0)
            mark = jnp.where(local == place, 1.0, 0.0)
            marks_ref[i * SET_DEV : (i + 1) * SET_DEV, at] = mark.astype(jnp.bfloat16)
    sums = f32_dot(chosen_ref[...], marks_ref[...], NT)
    half = own_ref.shape[0]
    own_ref[...] = sums[:half]
    narrow_ref[...] = sums[:half].astype(jnp.bfloat16)
    other_ref[...] = sums[half:].astype(jnp.bfloat16)


def merge_kernel(*refs):
    part_refs, shares_ref = refs[:-1], refs[-1]
    rows, columns = part_refs[0].shape
    pair = 2 * SET_DEV
    for i in range(len(part_refs) // 2):
        own_ref, other_ref = part_refs[2 * i : 2 * i + 2]
        for at in range(0, columns, pair):
            own = own_ref[:, at : at + pair].astype(jnp.float32)
            other = pltpu.roll(other_ref[:, at : at + pair].astype(jnp.float32), SET_DEV, 1)
            shares_ref[i * rows : (i + 1) * rows, at : at + pair] = (own + other).astype(jnp.bfloat16)


def value_kernel(part, held, scen_count, *refs):
    cores_refs, price_refs = refs[:2], refs[2:4]
    out_refs, whole_ref = refs[4:-1], refs[-1]
    scen = lax.axis_index("scen")
    for i in range(scen_count):
        column = (scen ^ i) * part
        for b in range(2 * held):
            row = (i // 2 * 2 * held + b) * part
            at = pl.ds(pl.multiple_of(b * BLOCK + column, part), part)
            whole_ref[at, :] = cores_refs[i % 2][row : row + part, :].astype(jnp.float32)
    width = held * BLOCK
    total = None
    for i, price_ref in enumerate(price_refs):
        whole = whole_ref[i * width : (i + 1) * width, :].T.astype(jnp.bfloat16)
        term = f32_dot(whole, price_ref[...], NT)
        total = term if total is None else total + term
    for p, out_ref in enumerate(out_refs):
        out_ref[...] = total[p * SET_DEV : (p + 1) * SET_DEV].astype(out_ref.dtype)


def exposure_of(part_refs, date, rows):
    at = slice(date * rows, (date + 1) * rows)
    nets = part_refs[0][:, at]
    for ref in part_refs[1:]:
        nets = nets + ref[:, at].astype(jnp.float32)
    return jnp.maximum(nets, 0.0)


def totals_kernel(rows, *refs):
    for date in range(DATES):
        refs[-1][date] = jnp.sum(exposure_of(refs[:-1], date, rows), axis=1)


def expose_kernel(rows, *refs):
    for date in range(DATES):
        refs[-1][date] = exposure_of(refs[:-1], date, rows)


def from_partner(x, axis, flip):
    count = lax.axis_size(axis)
    return lax.ppermute(x, axis, [(i, i ^ flip) for i in range(count)])


def from_both(x, scen_flip, fac_flip):
    count = lax.axis_size("fac")
    pairs = [
        (i * count + j, (i ^ scen_flip) * count + (j ^ fac_flip))
        for i in range(lax.axis_size("scen"))
        for j in range(count)
    ]
    return lax.ppermute(x, ("scen", "fac"), pairs)


def body(
    shocks,
    loadings,
    vol,
    jump_counts,
    jump_noise,
    jump_mean,
    jump_vol,
    dependencies,
    block_slot,
    trade_weights,
    netting,
):
    fac_count = lax.axis_size("fac")
    scen_count = lax.axis_size("scen")
    rows = shocks.shape[1]
    width = loadings.shape[1]
    held = width // BLOCK
    trades = trade_weights.shape[0]
    part = BLOCK // scen_count
    column_flips = [i for i in range(fac_count) if not i & SIDE_FLIP]
    owner_flips = [i for i in range(fac_count) if (i // PRICE_FLIP) % 4 in (0, 3)]

    packet = pl.pallas_call(
        functools.partial(pack_kernel, part),
        out_shape=jax.ShapeDtypeStruct((2 * part + TAGS, trades), jnp.bfloat16),
        in_specs=[VMEM] * 2,
        out_specs=VMEM,
        compiler_params=PARAMS,
        name="pack",
    )(trade_weights, jnp.concatenate([dependencies.T, netting[None]]))
    order = column_flips[1:2] + column_flips[:1:-1]
    packets = [packet] + [from_partner(packet, "fac", i) for i in order]

    packet, shocks = lax.optimization_barrier((packet, shocks))
    inputs = (loadings, vol[None], jump_mean[None], jump_vol[None], shocks, jump_counts, jump_noise)
    prices_shape = jax.ShapeDtypeStruct((DATES, rows, width), jnp.bfloat16)
    prices = pl.pallas_call(
        price_kernel,
        out_shape=prices_shape,
        in_specs=[HBM] * len(inputs),
        out_specs=HBM,
        scratch_shapes=[pltpu.VMEM(x.shape, x.dtype) for x in inputs + (prices_shape,)]
        + [
            pltpu.SemaphoreType.DMA((4,)),
            pltpu.SemaphoreType.DMA((rows // CHUNK, 3)),
            pltpu.SemaphoreType.DMA((rows // CHUNK,)),
        ],
        compiler_params=FETCH_PARAMS,
        name="price",
    )(*inputs)
    prices = prices.reshape(DATES * rows, width)
    prices, *packets = lax.optimization_barrier((prices, *packets))
    share_shape = (2 * held * part, len(owner_flips) * SET_DEV)
    column_trades = len(column_flips) * trades
    own, narrow, other = pl.pallas_call(
        functools.partial(combine_kernel, part, held, owner_flips),
        out_shape=[
            jax.ShapeDtypeStruct(share_shape, jnp.float32),
            jax.ShapeDtypeStruct(share_shape, jnp.bfloat16),
            jax.ShapeDtypeStruct(share_shape, jnp.bfloat16),
        ],
        in_specs=[SMEM] + [VMEM] * len(packets),
        out_specs=[VMEM] * 3,
        scratch_shapes=[
            pltpu.VMEM((2 * share_shape[0], column_trades), jnp.bfloat16),
            pltpu.VMEM((share_shape[1], column_trades), jnp.bfloat16),
        ],
        compiler_params=PARAMS,
        name="combine",
    )(block_slot, *packets)
    pair_prices = [prices, from_partner(prices, "fac", PRICE_FLIP)]
    parts = []
    for i in range(0, scen_count, 2):
        parts.append(from_partner(narrow, "scen", i) if i else own)
        parts.append(from_both(other, i, SIDE_FLIP))
    shares = pl.pallas_call(
        merge_kernel,
        out_shape=jax.ShapeDtypeStruct((len(parts) // 2 * share_shape[0], share_shape[1]), jnp.bfloat16),
        in_specs=[VMEM] * len(parts),
        out_specs=VMEM,
        compiler_params=PARAMS,
        name="merge",
    )(*parts)
    shares = [shares, from_partner(shares, "scen", 1)]

    parts = pl.pallas_call(
        functools.partial(value_kernel, part, held, scen_count),
        out_shape=[
            jax.ShapeDtypeStruct((SET_DEV, DATES * rows), jnp.bfloat16 if flip else jnp.float32)
            for flip in owner_flips
        ],
        in_specs=[VMEM] * 4,
        out_specs=[VMEM] * len(owner_flips),
        scratch_shapes=[pltpu.VMEM((2 * width, share_shape[1]), jnp.float32)],
        compiler_params=PARAMS,
        name="value",
    )(*shares, *pair_prices)
    sends = list(zip(parts[1:], owner_flips[1:]))
    sends = sends[1:] + sends[:1]
    parts = [parts[0]] + [from_partner(x, "fac", i) for x, i in sends]

    totals = pl.pallas_call(
        functools.partial(totals_kernel, rows),
        out_shape=jax.ShapeDtypeStruct((DATES, SET_DEV), jnp.float32),
        in_specs=[VMEM] * len(parts),
        out_specs=VMEM,
        compiler_params=PARAMS,
        name="totals",
    )(*parts)
    exposure = pl.pallas_call(
        functools.partial(expose_kernel, rows),
        out_shape=jax.ShapeDtypeStruct((DATES, SET_DEV, rows), jnp.float32),
        in_specs=[VMEM] * len(parts),
        out_specs=VMEM,
        compiler_params=PARAMS,
        name="expose",
    )(*parts)
    sums = [totals] + [None] * (scen_count - 1)
    for i in [*range(1, scen_count, 2), *range(2, scen_count, 2)]:
        sums[i] = from_partner(totals, "scen", i)
    while len(sums) > 1:
        sums = [sums[i] + sums[i + 1] for i in range(0, len(sums), 2)]
    return (exposure, sums[0] / (rows * scen_count))


def solution(mesh):
    placed = (
        P(None, "scen", None),
        P(None, "fac"),
        P("fac"),
        P(None, "scen", "fac"),
        P(None, "scen", "fac"),
        P("fac"),
        P("fac"),
        P("fac", None),
        P(),
        P("fac", None, None),
        P("fac"),
    )
    return jax.shard_map(
        body,
        mesh=mesh,
        in_specs=placed,
        out_specs=(P(None, "fac", "scen"), P(None, "fac")),
        check_vma=False,
    )
```

```python
import functools

import jax
import jax.numpy as jnp
from jax import lax
from jax.experimental import pallas as pl
from jax.experimental.pallas import tpu as pltpu
from jax.sharding import PartitionSpec as P

BLOCK = 128
SET_DEV = 64
DATES = 2
SIDE_FLIP = 1
PRICE_FLIP = 2
TAGS = 16
CHUNK = 64

VMEM = pl.BlockSpec(memory_space=pltpu.VMEM)
HBM = pl.BlockSpec(memory_space=pltpu.HBM)
SMEM = pl.BlockSpec(memory_space=pltpu.SMEM)
PARAMS = pltpu.CompilerParams(vmem_limit_bytes=16 * 1024 * 1024)
NT = (((1,), (1,)), ((), ()))


def f32_dot(a, b, dims):
    return lax.dot_general(a, b, dims, preferred_element_type=jnp.float32)


def pick_kernel(part, pick_ref):
    row = lax.broadcasted_iota(jnp.int32, pick_ref.shape, 0)
    column = lax.broadcasted_iota(jnp.int32, pick_ref.shape, 1)
    pick = column == lax.axis_index("scen") * part + row
    pick_ref[...] = pick.astype(jnp.float32).astype(jnp.bfloat16)


def pack_kernel(part, pick_ref, weights_ref, deps_ref, netting_ref, packet_ref):
    for k in range(2):
        share = f32_dot(pick_ref[...], weights_ref[:, k, :], NT)
        packet_ref[k * part : (k + 1) * part, :] = share[:part].astype(jnp.bfloat16)
    netting = netting_ref[...]
    tags = jnp.concatenate(
        [
            deps_ref[...],
            netting // SET_DEV,
            netting % SET_DEV,
            jnp.zeros((TAGS - 4, netting.shape[1]), jnp.int32),
        ],
        axis=0,
    )
    packet_ref[2 * part :, :] = tags.astype(jnp.float32).astype(jnp.bfloat16)


def price_kernel(shocks_ref, loadings_ref, vol_ref, counts_ref, noise_ref, mean_ref, dev_ref, out_ref):
    rows = shocks_ref.shape[1]
    vol = vol_ref[...]
    drift = 0.5 * vol * vol
    mean = mean_ref[...]
    dev = dev_ref[...]
    loadings = loadings_ref[...]
    for i in range(0, rows, CHUNK):
        at = slice(i, i + CHUNK)
        level = jnp.zeros((CHUNK, vol.shape[1]), jnp.float32)
        for date in range(DATES):
            diffuse = jnp.dot(shocks_ref[date, at, :], loadings, preferred_element_type=jnp.float32)
            counts = counts_ref[date, at, :].astype(jnp.float32)
            noise = noise_ref[date, at, :].astype(jnp.float32)
            level = level + vol * diffuse - drift + counts * mean + jnp.sqrt(counts) * dev * noise
            out_ref[date * rows + i : date * rows + i + CHUNK, :] = (jnp.exp(level) - 1.0).astype(
                jnp.bfloat16
            )


def combine_kernel(part, held, flips, *refs):
    slot_ref, packet_refs = refs[0], refs[1:-5]
    own_ref, narrow_ref, other_ref, chosen_ref, marks_ref = refs[-5:]
    fac = lax.axis_index("fac")
    names = []
    for flip in (0, PRICE_FLIP, SIDE_FLIP, SIDE_FLIP ^ PRICE_FLIP):
        for h in range(held):
            slot = (fac ^ flip) * held + h

            def find(b, name):
                return jnp.where(slot_ref[b] == slot, b, name)

            names.append(lax.fori_loop(0, slot_ref.shape[0], find, 0, unroll=True).astype(jnp.float32))
    trades = packet_refs[0].shape[1]
    place = lax.broadcasted_iota(jnp.int32, (SET_DEV, trades), 0).astype(jnp.float32)
    for source, packet_ref in enumerate(packet_refs):
        at = slice(source * trades, (source + 1) * trades)
        tags = packet_ref[2 * part :, :].astype(jnp.float32)
        weights = [packet_ref[k * part : (k + 1) * part, :].astype(jnp.float32) for k in range(2)]
        for b, name in enumerate(names):
            picked = jnp.where(tags[0:1] == name, weights[0], 0.0)
            picked = jnp.where(tags[1:2] == name, weights[1], picked)
            chosen_ref[b * part : (b + 1) * part, at] = picked.astype(jnp.bfloat16)
        for i, flip in enumerate(flips):
            owner = (fac ^ flip).astype(jnp.float32)
            local = jnp.where(tags[2:3] == owner, tags[3:4], -1.0)
            mark = jnp.where(local == place, 1.0, 0.0)
            marks_ref[i * SET_DEV : (i + 1) * SET_DEV, at] = mark.astype(jnp.bfloat16)
    sums = f32_dot(chosen_ref[...], marks_ref[...], NT)
    half = own_ref.shape[0]
    own_ref[...] = sums[:half]
    narrow_ref[...] = sums[:half].astype(jnp.bfloat16)
    other_ref[...] = sums[half:].astype(jnp.bfloat16)


def merge_kernel(*refs):
    part_refs, shares_ref = refs[:-1], refs[-1]
    rows, columns = part_refs[0].shape
    pair = 2 * SET_DEV
    for i in range(len(part_refs) // 2):
        own_ref, other_ref = part_refs[2 * i : 2 * i + 2]
        for at in range(0, columns, pair):
            own = own_ref[:, at : at + pair].astype(jnp.float32)
            other = pltpu.roll(other_ref[:, at : at + pair].astype(jnp.float32), SET_DEV, 1)
            shares_ref[i * rows : (i + 1) * rows, at : at + pair] = (own + other).astype(jnp.bfloat16)


def value_kernel(part, held, scen_count, *refs):
    cores_refs, price_refs = refs[:2], refs[2:4]
    out_refs, whole_ref = refs[4:-1], refs[-1]
    scen = lax.axis_index("scen")
    for i in range(scen_count):
        column = (scen ^ i) * part
        for b in range(2 * held):
            row = (i // 2 * 2 * held + b) * part
            at = pl.ds(pl.multiple_of(b * BLOCK + column, part), part)
            whole_ref[at, :] = cores_refs[i % 2][row : row + part, :].astype(jnp.float32)
    width = held * BLOCK
    total = None
    for i, price_ref in enumerate(price_refs):
        whole = whole_ref[i * width : (i + 1) * width, :].T.astype(jnp.bfloat16)
        term = f32_dot(whole, price_ref[...], NT)
        total = term if total is None else total + term
    for p, out_ref in enumerate(out_refs):
        out_ref[...] = total[p * SET_DEV : (p + 1) * SET_DEV].astype(out_ref.dtype)


def exposure_of(part_refs, date, rows):
    at = slice(date * rows, (date + 1) * rows)
    nets = part_refs[0][:, at]
    for ref in part_refs[1:]:
        nets = nets + ref[:, at].astype(jnp.float32)
    return jnp.maximum(nets, 0.0)


def totals_kernel(rows, *refs):
    for date in range(DATES):
        refs[-1][date] = jnp.sum(exposure_of(refs[:-1], date, rows), axis=1)


def expose_kernel(rows, *refs):
    for date in range(DATES):
        refs[-1][date] = exposure_of(refs[:-1], date, rows)


def from_partner(x, axis, flip):
    count = lax.axis_size(axis)
    return lax.ppermute(x, axis, [(i, i ^ flip) for i in range(count)])


def from_both(x, scen_flip, fac_flip):
    count = lax.axis_size("fac")
    pairs = [
        (i * count + j, (i ^ scen_flip) * count + (j ^ fac_flip))
        for i in range(lax.axis_size("scen"))
        for j in range(count)
    ]
    return lax.ppermute(x, ("scen", "fac"), pairs)


def body(
    shocks,
    loadings,
    vol,
    jump_counts,
    jump_noise,
    jump_mean,
    jump_vol,
    dependencies,
    block_slot,
    trade_weights,
    netting,
):
    fac_count = lax.axis_size("fac")
    scen_count = lax.axis_size("scen")
    rows = shocks.shape[1]
    width = loadings.shape[1]
    held = width // BLOCK
    trades = trade_weights.shape[0]
    part = BLOCK // scen_count
    column_flips = [i for i in range(fac_count) if not i & SIDE_FLIP]
    owner_flips = [i for i in range(fac_count) if (i // PRICE_FLIP) % 4 in (0, 3)]

    pick = pl.pallas_call(
        functools.partial(pick_kernel, part),
        out_shape=jax.ShapeDtypeStruct((max(part, 16), BLOCK), jnp.bfloat16),
        out_specs=VMEM,
        compiler_params=PARAMS,
        cost_estimate=pl.CostEstimate(flops=10**10, bytes_accessed=0, transcendentals=0),
        name="pick",
    )()
    packet = pl.pallas_call(
        functools.partial(pack_kernel, part),
        out_shape=jax.ShapeDtypeStruct((2 * part + TAGS, trades), jnp.bfloat16),
        in_specs=[VMEM] * 4,
        out_specs=VMEM,
        compiler_params=PARAMS,
        name="pack",
    )(pick, trade_weights, dependencies.T, netting[None])
    order = column_flips[1:2] + column_flips[:1:-1]
    packets = [packet] + [from_partner(packet, "fac", i) for i in order]

    packet, shocks = lax.optimization_barrier((packet, shocks))
    prices = pl.pallas_call(
        price_kernel,
        out_shape=jax.ShapeDtypeStruct((DATES * rows, width), jnp.bfloat16),
        in_specs=[VMEM] * 7,
        out_specs=VMEM,
        compiler_params=PARAMS,
        name="price",
    )(shocks, loadings, vol[None], jump_counts, jump_noise, jump_mean[None], jump_vol[None])
    prices, *packets = lax.optimization_barrier((prices, *packets))
    share_shape = (2 * held * part, len(owner_flips) * SET_DEV)
    column_trades = len(column_flips) * trades
    own, narrow, other = pl.pallas_call(
        functools.partial(combine_kernel, part, held, owner_flips),
        out_shape=[
            jax.ShapeDtypeStruct(share_shape, jnp.float32),
            jax.ShapeDtypeStruct(share_shape, jnp.bfloat16),
            jax.ShapeDtypeStruct(share_shape, jnp.bfloat16),
        ],
        in_specs=[SMEM] + [VMEM] * len(packets),
        out_specs=[VMEM] * 3,
        scratch_shapes=[
            pltpu.VMEM((2 * share_shape[0], column_trades), jnp.bfloat16),
            pltpu.VMEM((share_shape[1], column_trades), jnp.bfloat16),
        ],
        compiler_params=PARAMS,
        name="combine",
    )(block_slot, *packets)
    pair_prices = [prices, from_partner(prices, "fac", PRICE_FLIP)]
    parts = []
    for i in range(0, scen_count, 2):
        parts.append(from_partner(narrow, "scen", i) if i else own)
        parts.append(from_both(other, i, SIDE_FLIP))
    shares = pl.pallas_call(
        merge_kernel,
        out_shape=jax.ShapeDtypeStruct((len(parts) // 2 * share_shape[0], share_shape[1]), jnp.bfloat16),
        in_specs=[VMEM] * len(parts),
        out_specs=VMEM,
        compiler_params=PARAMS,
        name="merge",
    )(*parts)
    shares = [shares, from_partner(shares, "scen", 1)]

    parts = pl.pallas_call(
        functools.partial(value_kernel, part, held, scen_count),
        out_shape=[
            jax.ShapeDtypeStruct((SET_DEV, DATES * rows), jnp.bfloat16 if flip else jnp.float32)
            for flip in owner_flips
        ],
        in_specs=[VMEM] * 4,
        out_specs=[VMEM] * len(owner_flips),
        scratch_shapes=[pltpu.VMEM((2 * width, share_shape[1]), jnp.float32)],
        compiler_params=PARAMS,
        name="value",
    )(*shares, *pair_prices)
    sends = list(zip(parts[1:], owner_flips[1:]))
    sends = sends[1:] + sends[:1]
    parts = [parts[0]] + [from_partner(x, "fac", i) for x, i in sends]

    totals = pl.pallas_call(
        functools.partial(totals_kernel, rows),
        out_shape=jax.ShapeDtypeStruct((DATES, SET_DEV), jnp.float32),
        in_specs=[VMEM] * len(parts),
        out_specs=VMEM,
        compiler_params=PARAMS,
        name="totals",
    )(*parts)
    exposure = pl.pallas_call(
        functools.partial(expose_kernel, rows),
        out_shape=jax.ShapeDtypeStruct((DATES, SET_DEV, rows), jnp.float32),
        in_specs=[VMEM] * len(parts),
        out_specs=VMEM,
        compiler_params=PARAMS,
        name="expose",
    )(*parts)
    sums = [totals] + [None] * (scen_count - 1)
    for i in [*range(1, scen_count, 2), *range(2, scen_count, 2)]:
        sums[i] = from_partner(totals, "scen", i)
    while len(sums) > 1:
        sums = [sums[i] + sums[i + 1] for i in range(0, len(sums), 2)]
    return (exposure, sums[0] / (rows * scen_count))


def solution(mesh):
    placed = (
        P(None, "scen", None),
        P(None, "fac"),
        P("fac"),
        P(None, "scen", "fac"),
        P(None, "scen", "fac"),
        P("fac"),
        P("fac"),
        P("fac", None),
        P(),
        P("fac", None, None),
        P("fac"),
    )
    return jax.shard_map(
        body,
        mesh=mesh,
        in_specs=placed,
        out_specs=(P(None, "fac", "scen"), P(None, "fac")),
        check_vma=False,
    )
```

```python
import functools

import jax
import jax.numpy as jnp
from jax import lax
from jax.experimental import pallas as pl
from jax.experimental.pallas import tpu as pltpu
from jax.sharding import PartitionSpec as P

BLOCK = 128
SET_DEV = 64
DATES = 2
SIDE_FLIP = 1
PRICE_FLIP = 2
TAGS = 16
CHUNK = 64

VMEM = pl.BlockSpec(memory_space=pltpu.VMEM)
HBM = pl.BlockSpec(memory_space=pltpu.HBM)
SMEM = pl.BlockSpec(memory_space=pltpu.SMEM)
PARAMS = pltpu.CompilerParams(vmem_limit_bytes=16 * 1024 * 1024)
NT = (((1,), (1,)), ((), ()))


def f32_dot(a, b, dims):
    return lax.dot_general(a, b, dims, preferred_element_type=jnp.float32)


def pick_kernel(part, pick_ref):
    row = lax.broadcasted_iota(jnp.int32, pick_ref.shape, 0)
    column = lax.broadcasted_iota(jnp.int32, pick_ref.shape, 1)
    pick = column == lax.axis_index("scen") * part + row
    pick_ref[...] = pick.astype(jnp.float32).astype(jnp.bfloat16)


def pack_kernel(part, pick_ref, weights_ref, deps_ref, netting_ref, packet_ref):
    for k in range(2):
        share = f32_dot(pick_ref[...], weights_ref[:, k, :], NT)
        packet_ref[k * part : (k + 1) * part, :] = share[:part].astype(jnp.bfloat16)
    netting = netting_ref[...]
    tags = jnp.concatenate(
        [
            deps_ref[...],
            netting // SET_DEV,
            netting % SET_DEV,
            jnp.zeros((TAGS - 4, netting.shape[1]), jnp.int32),
        ],
        axis=0,
    )
    packet_ref[2 * part :, :] = tags.astype(jnp.float32).astype(jnp.bfloat16)


def price_kernel(shocks_ref, loadings_ref, vol_ref, counts_ref, noise_ref, mean_ref, dev_ref, out_ref):
    rows = shocks_ref.shape[1]
    vol = vol_ref[...]
    drift = 0.5 * vol * vol
    mean = mean_ref[...]
    dev = dev_ref[...]
    loadings = loadings_ref[...]
    for i in range(0, rows, CHUNK):
        at = slice(i, i + CHUNK)
        level = jnp.zeros((CHUNK, vol.shape[1]), jnp.float32)
        for date in range(DATES):
            diffuse = jnp.dot(shocks_ref[date, at, :], loadings, preferred_element_type=jnp.float32)
            counts = counts_ref[date, at, :].astype(jnp.float32)
            noise = noise_ref[date, at, :].astype(jnp.float32)
            level = level + vol * diffuse - drift + counts * mean + jnp.sqrt(counts) * dev * noise
            out_ref[date * rows + i : date * rows + i + CHUNK, :] = (jnp.exp(level) - 1.0).astype(
                jnp.bfloat16
            )


def combine_kernel(part, held, flips, *refs):
    slot_ref, packet_refs = refs[0], refs[1:-5]
    own_ref, narrow_ref, other_ref, chosen_ref, marks_ref = refs[-5:]
    fac = lax.axis_index("fac")
    names = []
    for flip in (0, PRICE_FLIP, SIDE_FLIP, SIDE_FLIP ^ PRICE_FLIP):
        for h in range(held):
            slot = (fac ^ flip) * held + h

            def find(b, name):
                return jnp.where(slot_ref[b] == slot, b, name)

            names.append(lax.fori_loop(0, slot_ref.shape[0], find, 0, unroll=True).astype(jnp.float32))
    trades = packet_refs[0].shape[1]
    place = lax.broadcasted_iota(jnp.int32, (SET_DEV, trades), 0).astype(jnp.float32)
    for source, packet_ref in enumerate(packet_refs):
        at = slice(source * trades, (source + 1) * trades)
        tags = packet_ref[2 * part :, :].astype(jnp.float32)
        weights = [packet_ref[k * part : (k + 1) * part, :].astype(jnp.float32) for k in range(2)]
        for b, name in enumerate(names):
            picked = jnp.where(tags[0:1] == name, weights[0], 0.0)
            picked = jnp.where(tags[1:2] == name, weights[1], picked)
            chosen_ref[b * part : (b + 1) * part, at] = picked.astype(jnp.bfloat16)
        for i, flip in enumerate(flips):
            owner = (fac ^ flip).astype(jnp.float32)
            local = jnp.where(tags[2:3] == owner, tags[3:4], -1.0)
            mark = jnp.where(local == place, 1.0, 0.0)
            marks_ref[i * SET_DEV : (i + 1) * SET_DEV, at] = mark.astype(jnp.bfloat16)
    sums = f32_dot(chosen_ref[...], marks_ref[...], NT)
    half = own_ref.shape[0]
    own_ref[...] = sums[:half]
    narrow_ref[...] = sums[:half].astype(jnp.bfloat16)
    other_ref[...] = sums[half:].astype(jnp.bfloat16)


def merge_kernel(*refs):
    part_refs, shares_ref = refs[:-1], refs[-1]
    rows, columns = part_refs[0].shape
    pair = 2 * SET_DEV
    for i in range(len(part_refs) // 2):
        own_ref, other_ref = part_refs[2 * i : 2 * i + 2]
        for at in range(0, columns, pair):
            own = own_ref[:, at : at + pair].astype(jnp.float32)
            other = pltpu.roll(other_ref[:, at : at + pair].astype(jnp.float32), SET_DEV, 1)
            shares_ref[i * rows : (i + 1) * rows, at : at + pair] = (own + other).astype(jnp.bfloat16)


def value_kernel(part, held, scen_count, *refs):
    cores_refs, price_refs = refs[:2], refs[2:4]
    out_refs, whole_ref = refs[4:-1], refs[-1]
    scen = lax.axis_index("scen")
    for i in range(scen_count):
        column = (scen ^ i) * part
        for b in range(2 * held):
            row = (i // 2 * 2 * held + b) * part
            at = pl.ds(pl.multiple_of(b * BLOCK + column, part), part)
            whole_ref[at, :] = cores_refs[i % 2][row : row + part, :].astype(jnp.float32)
    width = held * BLOCK
    total = None
    for i, price_ref in enumerate(price_refs):
        whole = whole_ref[i * width : (i + 1) * width, :].T.astype(jnp.bfloat16)
        term = f32_dot(whole, price_ref[...], NT)
        total = term if total is None else total + term
    for p, out_ref in enumerate(out_refs):
        out_ref[...] = total[p * SET_DEV : (p + 1) * SET_DEV].astype(out_ref.dtype)


def exposure_of(part_refs, date, rows):
    at = slice(date * rows, (date + 1) * rows)
    nets = part_refs[0][:, at]
    for ref in part_refs[1:]:
        nets = nets + ref[:, at].astype(jnp.float32)
    return jnp.maximum(nets, 0.0)


def totals_kernel(rows, *refs):
    for date in range(DATES):
        refs[-1][date] = jnp.sum(exposure_of(refs[:-1], date, rows), axis=1)


def expose_kernel(rows, *refs):
    for date in range(DATES):
        refs[-1][date] = exposure_of(refs[:-1], date, rows)


def from_partner(x, axis, flip):
    count = lax.axis_size(axis)
    return lax.ppermute(x, axis, [(i, i ^ flip) for i in range(count)])


def from_both(x, scen_flip, fac_flip):
    count = lax.axis_size("fac")
    pairs = [
        (i * count + j, (i ^ scen_flip) * count + (j ^ fac_flip))
        for i in range(lax.axis_size("scen"))
        for j in range(count)
    ]
    return lax.ppermute(x, ("scen", "fac"), pairs)


def body(
    shocks,
    loadings,
    vol,
    jump_counts,
    jump_noise,
    jump_mean,
    jump_vol,
    dependencies,
    block_slot,
    trade_weights,
    netting,
):
    fac_count = lax.axis_size("fac")
    scen_count = lax.axis_size("scen")
    rows = shocks.shape[1]
    width = loadings.shape[1]
    held = width // BLOCK
    trades = trade_weights.shape[0]
    part = BLOCK // scen_count
    column_flips = [i for i in range(fac_count) if not i & SIDE_FLIP]
    owner_flips = [i for i in range(fac_count) if (i // PRICE_FLIP) % 4 in (0, 3)]

    pick = pl.pallas_call(
        functools.partial(pick_kernel, part),
        out_shape=jax.ShapeDtypeStruct((max(part, 16), BLOCK), jnp.bfloat16),
        out_specs=VMEM,
        compiler_params=PARAMS,
        cost_estimate=pl.CostEstimate(flops=10**10, bytes_accessed=0, transcendentals=0),
        name="pick",
    )()
    packet = pl.pallas_call(
        functools.partial(pack_kernel, part),
        out_shape=jax.ShapeDtypeStruct((2 * part + TAGS, trades), jnp.bfloat16),
        in_specs=[VMEM] * 4,
        out_specs=VMEM,
        compiler_params=PARAMS,
        name="pack",
    )(pick, trade_weights, dependencies.T, netting[None])
    order = column_flips[1:2] + column_flips[:1:-1]
    packets = [packet] + [from_partner(packet, "fac", i) for i in order]

    packet, shocks = lax.optimization_barrier((packet, shocks))
    prices = pl.pallas_call(
        price_kernel,
        out_shape=jax.ShapeDtypeStruct((DATES * rows, width), jnp.bfloat16),
        in_specs=[VMEM] * 7,
        out_specs=VMEM,
        compiler_params=PARAMS,
        name="price",
    )(shocks, loadings, vol[None], jump_counts, jump_noise, jump_mean[None], jump_vol[None])
    share_shape = (2 * held * part, len(owner_flips) * SET_DEV)
    column_trades = len(column_flips) * trades
    own, narrow, other = pl.pallas_call(
        functools.partial(combine_kernel, part, held, owner_flips),
        out_shape=[
            jax.ShapeDtypeStruct(share_shape, jnp.float32),
            jax.ShapeDtypeStruct(share_shape, jnp.bfloat16),
            jax.ShapeDtypeStruct(share_shape, jnp.bfloat16),
        ],
        in_specs=[SMEM] + [VMEM] * len(packets),
        out_specs=[VMEM] * 3,
        scratch_shapes=[
            pltpu.VMEM((2 * share_shape[0], column_trades), jnp.bfloat16),
            pltpu.VMEM((share_shape[1], column_trades), jnp.bfloat16),
        ],
        compiler_params=PARAMS,
        cost_estimate=pl.CostEstimate(flops=10**9, bytes_accessed=0, transcendentals=0),
        name="combine",
    )(block_slot, *packets)
    pair_prices = [prices, from_partner(prices, "fac", PRICE_FLIP)]
    parts = []
    for i in range(0, scen_count, 2):
        parts.append(from_partner(narrow, "scen", i) if i else own)
        parts.append(from_both(other, i, SIDE_FLIP))
    shares = pl.pallas_call(
        merge_kernel,
        out_shape=jax.ShapeDtypeStruct((len(parts) // 2 * share_shape[0], share_shape[1]), jnp.bfloat16),
        in_specs=[VMEM] * len(parts),
        out_specs=VMEM,
        compiler_params=PARAMS,
        name="merge",
    )(*parts)
    shares = [shares, from_partner(shares, "scen", 1)]

    parts = pl.pallas_call(
        functools.partial(value_kernel, part, held, scen_count),
        out_shape=[
            jax.ShapeDtypeStruct((SET_DEV, DATES * rows), jnp.bfloat16 if flip else jnp.float32)
            for flip in owner_flips
        ],
        in_specs=[VMEM] * 4,
        out_specs=[VMEM] * len(owner_flips),
        scratch_shapes=[pltpu.VMEM((2 * width, share_shape[1]), jnp.float32)],
        compiler_params=PARAMS,
        name="value",
    )(*shares, *pair_prices)
    sends = list(zip(parts[1:], owner_flips[1:]))
    sends = sends[1:] + sends[:1]
    parts = [parts[0]] + [from_partner(x, "fac", i) for x, i in sends]

    totals = pl.pallas_call(
        functools.partial(totals_kernel, rows),
        out_shape=jax.ShapeDtypeStruct((DATES, SET_DEV), jnp.float32),
        in_specs=[VMEM] * len(parts),
        out_specs=VMEM,
        compiler_params=PARAMS,
        name="totals",
    )(*parts)
    exposure = pl.pallas_call(
        functools.partial(expose_kernel, rows),
        out_shape=jax.ShapeDtypeStruct((DATES, SET_DEV, rows), jnp.float32),
        in_specs=[VMEM] * len(parts),
        out_specs=VMEM,
        compiler_params=PARAMS,
        name="expose",
    )(*parts)
    sums = [totals] + [None] * (scen_count - 1)
    for i in [*range(1, scen_count, 2), *range(2, scen_count, 2)]:
        sums[i] = from_partner(totals, "scen", i)
    while len(sums) > 1:
        sums = [sums[i] + sums[i + 1] for i in range(0, len(sums), 2)]
    return (exposure, sums[0] / (rows * scen_count))


def solution(mesh):
    placed = (
        P(None, "scen", None),
        P(None, "fac"),
        P("fac"),
        P(None, "scen", "fac"),
        P(None, "scen", "fac"),
        P("fac"),
        P("fac"),
        P("fac", None),
        P(),
        P("fac", None, None),
        P("fac"),
    )
    return jax.shard_map(
        body,
        mesh=mesh,
        in_specs=placed,
        out_specs=(P(None, "fac", "scen"), P(None, "fac")),
        check_vma=False,
    )
```

```python
import functools

import jax
import jax.numpy as jnp
from jax import lax
from jax.experimental import pallas as pl
from jax.experimental.pallas import tpu as pltpu
from jax.sharding import PartitionSpec as P

BLOCK = 128
SET_DEV = 64
DATES = 2
SIDE_FLIP = 1
PRICE_FLIP = 2
TAGS = 16
CHUNK = 64

VMEM = pl.BlockSpec(memory_space=pltpu.VMEM)
HBM = pl.BlockSpec(memory_space=pltpu.HBM)
SMEM = pl.BlockSpec(memory_space=pltpu.SMEM)
PARAMS = pltpu.CompilerParams(vmem_limit_bytes=16 * 1024 * 1024)
NT = (((1,), (1,)), ((), ()))


def f32_dot(a, b, dims):
    return lax.dot_general(a, b, dims, preferred_element_type=jnp.float32)


def pick_kernel(part, pick_ref):
    row = lax.broadcasted_iota(jnp.int32, pick_ref.shape, 0)
    column = lax.broadcasted_iota(jnp.int32, pick_ref.shape, 1)
    pick = column == lax.axis_index("scen") * part + row
    pick_ref[...] = pick.astype(jnp.float32).astype(jnp.bfloat16)


def pack_kernel(part, pick_ref, weights_ref, deps_ref, netting_ref, packet_ref):
    for k in range(2):
        share = f32_dot(pick_ref[...], weights_ref[:, k, :], NT)
        packet_ref[k * part : (k + 1) * part, :] = share[:part].astype(jnp.bfloat16)
    netting = netting_ref[...]
    tags = jnp.concatenate(
        [
            deps_ref[...],
            netting // SET_DEV,
            netting % SET_DEV,
            jnp.zeros((TAGS - 4, netting.shape[1]), jnp.int32),
        ],
        axis=0,
    )
    packet_ref[2 * part :, :] = tags.astype(jnp.float32).astype(jnp.bfloat16)


def price_kernel(shocks_ref, loadings_ref, vol_ref, counts_ref, noise_ref, mean_ref, dev_ref, out_ref):
    rows = shocks_ref.shape[1]
    vol = vol_ref[...]
    drift = 0.5 * vol * vol
    mean = mean_ref[...]
    dev = dev_ref[...]
    loadings = loadings_ref[...]
    for i in range(0, rows, CHUNK):
        at = slice(i, i + CHUNK)
        level = jnp.zeros((CHUNK, vol.shape[1]), jnp.float32)
        for date in range(DATES):
            diffuse = jnp.dot(shocks_ref[date, at, :], loadings, preferred_element_type=jnp.float32)
            counts = counts_ref[date, at, :].astype(jnp.float32)
            noise = noise_ref[date, at, :].astype(jnp.float32)
            level = level + vol * diffuse - drift + counts * mean + jnp.sqrt(counts) * dev * noise
            out_ref[date * rows + i : date * rows + i + CHUNK, :] = (jnp.exp(level) - 1.0).astype(
                jnp.bfloat16
            )


def combine_kernel(part, held, flips, *refs):
    slot_ref, packet_refs = refs[0], refs[1:-5]
    own_ref, narrow_ref, other_ref, chosen_ref, marks_ref = refs[-5:]
    fac = lax.axis_index("fac")
    names = []
    for flip in (0, PRICE_FLIP, SIDE_FLIP, SIDE_FLIP ^ PRICE_FLIP):
        for h in range(held):
            slot = (fac ^ flip) * held + h

            def find(b, name):
                return jnp.where(slot_ref[b] == slot, b, name)

            names.append(lax.fori_loop(0, slot_ref.shape[0], find, 0, unroll=True).astype(jnp.float32))
    trades = packet_refs[0].shape[1]
    place = lax.broadcasted_iota(jnp.int32, (SET_DEV, trades), 0).astype(jnp.float32)
    for source, packet_ref in enumerate(packet_refs):
        at = slice(source * trades, (source + 1) * trades)
        tags = packet_ref[2 * part :, :].astype(jnp.float32)
        weights = [packet_ref[k * part : (k + 1) * part, :].astype(jnp.float32) for k in range(2)]
        for b, name in enumerate(names):
            picked = jnp.where(tags[0:1] == name, weights[0], 0.0)
            picked = jnp.where(tags[1:2] == name, weights[1], picked)
            chosen_ref[b * part : (b + 1) * part, at] = picked.astype(jnp.bfloat16)
        for i, flip in enumerate(flips):
            owner = (fac ^ flip).astype(jnp.float32)
            local = jnp.where(tags[2:3] == owner, tags[3:4], -1.0)
            mark = jnp.where(local == place, 1.0, 0.0)
            marks_ref[i * SET_DEV : (i + 1) * SET_DEV, at] = mark.astype(jnp.bfloat16)
    sums = f32_dot(chosen_ref[...], marks_ref[...], NT)
    half = own_ref.shape[0]
    own_ref[...] = sums[:half]
    narrow_ref[...] = sums[:half].astype(jnp.bfloat16)
    other_ref[...] = sums[half:].astype(jnp.bfloat16)


def merge_kernel(*refs):
    part_refs, shares_ref = refs[:-1], refs[-1]
    rows, columns = part_refs[0].shape
    pair = 2 * SET_DEV
    for i in range(len(part_refs) // 2):
        own_ref, other_ref = part_refs[2 * i : 2 * i + 2]
        for at in range(0, columns, pair):
            own = own_ref[:, at : at + pair].astype(jnp.float32)
            other = pltpu.roll(other_ref[:, at : at + pair].astype(jnp.float32), SET_DEV, 1)
            shares_ref[i * rows : (i + 1) * rows, at : at + pair] = (own + other).astype(jnp.bfloat16)


def value_kernel(part, held, scen_count, *refs):
    cores_refs, price_refs = refs[:2], refs[2:4]
    out_refs, whole_ref = refs[4:-1], refs[-1]
    scen = lax.axis_index("scen")
    for i in range(scen_count):
        column = (scen ^ i) * part
        for b in range(2 * held):
            row = (i // 2 * 2 * held + b) * part
            at = pl.ds(pl.multiple_of(b * BLOCK + column, part), part)
            whole_ref[at, :] = cores_refs[i % 2][row : row + part, :].astype(jnp.float32)
    width = held * BLOCK
    total = None
    for i, price_ref in enumerate(price_refs):
        whole = whole_ref[i * width : (i + 1) * width, :].T.astype(jnp.bfloat16)
        term = f32_dot(whole, price_ref[...], NT)
        total = term if total is None else total + term
    for p, out_ref in enumerate(out_refs):
        out_ref[...] = total[p * SET_DEV : (p + 1) * SET_DEV].astype(out_ref.dtype)


def exposure_of(part_refs, date, rows):
    at = slice(date * rows, (date + 1) * rows)
    nets = part_refs[0][:, at]
    for ref in part_refs[1:]:
        nets = nets + ref[:, at].astype(jnp.float32)
    return jnp.maximum(nets, 0.0)


def totals_kernel(rows, *refs):
    for date in range(DATES):
        refs[-1][date] = jnp.sum(exposure_of(refs[:-1], date, rows), axis=1)


def expose_kernel(rows, *refs):
    for date in range(DATES):
        refs[-1][date] = exposure_of(refs[:-1], date, rows)


def from_partner(x, axis, flip):
    count = lax.axis_size(axis)
    return lax.ppermute(x, axis, [(i, i ^ flip) for i in range(count)])


def from_both(x, scen_flip, fac_flip):
    count = lax.axis_size("fac")
    pairs = [
        (i * count + j, (i ^ scen_flip) * count + (j ^ fac_flip))
        for i in range(lax.axis_size("scen"))
        for j in range(count)
    ]
    return lax.ppermute(x, ("scen", "fac"), pairs)


def body(
    shocks,
    loadings,
    vol,
    jump_counts,
    jump_noise,
    jump_mean,
    jump_vol,
    dependencies,
    block_slot,
    trade_weights,
    netting,
):
    fac_count = lax.axis_size("fac")
    scen_count = lax.axis_size("scen")
    rows = shocks.shape[1]
    width = loadings.shape[1]
    held = width // BLOCK
    trades = trade_weights.shape[0]
    part = BLOCK // scen_count
    column_flips = [i for i in range(fac_count) if not i & SIDE_FLIP]
    owner_flips = [i for i in range(fac_count) if (i // PRICE_FLIP) % 4 in (0, 3)]

    pick = pl.pallas_call(
        functools.partial(pick_kernel, part),
        out_shape=jax.ShapeDtypeStruct((max(part, 16), BLOCK), jnp.bfloat16),
        out_specs=VMEM,
        compiler_params=PARAMS,
        cost_estimate=pl.CostEstimate(flops=10**10, bytes_accessed=0, transcendentals=0),
        name="pick",
    )()
    packet = pl.pallas_call(
        functools.partial(pack_kernel, part),
        out_shape=jax.ShapeDtypeStruct((2 * part + TAGS, trades), jnp.bfloat16),
        in_specs=[VMEM] * 4,
        out_specs=VMEM,
        compiler_params=PARAMS,
        name="pack",
    )(pick, trade_weights, dependencies.T, netting[None])
    packets = [packet] + [from_partner(packet, "fac", i) for i in column_flips[1:]]

    packet, shocks = lax.optimization_barrier((packet, shocks))
    prices = pl.pallas_call(
        price_kernel,
        out_shape=jax.ShapeDtypeStruct((DATES * rows, width), jnp.bfloat16),
        in_specs=[VMEM] * 7,
        out_specs=VMEM,
        compiler_params=PARAMS,
        name="price",
    )(shocks, loadings, vol[None], jump_counts, jump_noise, jump_mean[None], jump_vol[None])
    share_shape = (2 * held * part, len(owner_flips) * SET_DEV)
    column_trades = len(column_flips) * trades
    own, narrow, other = pl.pallas_call(
        functools.partial(combine_kernel, part, held, owner_flips),
        out_shape=[
            jax.ShapeDtypeStruct(share_shape, jnp.float32),
            jax.ShapeDtypeStruct(share_shape, jnp.bfloat16),
            jax.ShapeDtypeStruct(share_shape, jnp.bfloat16),
        ],
        in_specs=[SMEM] + [VMEM] * len(packets),
        out_specs=[VMEM] * 3,
        scratch_shapes=[
            pltpu.VMEM((2 * share_shape[0], column_trades), jnp.bfloat16),
            pltpu.VMEM((share_shape[1], column_trades), jnp.bfloat16),
        ],
        compiler_params=PARAMS,
        cost_estimate=pl.CostEstimate(flops=10**9, bytes_accessed=0, transcendentals=0),
        name="combine",
    )(block_slot, *packets)
    pair_prices = [prices, from_partner(prices, "fac", PRICE_FLIP)]
    parts = []
    for i in range(0, scen_count, 2):
        parts.append(from_partner(narrow, "scen", i) if i else own)
        parts.append(from_both(other, i, SIDE_FLIP))
    shares = pl.pallas_call(
        merge_kernel,
        out_shape=jax.ShapeDtypeStruct((len(parts) // 2 * share_shape[0], share_shape[1]), jnp.bfloat16),
        in_specs=[VMEM] * len(parts),
        out_specs=VMEM,
        compiler_params=PARAMS,
        name="merge",
    )(*parts)
    shares = [shares, from_partner(shares, "scen", 1)]

    parts = pl.pallas_call(
        functools.partial(value_kernel, part, held, scen_count),
        out_shape=[
            jax.ShapeDtypeStruct((SET_DEV, DATES * rows), jnp.bfloat16 if flip else jnp.float32)
            for flip in owner_flips
        ],
        in_specs=[VMEM] * 4,
        out_specs=[VMEM] * len(owner_flips),
        scratch_shapes=[pltpu.VMEM((2 * width, share_shape[1]), jnp.float32)],
        compiler_params=PARAMS,
        name="value",
    )(*shares, *pair_prices)
    sends = list(zip(parts[1:], owner_flips[1:]))
    sends = sends[1:] + sends[:1]
    parts = [parts[0]] + [from_partner(x, "fac", i) for x, i in sends]

    totals = pl.pallas_call(
        functools.partial(totals_kernel, rows),
        out_shape=jax.ShapeDtypeStruct((DATES, SET_DEV), jnp.float32),
        in_specs=[VMEM] * len(parts),
        out_specs=VMEM,
        compiler_params=PARAMS,
        name="totals",
    )(*parts)
    exposure = pl.pallas_call(
        functools.partial(expose_kernel, rows),
        out_shape=jax.ShapeDtypeStruct((DATES, SET_DEV, rows), jnp.float32),
        in_specs=[VMEM] * len(parts),
        out_specs=VMEM,
        compiler_params=PARAMS,
        name="expose",
    )(*parts)
    sums = [totals] + [None] * (scen_count - 1)
    for i in [*range(1, scen_count, 2), *range(2, scen_count, 2)]:
        sums[i] = from_partner(totals, "scen", i)
    while len(sums) > 1:
        sums = [sums[i] + sums[i + 1] for i in range(0, len(sums), 2)]
    return (exposure, sums[0] / (rows * scen_count))


def solution(mesh):
    placed = (
        P(None, "scen", None),
        P(None, "fac"),
        P("fac"),
        P(None, "scen", "fac"),
        P(None, "scen", "fac"),
        P("fac"),
        P("fac"),
        P("fac", None),
        P(),
        P("fac", None, None),
        P("fac"),
    )
    return jax.shard_map(
        body,
        mesh=mesh,
        in_specs=placed,
        out_specs=(P(None, "fac", "scen"), P(None, "fac")),
        check_vma=False,
    )
```

```python
import functools

import jax
import jax.numpy as jnp
from jax import lax
from jax.experimental import pallas as pl
from jax.experimental.pallas import tpu as pltpu
from jax.sharding import PartitionSpec as P

BLOCK = 128
SET_DEV = 64
DATES = 2
SIDE_FLIP = 1
PRICE_FLIP = 2
TAGS = 16
CHUNK = 64

VMEM = pl.BlockSpec(memory_space=pltpu.VMEM)
HBM = pl.BlockSpec(memory_space=pltpu.HBM)
SMEM = pl.BlockSpec(memory_space=pltpu.SMEM)
PARAMS = pltpu.CompilerParams(vmem_limit_bytes=16 * 1024 * 1024)
NT = (((1,), (1,)), ((), ()))


def f32_dot(a, b, dims):
    return lax.dot_general(a, b, dims, preferred_element_type=jnp.float32)


def pick_kernel(part, pick_ref):
    row = lax.broadcasted_iota(jnp.int32, pick_ref.shape, 0)
    column = lax.broadcasted_iota(jnp.int32, pick_ref.shape, 1)
    pick = column == lax.axis_index("scen") * part + row
    pick_ref[...] = pick.astype(jnp.float32).astype(jnp.bfloat16)


def pack_kernel(part, pick_ref, weights_ref, deps_ref, netting_ref, packet_ref):
    for k in range(2):
        share = f32_dot(pick_ref[...], weights_ref[:, k, :], NT)
        packet_ref[k * part : (k + 1) * part, :] = share[:part].astype(jnp.bfloat16)
    netting = netting_ref[...]
    tags = jnp.concatenate(
        [
            deps_ref[...],
            netting // SET_DEV,
            netting % SET_DEV,
            jnp.zeros((TAGS - 4, netting.shape[1]), jnp.int32),
        ],
        axis=0,
    )
    packet_ref[2 * part :, :] = tags.astype(jnp.float32).astype(jnp.bfloat16)


def price_kernel(shocks_ref, loadings_ref, vol_ref, counts_ref, noise_ref, mean_ref, dev_ref, out_ref):
    rows = shocks_ref.shape[1]
    vol = vol_ref[...]
    drift = 0.5 * vol * vol
    mean = mean_ref[...]
    dev = dev_ref[...]
    loadings = loadings_ref[...]
    for i in range(0, rows, CHUNK):
        at = slice(i, i + CHUNK)
        level = jnp.zeros((CHUNK, vol.shape[1]), jnp.float32)
        for date in range(DATES):
            diffuse = jnp.dot(shocks_ref[date, at, :], loadings, preferred_element_type=jnp.float32)
            counts = counts_ref[date, at, :].astype(jnp.float32)
            noise = noise_ref[date, at, :].astype(jnp.float32)
            level = level + vol * diffuse - drift + counts * mean + jnp.sqrt(counts) * dev * noise
            out_ref[date * rows + i : date * rows + i + CHUNK, :] = (jnp.exp(level) - 1.0).astype(
                jnp.bfloat16
            )


def combine_kernel(part, held, flips, *refs):
    slot_ref, packet_refs = refs[0], refs[1:-5]
    own_ref, narrow_ref, other_ref, chosen_ref, marks_ref = refs[-5:]
    fac = lax.axis_index("fac")
    names = []
    for flip in (0, PRICE_FLIP, SIDE_FLIP, SIDE_FLIP ^ PRICE_FLIP):
        for h in range(held):
            slot = (fac ^ flip) * held + h

            def find(b, name):
                return jnp.where(slot_ref[b] == slot, b, name)

            names.append(lax.fori_loop(0, slot_ref.shape[0], find, 0, unroll=True).astype(jnp.float32))
    trades = packet_refs[0].shape[1]
    place = lax.broadcasted_iota(jnp.int32, (SET_DEV, trades), 0).astype(jnp.float32)
    for source, packet_ref in enumerate(packet_refs):
        at = slice(source * trades, (source + 1) * trades)
        tags = packet_ref[2 * part :, :].astype(jnp.float32)
        weights = [packet_ref[k * part : (k + 1) * part, :].astype(jnp.float32) for k in range(2)]
        for b, name in enumerate(names):
            picked = jnp.where(tags[0:1] == name, weights[0], 0.0)
            picked = jnp.where(tags[1:2] == name, weights[1], picked)
            chosen_ref[b * part : (b + 1) * part, at] = picked.astype(jnp.bfloat16)
        for i, flip in enumerate(flips):
            owner = (fac ^ flip).astype(jnp.float32)
            local = jnp.where(tags[2:3] == owner, tags[3:4], -1.0)
            mark = jnp.where(local == place, 1.0, 0.0)
            marks_ref[i * SET_DEV : (i + 1) * SET_DEV, at] = mark.astype(jnp.bfloat16)
    sums = f32_dot(chosen_ref[...], marks_ref[...], NT)
    half = own_ref.shape[0]
    own_ref[...] = sums[:half]
    narrow_ref[...] = sums[:half].astype(jnp.bfloat16)
    other_ref[...] = sums[half:].astype(jnp.bfloat16)


def merge_kernel(*refs):
    part_refs, shares_ref = refs[:-1], refs[-1]
    rows, columns = part_refs[0].shape
    pair = 2 * SET_DEV
    for i in range(len(part_refs) // 2):
        own_ref, other_ref = part_refs[2 * i : 2 * i + 2]
        for at in range(0, columns, pair):
            own = own_ref[:, at : at + pair].astype(jnp.float32)
            other = pltpu.roll(other_ref[:, at : at + pair].astype(jnp.float32), SET_DEV, 1)
            shares_ref[i * rows : (i + 1) * rows, at : at + pair] = (own + other).astype(jnp.bfloat16)


def value_kernel(part, held, scen_count, *refs):
    cores_refs, price_refs = refs[:2], refs[2:4]
    out_refs, whole_ref = refs[4:-1], refs[-1]
    scen = lax.axis_index("scen")
    for i in range(scen_count):
        column = (scen ^ i) * part
        for b in range(2 * held):
            row = (i // 2 * 2 * held + b) * part
            at = pl.ds(pl.multiple_of(b * BLOCK + column, part), part)
            whole_ref[at, :] = cores_refs[i % 2][row : row + part, :].astype(jnp.float32)
    width = held * BLOCK
    total = None
    for i, price_ref in enumerate(price_refs):
        whole = whole_ref[i * width : (i + 1) * width, :].T.astype(jnp.bfloat16)
        term = f32_dot(whole, price_ref[...], NT)
        total = term if total is None else total + term
    for p, out_ref in enumerate(out_refs):
        out_ref[...] = total[p * SET_DEV : (p + 1) * SET_DEV].astype(out_ref.dtype)


def exposure_of(part_refs, date, rows):
    at = slice(date * rows, (date + 1) * rows)
    nets = part_refs[0][:, at]
    for ref in part_refs[1:]:
        nets = nets + ref[:, at].astype(jnp.float32)
    return jnp.maximum(nets, 0.0)


def totals_kernel(rows, *refs):
    for date in range(DATES):
        refs[-1][date] = jnp.sum(exposure_of(refs[:-1], date, rows), axis=1)


def expose_kernel(rows, *refs):
    for date in range(DATES):
        refs[-1][date] = exposure_of(refs[:-1], date, rows)


def from_partner(x, axis, flip):
    count = lax.axis_size(axis)
    return lax.ppermute(x, axis, [(i, i ^ flip) for i in range(count)])


def from_both(x, scen_flip, fac_flip):
    count = lax.axis_size("fac")
    pairs = [
        (i * count + j, (i ^ scen_flip) * count + (j ^ fac_flip))
        for i in range(lax.axis_size("scen"))
        for j in range(count)
    ]
    return lax.ppermute(x, ("scen", "fac"), pairs)


def body(
    shocks,
    loadings,
    vol,
    jump_counts,
    jump_noise,
    jump_mean,
    jump_vol,
    dependencies,
    block_slot,
    trade_weights,
    netting,
):
    fac_count = lax.axis_size("fac")
    scen_count = lax.axis_size("scen")
    rows = shocks.shape[1]
    width = loadings.shape[1]
    held = width // BLOCK
    trades = trade_weights.shape[0]
    part = BLOCK // scen_count
    column_flips = [i for i in range(fac_count) if not i & SIDE_FLIP]
    owner_flips = [i for i in range(fac_count) if not i & PRICE_FLIP]

    pick = pl.pallas_call(
        functools.partial(pick_kernel, part),
        out_shape=jax.ShapeDtypeStruct((max(part, 16), BLOCK), jnp.bfloat16),
        out_specs=VMEM,
        compiler_params=PARAMS,
        cost_estimate=pl.CostEstimate(flops=10**10, bytes_accessed=0, transcendentals=0),
        name="pick",
    )()
    packet = pl.pallas_call(
        functools.partial(pack_kernel, part),
        out_shape=jax.ShapeDtypeStruct((2 * part + TAGS, trades), jnp.bfloat16),
        in_specs=[VMEM] * 4,
        out_specs=VMEM,
        compiler_params=PARAMS,
        name="pack",
    )(pick, trade_weights, dependencies.T, netting[None])
    order = column_flips[1:2] + column_flips[:1:-1]
    packets = [packet] + [from_partner(packet, "fac", i) for i in order]

    packet, shocks = lax.optimization_barrier((packet, shocks))
    prices = pl.pallas_call(
        price_kernel,
        out_shape=jax.ShapeDtypeStruct((DATES * rows, width), jnp.bfloat16),
        in_specs=[VMEM] * 7,
        out_specs=VMEM,
        compiler_params=PARAMS,
        name="price",
    )(shocks, loadings, vol[None], jump_counts, jump_noise, jump_mean[None], jump_vol[None])
    share_shape = (2 * held * part, len(owner_flips) * SET_DEV)
    column_trades = len(column_flips) * trades
    own, narrow, other = pl.pallas_call(
        functools.partial(combine_kernel, part, held, owner_flips),
        out_shape=[
            jax.ShapeDtypeStruct(share_shape, jnp.float32),
            jax.ShapeDtypeStruct(share_shape, jnp.bfloat16),
            jax.ShapeDtypeStruct(share_shape, jnp.bfloat16),
        ],
        in_specs=[SMEM] + [VMEM] * len(packets),
        out_specs=[VMEM] * 3,
        scratch_shapes=[
            pltpu.VMEM((2 * share_shape[0], column_trades), jnp.bfloat16),
            pltpu.VMEM((share_shape[1], column_trades), jnp.bfloat16),
        ],
        compiler_params=PARAMS,
        cost_estimate=pl.CostEstimate(flops=10**9, bytes_accessed=0, transcendentals=0),
        name="combine",
    )(block_slot, *packets)
    pair_prices = [prices, from_partner(prices, "fac", PRICE_FLIP)]
    parts = []
    for i in range(0, scen_count, 2):
        parts.append(from_partner(narrow, "scen", i) if i else own)
        parts.append(from_both(other, i, SIDE_FLIP))
    shares = pl.pallas_call(
        merge_kernel,
        out_shape=jax.ShapeDtypeStruct((len(parts) // 2 * share_shape[0], share_shape[1]), jnp.bfloat16),
        in_specs=[VMEM] * len(parts),
        out_specs=VMEM,
        compiler_params=PARAMS,
        name="merge",
    )(*parts)
    shares = [shares, from_partner(shares, "scen", 1)]

    parts = pl.pallas_call(
        functools.partial(value_kernel, part, held, scen_count),
        out_shape=[
            jax.ShapeDtypeStruct((SET_DEV, DATES * rows), jnp.bfloat16 if flip else jnp.float32)
            for flip in owner_flips
        ],
        in_specs=[VMEM] * 4,
        out_specs=[VMEM] * len(owner_flips),
        scratch_shapes=[pltpu.VMEM((2 * width, share_shape[1]), jnp.float32)],
        compiler_params=PARAMS,
        name="value",
    )(*shares, *pair_prices)
    sends = list(zip(parts[1:], owner_flips[1:]))
    sends = sends[1:] + sends[:1]
    parts = [parts[0]] + [from_partner(x, "fac", i) for x, i in sends]

    totals = pl.pallas_call(
        functools.partial(totals_kernel, rows),
        out_shape=jax.ShapeDtypeStruct((DATES, SET_DEV), jnp.float32),
        in_specs=[VMEM] * len(parts),
        out_specs=VMEM,
        compiler_params=PARAMS,
        name="totals",
    )(*parts)
    exposure = pl.pallas_call(
        functools.partial(expose_kernel, rows),
        out_shape=jax.ShapeDtypeStruct((DATES, SET_DEV, rows), jnp.float32),
        in_specs=[VMEM] * len(parts),
        out_specs=VMEM,
        compiler_params=PARAMS,
        name="expose",
    )(*parts)
    sums = [totals] + [None] * (scen_count - 1)
    for i in [*range(1, scen_count, 2), *range(2, scen_count, 2)]:
        sums[i] = from_partner(totals, "scen", i)
    while len(sums) > 1:
        sums = [sums[i] + sums[i + 1] for i in range(0, len(sums), 2)]
    return (exposure, sums[0] / (rows * scen_count))


def solution(mesh):
    placed = (
        P(None, "scen", None),
        P(None, "fac"),
        P("fac"),
        P(None, "scen", "fac"),
        P(None, "scen", "fac"),
        P("fac"),
        P("fac"),
        P("fac", None),
        P(),
        P("fac", None, None),
        P("fac"),
    )
    return jax.shard_map(
        body,
        mesh=mesh,
        in_specs=placed,
        out_specs=(P(None, "fac", "scen"), P(None, "fac")),
        check_vma=False,
    )
```

```python
import functools

import jax
import jax.numpy as jnp
from jax import lax
from jax.experimental import pallas as pl
from jax.experimental.pallas import tpu as pltpu
from jax.sharding import PartitionSpec as P

BLOCK = 128
SET_DEV = 64
DATES = 2
SIDE_FLIP = 1
PRICE_FLIP = 6
HALF_FLIP = 4
TAGS = 16
CHUNK = 64

VMEM = pl.BlockSpec(memory_space=pltpu.VMEM)
HBM = pl.BlockSpec(memory_space=pltpu.HBM)
SMEM = pl.BlockSpec(memory_space=pltpu.SMEM)
PARAMS = pltpu.CompilerParams(vmem_limit_bytes=16 * 1024 * 1024)
NT = (((1,), (1,)), ((), ()))


def f32_dot(a, b, dims):
    return lax.dot_general(a, b, dims, preferred_element_type=jnp.float32)


def pick_kernel(part, pick_ref):
    row = lax.broadcasted_iota(jnp.int32, pick_ref.shape, 0)
    column = lax.broadcasted_iota(jnp.int32, pick_ref.shape, 1)
    pick = column == lax.axis_index("scen") * part + row
    pick_ref[...] = pick.astype(jnp.float32).astype(jnp.bfloat16)


def pack_kernel(part, pick_ref, weights_ref, deps_ref, netting_ref, packet_ref):
    for k in range(2):
        share = f32_dot(pick_ref[...], weights_ref[:, k, :], NT)
        packet_ref[k * part : (k + 1) * part, :] = share[:part].astype(jnp.bfloat16)
    netting = netting_ref[...]
    tags = jnp.concatenate(
        [
            deps_ref[...],
            netting // SET_DEV,
            netting % SET_DEV,
            jnp.zeros((TAGS - 4, netting.shape[1]), jnp.int32),
        ],
        axis=0,
    )
    packet_ref[2 * part :, :] = tags.astype(jnp.float32).astype(jnp.bfloat16)


def price_kernel(shocks_ref, loadings_ref, vol_ref, counts_ref, noise_ref, mean_ref, dev_ref, out_ref):
    rows = shocks_ref.shape[1]
    vol = vol_ref[...]
    drift = 0.5 * vol * vol
    mean = mean_ref[...]
    dev = dev_ref[...]
    loadings = loadings_ref[...]
    for i in range(0, rows, CHUNK):
        at = slice(i, i + CHUNK)
        level = jnp.zeros((CHUNK, vol.shape[1]), jnp.float32)
        for date in range(DATES):
            diffuse = jnp.dot(shocks_ref[date, at, :], loadings, preferred_element_type=jnp.float32)
            counts = counts_ref[date, at, :].astype(jnp.float32)
            noise = noise_ref[date, at, :].astype(jnp.float32)
            level = level + vol * diffuse - drift + counts * mean + jnp.sqrt(counts) * dev * noise
            out_ref[date * rows + i : date * rows + i + CHUNK, :] = (jnp.exp(level) - 1.0).astype(
                jnp.bfloat16
            )


def combine_kernel(part, held, flips, *refs):
    slot_ref, packet_refs = refs[0], refs[1:-5]
    own_ref, narrow_ref, other_ref, chosen_ref, marks_ref = refs[-5:]
    fac = lax.axis_index("fac")
    names = []
    for flip in (0, PRICE_FLIP, SIDE_FLIP, SIDE_FLIP ^ PRICE_FLIP):
        for h in range(held):
            slot = (fac ^ flip) * held + h

            def find(b, name):
                return jnp.where(slot_ref[b] == slot, b, name)

            names.append(lax.fori_loop(0, slot_ref.shape[0], find, 0, unroll=True).astype(jnp.float32))
    trades = packet_refs[0].shape[1]
    place = lax.broadcasted_iota(jnp.int32, (SET_DEV, trades), 0).astype(jnp.float32)
    for source, packet_ref in enumerate(packet_refs):
        at = slice(source * trades, (source + 1) * trades)
        tags = packet_ref[2 * part :, :].astype(jnp.float32)
        weights = [packet_ref[k * part : (k + 1) * part, :].astype(jnp.float32) for k in range(2)]
        for b, name in enumerate(names):
            picked = jnp.where(tags[0:1] == name, weights[0], 0.0)
            picked = jnp.where(tags[1:2] == name, weights[1], picked)
            chosen_ref[b * part : (b + 1) * part, at] = picked.astype(jnp.bfloat16)
        for i, flip in enumerate(flips):
            owner = (fac ^ flip).astype(jnp.float32)
            local = jnp.where(tags[2:3] == owner, tags[3:4], -1.0)
            mark = jnp.where(local == place, 1.0, 0.0)
            marks_ref[i * SET_DEV : (i + 1) * SET_DEV, at] = mark.astype(jnp.bfloat16)
    sums = f32_dot(chosen_ref[...], marks_ref[...], NT)
    half = own_ref.shape[0]
    own_ref[...] = sums[:half]
    narrow_ref[...] = sums[:half].astype(jnp.bfloat16)
    other_ref[...] = sums[half:].astype(jnp.bfloat16)


def merge_kernel(*refs):
    part_refs, shares_ref = refs[:-1], refs[-1]
    rows, columns = part_refs[0].shape
    pair = 2 * SET_DEV
    for i in range(len(part_refs) // 2):
        own_ref, other_ref = part_refs[2 * i : 2 * i + 2]
        for at in range(0, columns, pair):
            own = own_ref[:, at : at + pair].astype(jnp.float32)
            other = pltpu.roll(other_ref[:, at : at + pair].astype(jnp.float32), SET_DEV, 1)
            shares_ref[i * rows : (i + 1) * rows, at : at + pair] = (own + other).astype(jnp.bfloat16)


def value_kernel(part, held, scen_count, *refs):
    cores_refs, price_refs = refs[:2], refs[2:4]
    out_refs, whole_ref = refs[4:-1], refs[-1]
    scen = lax.axis_index("scen")
    for i in range(scen_count):
        column = (scen ^ i) * part
        for b in range(2 * held):
            row = (i // 2 * 2 * held + b) * part
            at = pl.ds(pl.multiple_of(b * BLOCK + column, part), part)
            whole_ref[at, :] = cores_refs[i % 2][row : row + part, :].astype(jnp.float32)
    width = held * BLOCK
    total = None
    for i, price_ref in enumerate(price_refs):
        whole = whole_ref[i * width : (i + 1) * width, :].T.astype(jnp.bfloat16)
        term = f32_dot(whole, price_ref[...], NT)
        total = term if total is None else total + term
    for p, out_ref in enumerate(out_refs):
        out_ref[...] = total[p * SET_DEV : (p + 1) * SET_DEV].astype(out_ref.dtype)


def exposure_of(part_refs, date, rows):
    at = slice(date * rows, (date + 1) * rows)
    nets = part_refs[0][:, at]
    for ref in part_refs[1:]:
        nets = nets + ref[:, at].astype(jnp.float32)
    return jnp.maximum(nets, 0.0)


def totals_kernel(rows, *refs):
    for date in range(DATES):
        refs[-1][date] = jnp.sum(exposure_of(refs[:-1], date, rows), axis=1)


def expose_kernel(rows, *refs):
    for date in range(DATES):
        refs[-1][date] = exposure_of(refs[:-1], date, rows)


def from_partner(x, axis, flip):
    count = lax.axis_size(axis)
    return lax.ppermute(x, axis, [(i, i ^ flip) for i in range(count)])


def from_both(x, scen_flip, fac_flip):
    count = lax.axis_size("fac")
    pairs = [
        (i * count + j, (i ^ scen_flip) * count + (j ^ fac_flip))
        for i in range(lax.axis_size("scen"))
        for j in range(count)
    ]
    return lax.ppermute(x, ("scen", "fac"), pairs)


def body(
    shocks,
    loadings,
    vol,
    jump_counts,
    jump_noise,
    jump_mean,
    jump_vol,
    dependencies,
    block_slot,
    trade_weights,
    netting,
):
    fac_count = lax.axis_size("fac")
    scen_count = lax.axis_size("scen")
    rows = shocks.shape[1]
    width = loadings.shape[1]
    held = width // BLOCK
    trades = trade_weights.shape[0]
    part = BLOCK // scen_count
    column_flips = [i for i in range(fac_count) if not i & SIDE_FLIP]
    owner_flips = [i for i in range(fac_count) if not i & HALF_FLIP]

    pick = pl.pallas_call(
        functools.partial(pick_kernel, part),
        out_shape=jax.ShapeDtypeStruct((max(part, 16), BLOCK), jnp.bfloat16),
        out_specs=VMEM,
        compiler_params=PARAMS,
        cost_estimate=pl.CostEstimate(flops=10**10, bytes_accessed=0, transcendentals=0),
        name="pick",
    )()
    packet = pl.pallas_call(
        functools.partial(pack_kernel, part),
        out_shape=jax.ShapeDtypeStruct((2 * part + TAGS, trades), jnp.bfloat16),
        in_specs=[VMEM] * 4,
        out_specs=VMEM,
        compiler_params=PARAMS,
        name="pack",
    )(pick, trade_weights, dependencies.T, netting[None])
    packets = [packet] + [from_partner(packet, "fac", i) for i in column_flips[1:]]

    packet, shocks = lax.optimization_barrier((packet, shocks))
    prices = pl.pallas_call(
        price_kernel,
        out_shape=jax.ShapeDtypeStruct((DATES * rows, width), jnp.bfloat16),
        in_specs=[VMEM] * 7,
        out_specs=VMEM,
        compiler_params=PARAMS,
        name="price",
    )(shocks, loadings, vol[None], jump_counts, jump_noise, jump_mean[None], jump_vol[None])
    share_shape = (2 * held * part, len(owner_flips) * SET_DEV)
    column_trades = len(column_flips) * trades
    own, narrow, other = pl.pallas_call(
        functools.partial(combine_kernel, part, held, owner_flips),
        out_shape=[
            jax.ShapeDtypeStruct(share_shape, jnp.float32),
            jax.ShapeDtypeStruct(share_shape, jnp.bfloat16),
            jax.ShapeDtypeStruct(share_shape, jnp.bfloat16),
        ],
        in_specs=[SMEM] + [VMEM] * len(packets),
        out_specs=[VMEM] * 3,
        scratch_shapes=[
            pltpu.VMEM((2 * share_shape[0], column_trades), jnp.bfloat16),
            pltpu.VMEM((share_shape[1], column_trades), jnp.bfloat16),
        ],
        compiler_params=PARAMS,
        cost_estimate=pl.CostEstimate(flops=10**9, bytes_accessed=0, transcendentals=0),
        name="combine",
    )(block_slot, *packets)
    pair_prices = [prices, from_partner(prices, "fac", PRICE_FLIP)]
    parts = []
    for i in range(0, scen_count, 2):
        parts.append(from_partner(narrow, "scen", i) if i else own)
        parts.append(from_both(other, i, SIDE_FLIP))
    shares = pl.pallas_call(
        merge_kernel,
        out_shape=jax.ShapeDtypeStruct((len(parts) // 2 * share_shape[0], share_shape[1]), jnp.bfloat16),
        in_specs=[VMEM] * len(parts),
        out_specs=VMEM,
        compiler_params=PARAMS,
        name="merge",
    )(*parts)
    shares = [shares, from_partner(shares, "scen", 1)]

    parts = pl.pallas_call(
        functools.partial(value_kernel, part, held, scen_count),
        out_shape=[
            jax.ShapeDtypeStruct((SET_DEV, DATES * rows), jnp.bfloat16 if flip else jnp.float32)
            for flip in owner_flips
        ],
        in_specs=[VMEM] * 4,
        out_specs=[VMEM] * len(owner_flips),
        scratch_shapes=[pltpu.VMEM((2 * width, share_shape[1]), jnp.float32)],
        compiler_params=PARAMS,
        name="value",
    )(*shares, *pair_prices)
    sends = list(zip(parts[1:], owner_flips[1:]))
    sends = sends[1:] + sends[:1]
    parts = [parts[0]] + [from_partner(x, "fac", i) for x, i in sends]

    totals = pl.pallas_call(
        functools.partial(totals_kernel, rows),
        out_shape=jax.ShapeDtypeStruct((DATES, SET_DEV), jnp.float32),
        in_specs=[VMEM] * len(parts),
        out_specs=VMEM,
        compiler_params=PARAMS,
        name="totals",
    )(*parts)
    exposure = pl.pallas_call(
        functools.partial(expose_kernel, rows),
        out_shape=jax.ShapeDtypeStruct((DATES, SET_DEV, rows), jnp.float32),
        in_specs=[VMEM] * len(parts),
        out_specs=VMEM,
        compiler_params=PARAMS,
        name="expose",
    )(*parts)
    sums = [totals] + [None] * (scen_count - 1)
    for i in [*range(1, scen_count, 2), *range(2, scen_count, 2)]:
        sums[i] = from_partner(totals, "scen", i)
    while len(sums) > 1:
        sums = [sums[i] + sums[i + 1] for i in range(0, len(sums), 2)]
    return (exposure, sums[0] / (rows * scen_count))


def solution(mesh):
    placed = (
        P(None, "scen", None),
        P(None, "fac"),
        P("fac"),
        P(None, "scen", "fac"),
        P(None, "scen", "fac"),
        P("fac"),
        P("fac"),
        P("fac", None),
        P(),
        P("fac", None, None),
        P("fac"),
    )
    return jax.shard_map(
        body,
        mesh=mesh,
        in_specs=placed,
        out_specs=(P(None, "fac", "scen"), P(None, "fac")),
        check_vma=False,
    )
```

```python
import functools

import jax
import jax.numpy as jnp
from jax import lax
from jax.experimental import pallas as pl
from jax.experimental.pallas import tpu as pltpu
from jax.sharding import PartitionSpec as P

BLOCK = 128
SET_DEV = 64
DATES = 2
SIDE_FLIP = 1
PRICE_FLIP = 4
TAGS = 16
CHUNK = 64

VMEM = pl.BlockSpec(memory_space=pltpu.VMEM)
HBM = pl.BlockSpec(memory_space=pltpu.HBM)
SMEM = pl.BlockSpec(memory_space=pltpu.SMEM)
PARAMS = pltpu.CompilerParams(vmem_limit_bytes=16 * 1024 * 1024)
NT = (((1,), (1,)), ((), ()))


def f32_dot(a, b, dims):
    return lax.dot_general(a, b, dims, preferred_element_type=jnp.float32)


def pick_kernel(part, pick_ref):
    row = lax.broadcasted_iota(jnp.int32, pick_ref.shape, 0)
    column = lax.broadcasted_iota(jnp.int32, pick_ref.shape, 1)
    pick = column == lax.axis_index("scen") * part + row
    pick_ref[...] = pick.astype(jnp.float32).astype(jnp.bfloat16)


def pack_kernel(part, pick_ref, weights_ref, deps_ref, netting_ref, packet_ref):
    for k in range(2):
        share = f32_dot(pick_ref[...], weights_ref[:, k, :], NT)
        packet_ref[k * part : (k + 1) * part, :] = share[:part].astype(jnp.bfloat16)
    netting = netting_ref[...]
    tags = jnp.concatenate(
        [
            deps_ref[...],
            netting // SET_DEV,
            netting % SET_DEV,
            jnp.zeros((TAGS - 4, netting.shape[1]), jnp.int32),
        ],
        axis=0,
    )
    packet_ref[2 * part :, :] = tags.astype(jnp.float32).astype(jnp.bfloat16)


def price_kernel(shocks_ref, loadings_ref, vol_ref, counts_ref, noise_ref, mean_ref, dev_ref, out_ref):
    rows = shocks_ref.shape[1]
    vol = vol_ref[...]
    drift = 0.5 * vol * vol
    mean = mean_ref[...]
    dev = dev_ref[...]
    loadings = loadings_ref[...]
    for i in range(0, rows, CHUNK):
        at = slice(i, i + CHUNK)
        level = jnp.zeros((CHUNK, vol.shape[1]), jnp.float32)
        for date in range(DATES):
            diffuse = jnp.dot(shocks_ref[date, at, :], loadings, preferred_element_type=jnp.float32)
            counts = counts_ref[date, at, :].astype(jnp.float32)
            noise = noise_ref[date, at, :].astype(jnp.float32)
            level = level + vol * diffuse - drift + counts * mean + jnp.sqrt(counts) * dev * noise
            out_ref[date * rows + i : date * rows + i + CHUNK, :] = (jnp.exp(level) - 1.0).astype(
                jnp.bfloat16
            )


def combine_kernel(part, held, flips, *refs):
    slot_ref, packet_refs = refs[0], refs[1:-5]
    own_ref, narrow_ref, other_ref, chosen_ref, marks_ref = refs[-5:]
    fac = lax.axis_index("fac")
    names = []
    for flip in (0, PRICE_FLIP, SIDE_FLIP, SIDE_FLIP ^ PRICE_FLIP):
        for h in range(held):
            slot = (fac ^ flip) * held + h

            def find(b, name):
                return jnp.where(slot_ref[b] == slot, b, name)

            names.append(lax.fori_loop(0, slot_ref.shape[0], find, 0, unroll=True).astype(jnp.float32))
    trades = packet_refs[0].shape[1]
    place = lax.broadcasted_iota(jnp.int32, (SET_DEV, trades), 0).astype(jnp.float32)
    for source, packet_ref in enumerate(packet_refs):
        at = slice(source * trades, (source + 1) * trades)
        tags = packet_ref[2 * part :, :].astype(jnp.float32)
        weights = [packet_ref[k * part : (k + 1) * part, :].astype(jnp.float32) for k in range(2)]
        for b, name in enumerate(names):
            picked = jnp.where(tags[0:1] == name, weights[0], 0.0)
            picked = jnp.where(tags[1:2] == name, weights[1], picked)
            chosen_ref[b * part : (b + 1) * part, at] = picked.astype(jnp.bfloat16)
        for i, flip in enumerate(flips):
            owner = (fac ^ flip).astype(jnp.float32)
            local = jnp.where(tags[2:3] == owner, tags[3:4], -1.0)
            mark = jnp.where(local == place, 1.0, 0.0)
            marks_ref[i * SET_DEV : (i + 1) * SET_DEV, at] = mark.astype(jnp.bfloat16)
    sums = f32_dot(chosen_ref[...], marks_ref[...], NT)
    half = own_ref.shape[0]
    own_ref[...] = sums[:half]
    narrow_ref[...] = sums[:half].astype(jnp.bfloat16)
    other_ref[...] = sums[half:].astype(jnp.bfloat16)


def merge_kernel(*refs):
    part_refs, shares_ref = refs[:-1], refs[-1]
    rows, columns = part_refs[0].shape
    pair = 2 * SET_DEV
    for i in range(len(part_refs) // 2):
        own_ref, other_ref = part_refs[2 * i : 2 * i + 2]
        for at in range(0, columns, pair):
            own = own_ref[:, at : at + pair].astype(jnp.float32)
            other = pltpu.roll(other_ref[:, at : at + pair].astype(jnp.float32), SET_DEV, 1)
            shares_ref[i * rows : (i + 1) * rows, at : at + pair] = (own + other).astype(jnp.bfloat16)


def value_kernel(part, held, scen_count, *refs):
    cores_refs, price_refs = refs[:2], refs[2:4]
    out_refs, whole_ref = refs[4:-1], refs[-1]
    scen = lax.axis_index("scen")
    for i in range(scen_count):
        column = (scen ^ i) * part
        for b in range(2 * held):
            row = (i // 2 * 2 * held + b) * part
            at = pl.ds(pl.multiple_of(b * BLOCK + column, part), part)
            whole_ref[at, :] = cores_refs[i % 2][row : row + part, :].astype(jnp.float32)
    width = held * BLOCK
    total = None
    for i, price_ref in enumerate(price_refs):
        whole = whole_ref[i * width : (i + 1) * width, :].T.astype(jnp.bfloat16)
        term = f32_dot(whole, price_ref[...], NT)
        total = term if total is None else total + term
    for p, out_ref in enumerate(out_refs):
        out_ref[...] = total[p * SET_DEV : (p + 1) * SET_DEV].astype(out_ref.dtype)


def exposure_of(part_refs, date, rows):
    at = slice(date * rows, (date + 1) * rows)
    nets = part_refs[0][:, at]
    for ref in part_refs[1:]:
        nets = nets + ref[:, at].astype(jnp.float32)
    return jnp.maximum(nets, 0.0)


def totals_kernel(rows, *refs):
    for date in range(DATES):
        refs[-1][date] = jnp.sum(exposure_of(refs[:-1], date, rows), axis=1)


def expose_kernel(rows, *refs):
    for date in range(DATES):
        refs[-1][date] = exposure_of(refs[:-1], date, rows)


def from_partner(x, axis, flip):
    count = lax.axis_size(axis)
    return lax.ppermute(x, axis, [(i, i ^ flip) for i in range(count)])


def from_both(x, scen_flip, fac_flip):
    count = lax.axis_size("fac")
    pairs = [
        (i * count + j, (i ^ scen_flip) * count + (j ^ fac_flip))
        for i in range(lax.axis_size("scen"))
        for j in range(count)
    ]
    return lax.ppermute(x, ("scen", "fac"), pairs)


def body(
    shocks,
    loadings,
    vol,
    jump_counts,
    jump_noise,
    jump_mean,
    jump_vol,
    dependencies,
    block_slot,
    trade_weights,
    netting,
):
    fac_count = lax.axis_size("fac")
    scen_count = lax.axis_size("scen")
    rows = shocks.shape[1]
    width = loadings.shape[1]
    held = width // BLOCK
    trades = trade_weights.shape[0]
    part = BLOCK // scen_count
    column_flips = [i for i in range(fac_count) if not i & SIDE_FLIP]
    owner_flips = [i for i in range(fac_count) if not i & PRICE_FLIP]

    pick = pl.pallas_call(
        functools.partial(pick_kernel, part),
        out_shape=jax.ShapeDtypeStruct((max(part, 16), BLOCK), jnp.bfloat16),
        out_specs=VMEM,
        compiler_params=PARAMS,
        cost_estimate=pl.CostEstimate(flops=10**10, bytes_accessed=0, transcendentals=0),
        name="pick",
    )()
    packet = pl.pallas_call(
        functools.partial(pack_kernel, part),
        out_shape=jax.ShapeDtypeStruct((2 * part + TAGS, trades), jnp.bfloat16),
        in_specs=[VMEM] * 4,
        out_specs=VMEM,
        compiler_params=PARAMS,
        name="pack",
    )(pick, trade_weights, dependencies.T, netting[None])
    order = column_flips[1:2] + column_flips[:1:-1]
    packets = [packet] + [from_partner(packet, "fac", i) for i in order]

    packet, shocks = lax.optimization_barrier((packet, shocks))
    prices = pl.pallas_call(
        price_kernel,
        out_shape=jax.ShapeDtypeStruct((DATES * rows, width), jnp.bfloat16),
        in_specs=[VMEM] * 7,
        out_specs=VMEM,
        compiler_params=PARAMS,
        name="price",
    )(shocks, loadings, vol[None], jump_counts, jump_noise, jump_mean[None], jump_vol[None])
    share_shape = (2 * held * part, len(owner_flips) * SET_DEV)
    column_trades = len(column_flips) * trades
    own, narrow, other = pl.pallas_call(
        functools.partial(combine_kernel, part, held, owner_flips),
        out_shape=[
            jax.ShapeDtypeStruct(share_shape, jnp.float32),
            jax.ShapeDtypeStruct(share_shape, jnp.bfloat16),
            jax.ShapeDtypeStruct(share_shape, jnp.bfloat16),
        ],
        in_specs=[SMEM] + [VMEM] * len(packets),
        out_specs=[VMEM] * 3,
        scratch_shapes=[
            pltpu.VMEM((2 * share_shape[0], column_trades), jnp.bfloat16),
            pltpu.VMEM((share_shape[1], column_trades), jnp.bfloat16),
        ],
        compiler_params=PARAMS,
        cost_estimate=pl.CostEstimate(flops=10**9, bytes_accessed=0, transcendentals=0),
        name="combine",
    )(block_slot, *packets)
    pair_prices = [prices, from_partner(prices, "fac", PRICE_FLIP)]
    parts = []
    for i in range(0, scen_count, 2):
        parts.append(from_partner(narrow, "scen", i) if i else own)
        parts.append(from_both(other, i, SIDE_FLIP))
    shares = pl.pallas_call(
        merge_kernel,
        out_shape=jax.ShapeDtypeStruct((len(parts) // 2 * share_shape[0], share_shape[1]), jnp.bfloat16),
        in_specs=[VMEM] * len(parts),
        out_specs=VMEM,
        compiler_params=PARAMS,
        name="merge",
    )(*parts)
    shares = [shares, from_partner(shares, "scen", 1)]

    parts = pl.pallas_call(
        functools.partial(value_kernel, part, held, scen_count),
        out_shape=[
            jax.ShapeDtypeStruct((SET_DEV, DATES * rows), jnp.bfloat16 if flip else jnp.float32)
            for flip in owner_flips
        ],
        in_specs=[VMEM] * 4,
        out_specs=[VMEM] * len(owner_flips),
        scratch_shapes=[pltpu.VMEM((2 * width, share_shape[1]), jnp.float32)],
        compiler_params=PARAMS,
        name="value",
    )(*shares, *pair_prices)
    sends = list(zip(parts[1:], owner_flips[1:]))
    sends = sends[1:] + sends[:1]
    parts = [parts[0]] + [from_partner(x, "fac", i) for x, i in sends]

    totals = pl.pallas_call(
        functools.partial(totals_kernel, rows),
        out_shape=jax.ShapeDtypeStruct((DATES, SET_DEV), jnp.float32),
        in_specs=[VMEM] * len(parts),
        out_specs=VMEM,
        compiler_params=PARAMS,
        name="totals",
    )(*parts)
    exposure = pl.pallas_call(
        functools.partial(expose_kernel, rows),
        out_shape=jax.ShapeDtypeStruct((DATES, SET_DEV, rows), jnp.float32),
        in_specs=[VMEM] * len(parts),
        out_specs=VMEM,
        compiler_params=PARAMS,
        name="expose",
    )(*parts)
    sums = [totals] + [None] * (scen_count - 1)
    for i in [*range(1, scen_count, 2), *range(2, scen_count, 2)]:
        sums[i] = from_partner(totals, "scen", i)
    while len(sums) > 1:
        sums = [sums[i] + sums[i + 1] for i in range(0, len(sums), 2)]
    return (exposure, sums[0] / (rows * scen_count))


def solution(mesh):
    placed = (
        P(None, "scen", None),
        P(None, "fac"),
        P("fac"),
        P(None, "scen", "fac"),
        P(None, "scen", "fac"),
        P("fac"),
        P("fac"),
        P("fac", None),
        P(),
        P("fac", None, None),
        P("fac"),
    )
    return jax.shard_map(
        body,
        mesh=mesh,
        in_specs=placed,
        out_specs=(P(None, "fac", "scen"), P(None, "fac")),
        check_vma=False,
    )
```

```python
import functools

import jax
import jax.numpy as jnp
from jax import lax
from jax.experimental import pallas as pl
from jax.experimental.pallas import tpu as pltpu
from jax.sharding import PartitionSpec as P

BLOCK = 128
SET_DEV = 64
DATES = 2
SIDE_FLIP = 1
PRICE_FLIP = 6
HALF_FLIP = 4
TAGS = 16
CHUNK = 64

VMEM = pl.BlockSpec(memory_space=pltpu.VMEM)
HBM = pl.BlockSpec(memory_space=pltpu.HBM)
SMEM = pl.BlockSpec(memory_space=pltpu.SMEM)
PARAMS = pltpu.CompilerParams(vmem_limit_bytes=16 * 1024 * 1024)
NT = (((1,), (1,)), ((), ()))


def f32_dot(a, b, dims):
    return lax.dot_general(a, b, dims, preferred_element_type=jnp.float32)


def pick_kernel(part, pick_ref):
    row = lax.broadcasted_iota(jnp.int32, pick_ref.shape, 0)
    column = lax.broadcasted_iota(jnp.int32, pick_ref.shape, 1)
    pick = column == lax.axis_index("scen") * part + row
    pick_ref[...] = pick.astype(jnp.float32).astype(jnp.bfloat16)


def pack_kernel(part, pick_ref, weights_ref, deps_ref, netting_ref, packet_ref):
    for k in range(2):
        share = f32_dot(pick_ref[...], weights_ref[:, k, :], NT)
        packet_ref[k * part : (k + 1) * part, :] = share[:part].astype(jnp.bfloat16)
    netting = netting_ref[...]
    tags = jnp.concatenate(
        [
            deps_ref[...],
            netting // SET_DEV,
            netting % SET_DEV,
            jnp.zeros((TAGS - 4, netting.shape[1]), jnp.int32),
        ],
        axis=0,
    )
    packet_ref[2 * part :, :] = tags.astype(jnp.float32).astype(jnp.bfloat16)


def price_kernel(shocks_ref, loadings_ref, vol_ref, counts_ref, noise_ref, mean_ref, dev_ref, out_ref):
    rows = shocks_ref.shape[1]
    vol = vol_ref[...]
    drift = 0.5 * vol * vol
    mean = mean_ref[...]
    dev = dev_ref[...]
    loadings = loadings_ref[...]
    for i in range(0, rows, CHUNK):
        at = slice(i, i + CHUNK)
        level = jnp.zeros((CHUNK, vol.shape[1]), jnp.float32)
        for date in range(DATES):
            diffuse = jnp.dot(shocks_ref[date, at, :], loadings, preferred_element_type=jnp.float32)
            counts = counts_ref[date, at, :].astype(jnp.float32)
            noise = noise_ref[date, at, :].astype(jnp.float32)
            level = level + vol * diffuse - drift + counts * mean + jnp.sqrt(counts) * dev * noise
            out_ref[date * rows + i : date * rows + i + CHUNK, :] = (jnp.exp(level) - 1.0).astype(
                jnp.bfloat16
            )


def combine_kernel(part, held, flips, *refs):
    slot_ref, packet_refs = refs[0], refs[1:-5]
    own_ref, narrow_ref, other_ref, chosen_ref, marks_ref = refs[-5:]
    fac = lax.axis_index("fac")
    names = []
    for flip in (0, PRICE_FLIP, SIDE_FLIP, SIDE_FLIP ^ PRICE_FLIP):
        for h in range(held):
            slot = (fac ^ flip) * held + h

            def find(b, name):
                return jnp.where(slot_ref[b] == slot, b, name)

            names.append(lax.fori_loop(0, slot_ref.shape[0], find, 0, unroll=True).astype(jnp.float32))
    trades = packet_refs[0].shape[1]
    place = lax.broadcasted_iota(jnp.int32, (SET_DEV, trades), 0).astype(jnp.float32)
    for source, packet_ref in enumerate(packet_refs):
        at = slice(source * trades, (source + 1) * trades)
        tags = packet_ref[2 * part :, :].astype(jnp.float32)
        weights = [packet_ref[k * part : (k + 1) * part, :].astype(jnp.float32) for k in range(2)]
        for b, name in enumerate(names):
            picked = jnp.where(tags[0:1] == name, weights[0], 0.0)
            picked = jnp.where(tags[1:2] == name, weights[1], picked)
            chosen_ref[b * part : (b + 1) * part, at] = picked.astype(jnp.bfloat16)
        for i, flip in enumerate(flips):
            owner = (fac ^ flip).astype(jnp.float32)
            local = jnp.where(tags[2:3] == owner, tags[3:4], -1.0)
            mark = jnp.where(local == place, 1.0, 0.0)
            marks_ref[i * SET_DEV : (i + 1) * SET_DEV, at] = mark.astype(jnp.bfloat16)
    sums = f32_dot(chosen_ref[...], marks_ref[...], NT)
    half = own_ref.shape[0]
    own_ref[...] = sums[:half]
    narrow_ref[...] = sums[:half].astype(jnp.bfloat16)
    other_ref[...] = sums[half:].astype(jnp.bfloat16)


def merge_kernel(*refs):
    part_refs, shares_ref = refs[:-1], refs[-1]
    rows, columns = part_refs[0].shape
    pair = 2 * SET_DEV
    for i in range(len(part_refs) // 2):
        own_ref, other_ref = part_refs[2 * i : 2 * i + 2]
        for at in range(0, columns, pair):
            own = own_ref[:, at : at + pair].astype(jnp.float32)
            other = pltpu.roll(other_ref[:, at : at + pair].astype(jnp.float32), SET_DEV, 1)
            shares_ref[i * rows : (i + 1) * rows, at : at + pair] = (own + other).astype(jnp.bfloat16)


def value_kernel(part, held, scen_count, *refs):
    cores_refs, price_refs = refs[:2], refs[2:4]
    out_refs, whole_ref = refs[4:-1], refs[-1]
    scen = lax.axis_index("scen")
    for i in range(scen_count):
        column = (scen ^ i) * part
        for b in range(2 * held):
            row = (i // 2 * 2 * held + b) * part
            at = pl.ds(pl.multiple_of(b * BLOCK + column, part), part)
            whole_ref[at, :] = cores_refs[i % 2][row : row + part, :].astype(jnp.float32)
    width = held * BLOCK
    total = None
    for i, price_ref in enumerate(price_refs):
        whole = whole_ref[i * width : (i + 1) * width, :].T.astype(jnp.bfloat16)
        term = f32_dot(whole, price_ref[...], NT)
        total = term if total is None else total + term
    for p, out_ref in enumerate(out_refs):
        out_ref[...] = total[p * SET_DEV : (p + 1) * SET_DEV].astype(out_ref.dtype)


def exposure_of(part_refs, date, rows):
    at = slice(date * rows, (date + 1) * rows)
    nets = part_refs[0][:, at]
    for ref in part_refs[1:]:
        nets = nets + ref[:, at].astype(jnp.float32)
    return jnp.maximum(nets, 0.0)


def totals_kernel(rows, *refs):
    for date in range(DATES):
        refs[-1][date] = jnp.sum(exposure_of(refs[:-1], date, rows), axis=1)


def expose_kernel(rows, *refs):
    for date in range(DATES):
        refs[-1][date] = exposure_of(refs[:-1], date, rows)


def from_partner(x, axis, flip):
    count = lax.axis_size(axis)
    return lax.ppermute(x, axis, [(i, i ^ flip) for i in range(count)])


def from_both(x, scen_flip, fac_flip):
    count = lax.axis_size("fac")
    pairs = [
        (i * count + j, (i ^ scen_flip) * count + (j ^ fac_flip))
        for i in range(lax.axis_size("scen"))
        for j in range(count)
    ]
    return lax.ppermute(x, ("scen", "fac"), pairs)


def body(
    shocks,
    loadings,
    vol,
    jump_counts,
    jump_noise,
    jump_mean,
    jump_vol,
    dependencies,
    block_slot,
    trade_weights,
    netting,
):
    fac_count = lax.axis_size("fac")
    scen_count = lax.axis_size("scen")
    rows = shocks.shape[1]
    width = loadings.shape[1]
    held = width // BLOCK
    trades = trade_weights.shape[0]
    part = BLOCK // scen_count
    column_flips = [i for i in range(fac_count) if not i & SIDE_FLIP]
    owner_flips = [i for i in range(fac_count) if not i & HALF_FLIP]

    pick = pl.pallas_call(
        functools.partial(pick_kernel, part),
        out_shape=jax.ShapeDtypeStruct((max(part, 16), BLOCK), jnp.bfloat16),
        out_specs=VMEM,
        compiler_params=PARAMS,
        cost_estimate=pl.CostEstimate(flops=10**10, bytes_accessed=0, transcendentals=0),
        name="pick",
    )()
    packet = pl.pallas_call(
        functools.partial(pack_kernel, part),
        out_shape=jax.ShapeDtypeStruct((2 * part + TAGS, trades), jnp.bfloat16),
        in_specs=[VMEM] * 4,
        out_specs=VMEM,
        compiler_params=PARAMS,
        name="pack",
    )(pick, trade_weights, dependencies.T, netting[None])
    order = column_flips[1:2] + column_flips[:1:-1]
    packets = [packet] + [from_partner(packet, "fac", i) for i in order]

    packet, shocks = lax.optimization_barrier((packet, shocks))
    prices = pl.pallas_call(
        price_kernel,
        out_shape=jax.ShapeDtypeStruct((DATES * rows, width), jnp.bfloat16),
        in_specs=[VMEM] * 7,
        out_specs=VMEM,
        compiler_params=PARAMS,
        name="price",
    )(shocks, loadings, vol[None], jump_counts, jump_noise, jump_mean[None], jump_vol[None])
    share_shape = (2 * held * part, len(owner_flips) * SET_DEV)
    column_trades = len(column_flips) * trades
    own, narrow, other = pl.pallas_call(
        functools.partial(combine_kernel, part, held, owner_flips),
        out_shape=[
            jax.ShapeDtypeStruct(share_shape, jnp.float32),
            jax.ShapeDtypeStruct(share_shape, jnp.bfloat16),
            jax.ShapeDtypeStruct(share_shape, jnp.bfloat16),
        ],
        in_specs=[SMEM] + [VMEM] * len(packets),
        out_specs=[VMEM] * 3,
        scratch_shapes=[
            pltpu.VMEM((2 * share_shape[0], column_trades), jnp.bfloat16),
            pltpu.VMEM((share_shape[1], column_trades), jnp.bfloat16),
        ],
        compiler_params=PARAMS,
        cost_estimate=pl.CostEstimate(flops=10**9, bytes_accessed=0, transcendentals=0),
        name="combine",
    )(block_slot, *packets)
    pair_prices = [prices, from_partner(prices, "fac", PRICE_FLIP)]
    parts = []
    for i in range(0, scen_count, 2):
        parts.append(from_partner(narrow, "scen", i) if i else own)
        parts.append(from_both(other, i, SIDE_FLIP))
    shares = pl.pallas_call(
        merge_kernel,
        out_shape=jax.ShapeDtypeStruct((len(parts) // 2 * share_shape[0], share_shape[1]), jnp.bfloat16),
        in_specs=[VMEM] * len(parts),
        out_specs=VMEM,
        compiler_params=PARAMS,
        name="merge",
    )(*parts)
    shares = [shares, from_partner(shares, "scen", 1)]

    parts = pl.pallas_call(
        functools.partial(value_kernel, part, held, scen_count),
        out_shape=[
            jax.ShapeDtypeStruct((SET_DEV, DATES * rows), jnp.bfloat16 if flip else jnp.float32)
            for flip in owner_flips
        ],
        in_specs=[VMEM] * 4,
        out_specs=[VMEM] * len(owner_flips),
        scratch_shapes=[pltpu.VMEM((2 * width, share_shape[1]), jnp.float32)],
        compiler_params=PARAMS,
        name="value",
    )(*shares, *pair_prices)
    sends = list(zip(parts[1:], owner_flips[1:]))
    sends = sends[1:2] + sends[:1] + sends[2:]
    parts = [parts[0]] + [from_partner(x, "fac", i) for x, i in sends]

    totals = pl.pallas_call(
        functools.partial(totals_kernel, rows),
        out_shape=jax.ShapeDtypeStruct((DATES, SET_DEV), jnp.float32),
        in_specs=[VMEM] * len(parts),
        out_specs=VMEM,
        compiler_params=PARAMS,
        name="totals",
    )(*parts)
    exposure = pl.pallas_call(
        functools.partial(expose_kernel, rows),
        out_shape=jax.ShapeDtypeStruct((DATES, SET_DEV, rows), jnp.float32),
        in_specs=[VMEM] * len(parts),
        out_specs=VMEM,
        compiler_params=PARAMS,
        name="expose",
    )(*parts)
    sums = [totals] + [None] * (scen_count - 1)
    for i in [*range(1, scen_count, 2), *range(2, scen_count, 2)]:
        sums[i] = from_partner(totals, "scen", i)
    while len(sums) > 1:
        sums = [sums[i] + sums[i + 1] for i in range(0, len(sums), 2)]
    return (exposure, sums[0] / (rows * scen_count))


def solution(mesh):
    placed = (
        P(None, "scen", None),
        P(None, "fac"),
        P("fac"),
        P(None, "scen", "fac"),
        P(None, "scen", "fac"),
        P("fac"),
        P("fac"),
        P("fac", None),
        P(),
        P("fac", None, None),
        P("fac"),
    )
    return jax.shard_map(
        body,
        mesh=mesh,
        in_specs=placed,
        out_specs=(P(None, "fac", "scen"), P(None, "fac")),
        check_vma=False,
    )
```

```python
import functools

import jax
import jax.numpy as jnp
from jax import lax
from jax.experimental import pallas as pl
from jax.experimental.pallas import tpu as pltpu
from jax.sharding import PartitionSpec as P

BLOCK = 128
SET_DEV = 64
DATES = 2
SIDE_FLIP = 1
PRICE_FLIP = 6
HALF_FLIP = 4
TAGS = 16
CHUNK = 64

VMEM = pl.BlockSpec(memory_space=pltpu.VMEM)
HBM = pl.BlockSpec(memory_space=pltpu.HBM)
SMEM = pl.BlockSpec(memory_space=pltpu.SMEM)
PARAMS = pltpu.CompilerParams(vmem_limit_bytes=16 * 1024 * 1024)
NT = (((1,), (1,)), ((), ()))


def f32_dot(a, b, dims):
    return lax.dot_general(a, b, dims, preferred_element_type=jnp.float32)


def pick_kernel(part, pick_ref):
    row = lax.broadcasted_iota(jnp.int32, pick_ref.shape, 0)
    column = lax.broadcasted_iota(jnp.int32, pick_ref.shape, 1)
    pick = column == lax.axis_index("scen") * part + row
    pick_ref[...] = pick.astype(jnp.float32).astype(jnp.bfloat16)


def pack_kernel(part, pick_ref, weights_ref, deps_ref, netting_ref, packet_ref):
    for k in range(2):
        share = f32_dot(pick_ref[...], weights_ref[:, k, :], NT)
        packet_ref[k * part : (k + 1) * part, :] = share[:part].astype(jnp.bfloat16)
    netting = netting_ref[...]
    tags = jnp.concatenate(
        [
            deps_ref[...],
            netting // SET_DEV,
            netting % SET_DEV,
            jnp.zeros((TAGS - 4, netting.shape[1]), jnp.int32),
        ],
        axis=0,
    )
    packet_ref[2 * part :, :] = tags.astype(jnp.float32).astype(jnp.bfloat16)


def price_kernel(shocks_ref, loadings_ref, vol_ref, counts_ref, noise_ref, mean_ref, dev_ref, out_ref):
    rows = shocks_ref.shape[1]
    vol = vol_ref[...]
    drift = 0.5 * vol * vol
    mean = mean_ref[...]
    dev = dev_ref[...]
    loadings = loadings_ref[...]
    for i in range(0, rows, CHUNK):
        at = slice(i, i + CHUNK)
        level = jnp.zeros((CHUNK, vol.shape[1]), jnp.float32)
        for date in range(DATES):
            diffuse = jnp.dot(shocks_ref[date, at, :], loadings, preferred_element_type=jnp.float32)
            counts = counts_ref[date, at, :].astype(jnp.float32)
            noise = noise_ref[date, at, :].astype(jnp.float32)
            level = level + vol * diffuse - drift + counts * mean + jnp.sqrt(counts) * dev * noise
            out_ref[date * rows + i : date * rows + i + CHUNK, :] = (jnp.exp(level) - 1.0).astype(
                jnp.bfloat16
            )


def combine_kernel(part, held, flips, *refs):
    slot_ref, packet_refs = refs[0], refs[1:-5]
    own_ref, narrow_ref, other_ref, chosen_ref, marks_ref = refs[-5:]
    fac = lax.axis_index("fac")
    names = []
    for flip in (0, PRICE_FLIP, SIDE_FLIP, SIDE_FLIP ^ PRICE_FLIP):
        for h in range(held):
            slot = (fac ^ flip) * held + h

            def find(b, name):
                return jnp.where(slot_ref[b] == slot, b, name)

            names.append(lax.fori_loop(0, slot_ref.shape[0], find, 0, unroll=True).astype(jnp.float32))
    trades = packet_refs[0].shape[1]
    place = lax.broadcasted_iota(jnp.int32, (SET_DEV, trades), 0).astype(jnp.float32)
    for source, packet_ref in enumerate(packet_refs):
        at = slice(source * trades, (source + 1) * trades)
        tags = packet_ref[2 * part :, :].astype(jnp.float32)
        weights = [packet_ref[k * part : (k + 1) * part, :].astype(jnp.float32) for k in range(2)]
        for b, name in enumerate(names):
            picked = jnp.where(tags[0:1] == name, weights[0], 0.0)
            picked = jnp.where(tags[1:2] == name, weights[1], picked)
            chosen_ref[b * part : (b + 1) * part, at] = picked.astype(jnp.bfloat16)
        for i, flip in enumerate(flips):
            owner = (fac ^ flip).astype(jnp.float32)
            local = jnp.where(tags[2:3] == owner, tags[3:4], -1.0)
            mark = jnp.where(local == place, 1.0, 0.0)
            marks_ref[i * SET_DEV : (i + 1) * SET_DEV, at] = mark.astype(jnp.bfloat16)
    sums = f32_dot(chosen_ref[...], marks_ref[...], NT)
    half = own_ref.shape[0]
    own_ref[...] = sums[:half]
    narrow_ref[...] = sums[:half].astype(jnp.bfloat16)
    other_ref[...] = sums[half:].astype(jnp.bfloat16)


def merge_kernel(*refs):
    part_refs, shares_ref = refs[:-1], refs[-1]
    rows, columns = part_refs[0].shape
    pair = 2 * SET_DEV
    for i in range(len(part_refs) // 2):
        own_ref, other_ref = part_refs[2 * i : 2 * i + 2]
        for at in range(0, columns, pair):
            own = own_ref[:, at : at + pair].astype(jnp.float32)
            other = pltpu.roll(other_ref[:, at : at + pair].astype(jnp.float32), SET_DEV, 1)
            shares_ref[i * rows : (i + 1) * rows, at : at + pair] = (own + other).astype(jnp.bfloat16)


def value_kernel(part, held, scen_count, *refs):
    cores_refs, price_refs = refs[:2], refs[2:4]
    out_refs, whole_ref = refs[4:-1], refs[-1]
    scen = lax.axis_index("scen")
    for i in range(scen_count):
        column = (scen ^ i) * part
        for b in range(2 * held):
            row = (i // 2 * 2 * held + b) * part
            at = pl.ds(pl.multiple_of(b * BLOCK + column, part), part)
            whole_ref[at, :] = cores_refs[i % 2][row : row + part, :].astype(jnp.float32)
    width = held * BLOCK
    total = None
    for i, price_ref in enumerate(price_refs):
        whole = whole_ref[i * width : (i + 1) * width, :].T.astype(jnp.bfloat16)
        term = f32_dot(whole, price_ref[...], NT)
        total = term if total is None else total + term
    for p, out_ref in enumerate(out_refs):
        out_ref[...] = total[p * SET_DEV : (p + 1) * SET_DEV].astype(out_ref.dtype)


def exposure_of(part_refs, date, rows):
    at = slice(date * rows, (date + 1) * rows)
    nets = part_refs[0][:, at]
    for ref in part_refs[1:]:
        nets = nets + ref[:, at].astype(jnp.float32)
    return jnp.maximum(nets, 0.0)


def totals_kernel(rows, *refs):
    for date in range(DATES):
        refs[-1][date] = jnp.sum(exposure_of(refs[:-1], date, rows), axis=1)


def expose_kernel(rows, *refs):
    for date in range(DATES):
        refs[-1][date] = exposure_of(refs[:-1], date, rows)


def from_partner(x, axis, flip):
    count = lax.axis_size(axis)
    return lax.ppermute(x, axis, [(i, i ^ flip) for i in range(count)])


def from_both(x, scen_flip, fac_flip):
    count = lax.axis_size("fac")
    pairs = [
        (i * count + j, (i ^ scen_flip) * count + (j ^ fac_flip))
        for i in range(lax.axis_size("scen"))
        for j in range(count)
    ]
    return lax.ppermute(x, ("scen", "fac"), pairs)


def body(
    shocks,
    loadings,
    vol,
    jump_counts,
    jump_noise,
    jump_mean,
    jump_vol,
    dependencies,
    block_slot,
    trade_weights,
    netting,
):
    fac_count = lax.axis_size("fac")
    scen_count = lax.axis_size("scen")
    rows = shocks.shape[1]
    width = loadings.shape[1]
    held = width // BLOCK
    trades = trade_weights.shape[0]
    part = BLOCK // scen_count
    column_flips = [i for i in range(fac_count) if not i & SIDE_FLIP]
    owner_flips = [i for i in range(fac_count) if not i & HALF_FLIP]

    pick = pl.pallas_call(
        functools.partial(pick_kernel, part),
        out_shape=jax.ShapeDtypeStruct((max(part, 16), BLOCK), jnp.bfloat16),
        out_specs=VMEM,
        compiler_params=PARAMS,
        cost_estimate=pl.CostEstimate(flops=10**10, bytes_accessed=0, transcendentals=0),
        name="pick",
    )()
    packet = pl.pallas_call(
        functools.partial(pack_kernel, part),
        out_shape=jax.ShapeDtypeStruct((2 * part + TAGS, trades), jnp.bfloat16),
        in_specs=[VMEM] * 4,
        out_specs=VMEM,
        compiler_params=PARAMS,
        name="pack",
    )(pick, trade_weights, dependencies.T, netting[None])
    order = column_flips[1:2] + column_flips[:1:-1]
    packets = [packet] + [from_partner(packet, "fac", i) for i in order]

    packet, shocks = lax.optimization_barrier((packet, shocks))
    prices = pl.pallas_call(
        price_kernel,
        out_shape=jax.ShapeDtypeStruct((DATES * rows, width), jnp.bfloat16),
        in_specs=[VMEM] * 7,
        out_specs=VMEM,
        compiler_params=PARAMS,
        name="price",
    )(shocks, loadings, vol[None], jump_counts, jump_noise, jump_mean[None], jump_vol[None])
    share_shape = (2 * held * part, len(owner_flips) * SET_DEV)
    column_trades = len(column_flips) * trades
    own, narrow, other = pl.pallas_call(
        functools.partial(combine_kernel, part, held, owner_flips),
        out_shape=[
            jax.ShapeDtypeStruct(share_shape, jnp.float32),
            jax.ShapeDtypeStruct(share_shape, jnp.bfloat16),
            jax.ShapeDtypeStruct(share_shape, jnp.bfloat16),
        ],
        in_specs=[SMEM] + [VMEM] * len(packets),
        out_specs=[VMEM] * 3,
        scratch_shapes=[
            pltpu.VMEM((2 * share_shape[0], column_trades), jnp.bfloat16),
            pltpu.VMEM((share_shape[1], column_trades), jnp.bfloat16),
        ],
        compiler_params=PARAMS,
        cost_estimate=pl.CostEstimate(flops=10**9, bytes_accessed=0, transcendentals=0),
        name="combine",
    )(block_slot, *packets)
    pair_prices = [prices, from_partner(prices, "fac", PRICE_FLIP)]
    parts = []
    for i in range(0, scen_count, 2):
        parts.append(from_partner(narrow, "scen", i) if i else own)
        parts.append(from_both(other, i, SIDE_FLIP))
    shares = pl.pallas_call(
        merge_kernel,
        out_shape=jax.ShapeDtypeStruct((len(parts) // 2 * share_shape[0], share_shape[1]), jnp.bfloat16),
        in_specs=[VMEM] * len(parts),
        out_specs=VMEM,
        compiler_params=PARAMS,
        name="merge",
    )(*parts)
    shares = [shares, from_partner(shares, "scen", 1)]

    parts = pl.pallas_call(
        functools.partial(value_kernel, part, held, scen_count),
        out_shape=[
            jax.ShapeDtypeStruct((SET_DEV, DATES * rows), jnp.bfloat16 if flip else jnp.float32)
            for flip in owner_flips
        ],
        in_specs=[VMEM] * 4,
        out_specs=[VMEM] * len(owner_flips),
        scratch_shapes=[pltpu.VMEM((2 * width, share_shape[1]), jnp.float32)],
        compiler_params=PARAMS,
        name="value",
    )(*shares, *pair_prices)
    sends = list(zip(parts[1:], owner_flips[1:]))
    sends = sends[1:] + sends[:1]
    parts = [parts[0]] + [from_partner(x, "fac", i) for x, i in sends]

    totals = pl.pallas_call(
        functools.partial(totals_kernel, rows),
        out_shape=jax.ShapeDtypeStruct((DATES, SET_DEV), jnp.float32),
        in_specs=[VMEM] * len(parts),
        out_specs=VMEM,
        compiler_params=PARAMS,
        name="totals",
    )(*parts)
    exposure = pl.pallas_call(
        functools.partial(expose_kernel, rows),
        out_shape=jax.ShapeDtypeStruct((DATES, SET_DEV, rows), jnp.float32),
        in_specs=[VMEM] * len(parts),
        out_specs=VMEM,
        compiler_params=PARAMS,
        name="expose",
    )(*parts)
    sums = [totals] + [None] * (scen_count - 1)
    for i in [*range(1, scen_count, 2), *range(2, scen_count, 2)]:
        sums[i] = from_partner(totals, "scen", i)
    while len(sums) > 1:
        sums = [sums[i] + sums[i + 1] for i in range(0, len(sums), 2)]
    return (exposure, sums[0] / (rows * scen_count))


def solution(mesh):
    placed = (
        P(None, "scen", None),
        P(None, "fac"),
        P("fac"),
        P(None, "scen", "fac"),
        P(None, "scen", "fac"),
        P("fac"),
        P("fac"),
        P("fac", None),
        P(),
        P("fac", None, None),
        P("fac"),
    )
    return jax.shard_map(
        body,
        mesh=mesh,
        in_specs=placed,
        out_specs=(P(None, "fac", "scen"), P(None, "fac")),
        check_vma=False,
    )
```

```python
import functools

import jax
import jax.numpy as jnp
from jax import lax
from jax.experimental import pallas as pl
from jax.experimental.pallas import tpu as pltpu
from jax.sharding import PartitionSpec as P

BLOCK = 128
SET_DEV = 64
DATES = 2
SIDE_FLIP = 1
PRICE_FLIP = 6
HALF_FLIP = 4
TAGS = 16
CHUNK = 64

VMEM = pl.BlockSpec(memory_space=pltpu.VMEM)
HBM = pl.BlockSpec(memory_space=pltpu.HBM)
SMEM = pl.BlockSpec(memory_space=pltpu.SMEM)
PARAMS = pltpu.CompilerParams(vmem_limit_bytes=16 * 1024 * 1024)
NT = (((1,), (1,)), ((), ()))


def f32_dot(a, b, dims):
    return lax.dot_general(a, b, dims, preferred_element_type=jnp.float32)


def pick_kernel(part, pick_ref):
    row = lax.broadcasted_iota(jnp.int32, pick_ref.shape, 0)
    column = lax.broadcasted_iota(jnp.int32, pick_ref.shape, 1)
    pick = column == lax.axis_index("scen") * part + row
    pick_ref[...] = pick.astype(jnp.float32).astype(jnp.bfloat16)


def pack_kernel(part, pick_ref, weights_ref, deps_ref, netting_ref, packet_ref):
    for k in range(2):
        share = f32_dot(pick_ref[...], weights_ref[:, k, :], NT)
        packet_ref[k * part : (k + 1) * part, :] = share[:part].astype(jnp.bfloat16)
    netting = netting_ref[...]
    tags = jnp.concatenate(
        [
            deps_ref[...],
            netting // SET_DEV,
            netting % SET_DEV,
            jnp.zeros((TAGS - 4, netting.shape[1]), jnp.int32),
        ],
        axis=0,
    )
    packet_ref[2 * part :, :] = tags.astype(jnp.float32).astype(jnp.bfloat16)


def price_kernel(shocks_ref, loadings_ref, vol_ref, counts_ref, noise_ref, mean_ref, dev_ref, out_ref):
    rows = shocks_ref.shape[1]
    vol = vol_ref[...]
    drift = 0.5 * vol * vol
    mean = mean_ref[...]
    dev = dev_ref[...]
    loadings = loadings_ref[...]
    for i in range(0, rows, CHUNK):
        at = slice(i, i + CHUNK)
        level = jnp.zeros((CHUNK, vol.shape[1]), jnp.float32)
        for date in range(DATES):
            diffuse = jnp.dot(shocks_ref[date, at, :], loadings, preferred_element_type=jnp.float32)
            counts = counts_ref[date, at, :].astype(jnp.float32)
            noise = noise_ref[date, at, :].astype(jnp.float32)
            level = level + vol * diffuse - drift + counts * mean + jnp.sqrt(counts) * dev * noise
            out_ref[date * rows + i : date * rows + i + CHUNK, :] = (jnp.exp(level) - 1.0).astype(
                jnp.bfloat16
            )


def combine_kernel(part, held, flips, *refs):
    slot_ref, packet_refs = refs[0], refs[1:-5]
    own_ref, narrow_ref, other_ref, chosen_ref, marks_ref = refs[-5:]
    fac = lax.axis_index("fac")
    names = []
    for flip in (0, PRICE_FLIP, SIDE_FLIP, SIDE_FLIP ^ PRICE_FLIP):
        for h in range(held):
            slot = (fac ^ flip) * held + h

            def find(b, name):
                return jnp.where(slot_ref[b] == slot, b, name)

            names.append(lax.fori_loop(0, slot_ref.shape[0], find, 0, unroll=True).astype(jnp.float32))
    trades = packet_refs[0].shape[1]
    place = lax.broadcasted_iota(jnp.int32, (SET_DEV, trades), 0).astype(jnp.float32)
    for source, packet_ref in enumerate(packet_refs):
        at = slice(source * trades, (source + 1) * trades)
        tags = packet_ref[2 * part :, :].astype(jnp.float32)
        weights = [packet_ref[k * part : (k + 1) * part, :].astype(jnp.float32) for k in range(2)]
        for b, name in enumerate(names):
            picked = jnp.where(tags[0:1] == name, weights[0], 0.0)
            picked = jnp.where(tags[1:2] == name, weights[1], picked)
            chosen_ref[b * part : (b + 1) * part, at] = picked.astype(jnp.bfloat16)
        for i, flip in enumerate(flips):
            owner = (fac ^ flip).astype(jnp.float32)
            local = jnp.where(tags[2:3] == owner, tags[3:4], -1.0)
            mark = jnp.where(local == place, 1.0, 0.0)
            marks_ref[i * SET_DEV : (i + 1) * SET_DEV, at] = mark.astype(jnp.bfloat16)
    sums = f32_dot(chosen_ref[...], marks_ref[...], NT)
    half = own_ref.shape[0]
    own_ref[...] = sums[:half]
    narrow_ref[...] = sums[:half].astype(jnp.bfloat16)
    other_ref[...] = sums[half:].astype(jnp.bfloat16)


def merge_kernel(*refs):
    part_refs, shares_ref = refs[:-1], refs[-1]
    rows, columns = part_refs[0].shape
    pair = 2 * SET_DEV
    for i in range(len(part_refs) // 2):
        own_ref, other_ref = part_refs[2 * i : 2 * i + 2]
        for at in range(0, columns, pair):
            own = own_ref[:, at : at + pair].astype(jnp.float32)
            other = pltpu.roll(other_ref[:, at : at + pair].astype(jnp.float32), SET_DEV, 1)
            shares_ref[i * rows : (i + 1) * rows, at : at + pair] = (own + other).astype(jnp.bfloat16)


def own_value_kernel(part, held, scen_count, *refs):
    cores_refs, price_ref = refs[:2], refs[2]
    own_ref, later_ref, whole_ref = refs[3:]
    scen = lax.axis_index("scen")
    for i in range(scen_count):
        column = (scen ^ i) * part
        for b in range(2 * held):
            row = (i // 2 * 2 * held + b) * part
            at = pl.ds(pl.multiple_of(b * BLOCK + column, part), part)
            whole_ref[at, :] = cores_refs[i % 2][row : row + part, :].astype(jnp.float32)
    width = held * BLOCK
    own_ref[...] = f32_dot(whole_ref[:width, :].T.astype(jnp.bfloat16), price_ref[...], NT)
    later_ref[...] = whole_ref[width:, :].T.astype(jnp.bfloat16)


def value_kernel(own_ref, later_ref, price_ref, *out_refs):
    for p, out_ref in enumerate(out_refs):
        at = slice(p * SET_DEV, (p + 1) * SET_DEV)
        total = own_ref[at, :] + f32_dot(later_ref[at, :], price_ref[...], NT)
        out_ref[...] = total.astype(out_ref.dtype)


def exposure_of(part_refs, date, rows):
    at = slice(date * rows, (date + 1) * rows)
    nets = part_refs[0][:, at]
    for ref in part_refs[1:]:
        nets = nets + ref[:, at].astype(jnp.float32)
    return jnp.maximum(nets, 0.0)


def totals_kernel(rows, *refs):
    for date in range(DATES):
        refs[-1][date] = jnp.sum(exposure_of(refs[:-1], date, rows), axis=1)


def expose_kernel(rows, *refs):
    for date in range(DATES):
        refs[-1][date] = exposure_of(refs[:-1], date, rows)


def from_partner(x, axis, flip):
    count = lax.axis_size(axis)
    return lax.ppermute(x, axis, [(i, i ^ flip) for i in range(count)])


def from_both(x, scen_flip, fac_flip):
    count = lax.axis_size("fac")
    pairs = [
        (i * count + j, (i ^ scen_flip) * count + (j ^ fac_flip))
        for i in range(lax.axis_size("scen"))
        for j in range(count)
    ]
    return lax.ppermute(x, ("scen", "fac"), pairs)


def body(
    shocks,
    loadings,
    vol,
    jump_counts,
    jump_noise,
    jump_mean,
    jump_vol,
    dependencies,
    block_slot,
    trade_weights,
    netting,
):
    fac_count = lax.axis_size("fac")
    scen_count = lax.axis_size("scen")
    rows = shocks.shape[1]
    width = loadings.shape[1]
    held = width // BLOCK
    trades = trade_weights.shape[0]
    part = BLOCK // scen_count
    column_flips = [i for i in range(fac_count) if not i & SIDE_FLIP]
    owner_flips = [i for i in range(fac_count) if not i & HALF_FLIP]

    pick = pl.pallas_call(
        functools.partial(pick_kernel, part),
        out_shape=jax.ShapeDtypeStruct((max(part, 16), BLOCK), jnp.bfloat16),
        out_specs=VMEM,
        compiler_params=PARAMS,
        cost_estimate=pl.CostEstimate(flops=10**10, bytes_accessed=0, transcendentals=0),
        name="pick",
    )()
    packet = pl.pallas_call(
        functools.partial(pack_kernel, part),
        out_shape=jax.ShapeDtypeStruct((2 * part + TAGS, trades), jnp.bfloat16),
        in_specs=[VMEM] * 4,
        out_specs=VMEM,
        compiler_params=PARAMS,
        name="pack",
    )(pick, trade_weights, dependencies.T, netting[None])
    order = column_flips[2:] + column_flips[1:2]
    packets = [packet] + [from_partner(packet, "fac", i) for i in order]

    packet, shocks = lax.optimization_barrier((packet, shocks))
    prices = pl.pallas_call(
        price_kernel,
        out_shape=jax.ShapeDtypeStruct((DATES * rows, width), jnp.bfloat16),
        in_specs=[VMEM] * 7,
        out_specs=VMEM,
        compiler_params=PARAMS,
        name="price",
    )(shocks, loadings, vol[None], jump_counts, jump_noise, jump_mean[None], jump_vol[None])
    share_shape = (2 * held * part, len(owner_flips) * SET_DEV)
    column_trades = len(column_flips) * trades
    own, narrow, other = pl.pallas_call(
        functools.partial(combine_kernel, part, held, owner_flips),
        out_shape=[
            jax.ShapeDtypeStruct(share_shape, jnp.float32),
            jax.ShapeDtypeStruct(share_shape, jnp.bfloat16),
            jax.ShapeDtypeStruct(share_shape, jnp.bfloat16),
        ],
        in_specs=[SMEM] + [VMEM] * len(packets),
        out_specs=[VMEM] * 3,
        scratch_shapes=[
            pltpu.VMEM((2 * share_shape[0], column_trades), jnp.bfloat16),
            pltpu.VMEM((share_shape[1], column_trades), jnp.bfloat16),
        ],
        compiler_params=PARAMS,
        cost_estimate=pl.CostEstimate(flops=10**9, bytes_accessed=0, transcendentals=0),
        name="combine",
    )(block_slot, *packets)
    pair_prices = [prices, from_partner(prices, "fac", PRICE_FLIP)]
    parts = []
    for i in range(0, scen_count, 2):
        parts.append(from_partner(narrow, "scen", i) if i else own)
        parts.append(from_both(other, i, SIDE_FLIP))
    shares = pl.pallas_call(
        merge_kernel,
        out_shape=jax.ShapeDtypeStruct((len(parts) // 2 * share_shape[0], share_shape[1]), jnp.bfloat16),
        in_specs=[VMEM] * len(parts),
        out_specs=VMEM,
        compiler_params=PARAMS,
        name="merge",
    )(*parts)
    shares = [shares, from_partner(shares, "scen", 1)]

    sets = share_shape[1]
    own_value, later = pl.pallas_call(
        functools.partial(own_value_kernel, part, held, scen_count),
        out_shape=[
            jax.ShapeDtypeStruct((sets, DATES * rows), jnp.float32),
            jax.ShapeDtypeStruct((sets, width), jnp.bfloat16),
        ],
        in_specs=[VMEM] * 3,
        out_specs=[VMEM] * 2,
        scratch_shapes=[pltpu.VMEM((2 * width, sets), jnp.float32)],
        compiler_params=PARAMS,
        name="own_value",
    )(*shares, pair_prices[0])
    parts = pl.pallas_call(
        value_kernel,
        out_shape=[
            jax.ShapeDtypeStruct((SET_DEV, DATES * rows), jnp.bfloat16 if flip else jnp.float32)
            for flip in owner_flips
        ],
        in_specs=[VMEM] * 3,
        out_specs=[VMEM] * len(owner_flips),
        compiler_params=PARAMS,
        name="value",
    )(own_value, later, pair_prices[1])
    sends = list(zip(parts[1:], owner_flips[1:]))
    sends = sends[2:] + sends[:2]
    parts = [parts[0]] + [from_partner(x, "fac", i) for x, i in sends]

    totals = pl.pallas_call(
        functools.partial(totals_kernel, rows),
        out_shape=jax.ShapeDtypeStruct((DATES, SET_DEV), jnp.float32),
        in_specs=[VMEM] * len(parts),
        out_specs=VMEM,
        compiler_params=PARAMS,
        name="totals",
    )(*parts)
    exposure = pl.pallas_call(
        functools.partial(expose_kernel, rows),
        out_shape=jax.ShapeDtypeStruct((DATES, SET_DEV, rows), jnp.float32),
        in_specs=[VMEM] * len(parts),
        out_specs=VMEM,
        compiler_params=PARAMS,
        name="expose",
    )(*parts)
    sums = [totals] + [None] * (scen_count - 1)
    for i in [*range(1, scen_count, 2), *range(2, scen_count, 2)]:
        sums[i] = from_partner(totals, "scen", i)
    while len(sums) > 1:
        sums = [sums[i] + sums[i + 1] for i in range(0, len(sums), 2)]
    return (exposure, sums[0] / (rows * scen_count))


def solution(mesh):
    placed = (
        P(None, "scen", None),
        P(None, "fac"),
        P("fac"),
        P(None, "scen", "fac"),
        P(None, "scen", "fac"),
        P("fac"),
        P("fac"),
        P("fac", None),
        P(),
        P("fac", None, None),
        P("fac"),
    )
    return jax.shard_map(
        body,
        mesh=mesh,
        in_specs=placed,
        out_specs=(P(None, "fac", "scen"), P(None, "fac")),
        check_vma=False,
    )
```

```python
import functools

import jax
import jax.numpy as jnp
from jax import lax
from jax.experimental import pallas as pl
from jax.experimental.pallas import tpu as pltpu
from jax.sharding import PartitionSpec as P

BLOCK = 128
SET_DEV = 64
DATES = 2
SIDE_FLIP = 1
PRICE_FLIP = 6
HALF_FLIP = 4
TAGS = 16
CHUNK = 64

VMEM = pl.BlockSpec(memory_space=pltpu.VMEM)
HBM = pl.BlockSpec(memory_space=pltpu.HBM)
SMEM = pl.BlockSpec(memory_space=pltpu.SMEM)
PARAMS = pltpu.CompilerParams(vmem_limit_bytes=16 * 1024 * 1024)
NT = (((1,), (1,)), ((), ()))


def f32_dot(a, b, dims):
    return lax.dot_general(a, b, dims, preferred_element_type=jnp.float32)


def pick_kernel(part, pick_ref):
    row = lax.broadcasted_iota(jnp.int32, pick_ref.shape, 0)
    column = lax.broadcasted_iota(jnp.int32, pick_ref.shape, 1)
    pick = column == lax.axis_index("scen") * part + row
    pick_ref[...] = pick.astype(jnp.float32).astype(jnp.bfloat16)


def pack_kernel(part, *refs):
    pick_ref, weights_ref, deps_ref, netting_ref = refs[:4]
    factor_refs, packet_ref, factors_ref = refs[4:-2], refs[-2], refs[-1]
    for k in range(2):
        share = f32_dot(pick_ref[...], weights_ref[:, k, :], NT)
        packet_ref[k * part : (k + 1) * part, :] = share[:part].astype(jnp.bfloat16)
    netting = netting_ref[...]
    tags = jnp.concatenate(
        [
            deps_ref[...],
            netting // SET_DEV,
            netting % SET_DEV,
            jnp.zeros((TAGS - 4, netting.shape[1]), jnp.int32),
        ],
        axis=0,
    )
    packet_ref[2 * part :, :] = tags.astype(jnp.float32).astype(jnp.bfloat16)
    for i, ref in enumerate(factor_refs):
        factors_ref[i : i + 1, :] = ref[...]


def price_kernel(shocks_ref, loadings_ref, counts_ref, noise_ref, factors_ref, out_ref):
    rows = shocks_ref.shape[1]
    vol = factors_ref[0:1, :]
    drift = 0.5 * vol * vol
    mean = factors_ref[1:2, :]
    dev = factors_ref[2:3, :]
    loadings = loadings_ref[...]
    for i in range(0, rows, CHUNK):
        at = slice(i, i + CHUNK)
        level = jnp.zeros((CHUNK, vol.shape[1]), jnp.float32)
        for date in range(DATES):
            diffuse = jnp.dot(shocks_ref[date, at, :], loadings, preferred_element_type=jnp.float32)
            counts = counts_ref[date, at, :].astype(jnp.float32)
            noise = noise_ref[date, at, :].astype(jnp.float32)
            level = level + vol * diffuse - drift + counts * mean + jnp.sqrt(counts) * dev * noise
            out_ref[date * rows + i : date * rows + i + CHUNK, :] = (jnp.exp(level) - 1.0).astype(
                jnp.bfloat16
            )


def combine_kernel(part, held, flips, *refs):
    slot_ref, packet_refs = refs[0], refs[1:-5]
    own_ref, narrow_ref, other_ref, chosen_ref, marks_ref = refs[-5:]
    fac = lax.axis_index("fac")
    names = []
    for flip in (0, PRICE_FLIP, SIDE_FLIP, SIDE_FLIP ^ PRICE_FLIP):
        for h in range(held):
            slot = (fac ^ flip) * held + h

            def find(b, name):
                return jnp.where(slot_ref[b] == slot, b, name)

            names.append(lax.fori_loop(0, slot_ref.shape[0], find, 0, unroll=True).astype(jnp.float32))
    trades = packet_refs[0].shape[1]
    place = lax.broadcasted_iota(jnp.int32, (SET_DEV, trades), 0).astype(jnp.float32)
    for source, packet_ref in enumerate(packet_refs):
        at = slice(source * trades, (source + 1) * trades)
        tags = packet_ref[2 * part :, :].astype(jnp.float32)
        weights = [packet_ref[k * part : (k + 1) * part, :].astype(jnp.float32) for k in range(2)]
        for b, name in enumerate(names):
            picked = jnp.where(tags[0:1] == name, weights[0], 0.0)
            picked = jnp.where(tags[1:2] == name, weights[1], picked)
            chosen_ref[b * part : (b + 1) * part, at] = picked.astype(jnp.bfloat16)
        for i, flip in enumerate(flips):
            owner = (fac ^ flip).astype(jnp.float32)
            local = jnp.where(tags[2:3] == owner, tags[3:4], -1.0)
            mark = jnp.where(local == place, 1.0, 0.0)
            marks_ref[i * SET_DEV : (i + 1) * SET_DEV, at] = mark.astype(jnp.bfloat16)
    sums = f32_dot(chosen_ref[...], marks_ref[...], NT)
    half = own_ref.shape[0]
    own_ref[...] = sums[:half]
    narrow_ref[...] = sums[:half].astype(jnp.bfloat16)
    other_ref[...] = sums[half:].astype(jnp.bfloat16)


def merge_kernel(*refs):
    part_refs, shares_ref = refs[:-1], refs[-1]
    rows, columns = part_refs[0].shape
    pair = 2 * SET_DEV
    for i in range(len(part_refs) // 2):
        own_ref, other_ref = part_refs[2 * i : 2 * i + 2]
        for at in range(0, columns, pair):
            own = own_ref[:, at : at + pair].astype(jnp.float32)
            other = pltpu.roll(other_ref[:, at : at + pair].astype(jnp.float32), SET_DEV, 1)
            shares_ref[i * rows : (i + 1) * rows, at : at + pair] = (own + other).astype(jnp.bfloat16)


def value_kernel(part, held, scen_count, *refs):
    cores_refs, price_refs = refs[:2], refs[2:4]
    out_refs, whole_ref = refs[4:-1], refs[-1]
    scen = lax.axis_index("scen")
    for i in range(scen_count):
        column = (scen ^ i) * part
        for b in range(2 * held):
            row = (i // 2 * 2 * held + b) * part
            at = pl.ds(pl.multiple_of(b * BLOCK + column, part), part)
            whole_ref[at, :] = cores_refs[i % 2][row : row + part, :].astype(jnp.float32)
    width = held * BLOCK
    total = None
    for i, price_ref in enumerate(price_refs):
        whole = whole_ref[i * width : (i + 1) * width, :].T.astype(jnp.bfloat16)
        term = f32_dot(whole, price_ref[...], NT)
        total = term if total is None else total + term
    for p, out_ref in enumerate(out_refs):
        out_ref[...] = total[p * SET_DEV : (p + 1) * SET_DEV].astype(out_ref.dtype)


def exposure_of(part_refs, date, rows):
    at = slice(date * rows, (date + 1) * rows)
    nets = part_refs[0][:, at]
    for ref in part_refs[1:]:
        nets = nets + ref[:, at].astype(jnp.float32)
    return jnp.maximum(nets, 0.0)


def totals_kernel(rows, *refs):
    for date in range(DATES):
        refs[-1][date] = jnp.sum(exposure_of(refs[:-1], date, rows), axis=1)


def expose_kernel(rows, *refs):
    for date in range(DATES):
        refs[-1][date] = exposure_of(refs[:-1], date, rows)


def from_partner(x, axis, flip):
    count = lax.axis_size(axis)
    return lax.ppermute(x, axis, [(i, i ^ flip) for i in range(count)])


def from_both(x, scen_flip, fac_flip):
    count = lax.axis_size("fac")
    pairs = [
        (i * count + j, (i ^ scen_flip) * count + (j ^ fac_flip))
        for i in range(lax.axis_size("scen"))
        for j in range(count)
    ]
    return lax.ppermute(x, ("scen", "fac"), pairs)


def body(
    shocks,
    loadings,
    vol,
    jump_counts,
    jump_noise,
    jump_mean,
    jump_vol,
    dependencies,
    block_slot,
    trade_weights,
    netting,
):
    fac_count = lax.axis_size("fac")
    scen_count = lax.axis_size("scen")
    rows = shocks.shape[1]
    width = loadings.shape[1]
    held = width // BLOCK
    trades = trade_weights.shape[0]
    part = BLOCK // scen_count
    column_flips = [i for i in range(fac_count) if not i & SIDE_FLIP]
    owner_flips = [i for i in range(fac_count) if not i & HALF_FLIP]

    pick = pl.pallas_call(
        functools.partial(pick_kernel, part),
        out_shape=jax.ShapeDtypeStruct((max(part, 16), BLOCK), jnp.bfloat16),
        out_specs=VMEM,
        compiler_params=PARAMS,
        cost_estimate=pl.CostEstimate(flops=10**10, bytes_accessed=0, transcendentals=0),
        name="pick",
    )()
    packet, factors = pl.pallas_call(
        functools.partial(pack_kernel, part),
        out_shape=[
            jax.ShapeDtypeStruct((2 * part + TAGS, trades), jnp.bfloat16),
            jax.ShapeDtypeStruct((3, width), jnp.float32),
        ],
        in_specs=[VMEM] * 7,
        out_specs=[VMEM] * 2,
        compiler_params=PARAMS,
        name="pack",
    )(
        pick,
        trade_weights,
        dependencies.T,
        netting[None],
        vol[None],
        jump_mean[None],
        jump_vol[None],
    )
    order = column_flips[1:2] + column_flips[:1:-1]
    packets = [packet] + [from_partner(packet, "fac", i) for i in order]

    packet, shocks = lax.optimization_barrier((packet, shocks))
    prices = pl.pallas_call(
        price_kernel,
        out_shape=jax.ShapeDtypeStruct((DATES * rows, width), jnp.bfloat16),
        in_specs=[VMEM] * 5,
        out_specs=VMEM,
        compiler_params=PARAMS,
        name="price",
    )(shocks, loadings, jump_counts, jump_noise, factors)
    share_shape = (2 * held * part, len(owner_flips) * SET_DEV)
    column_trades = len(column_flips) * trades
    own, narrow, other = pl.pallas_call(
        functools.partial(combine_kernel, part, held, owner_flips),
        out_shape=[
            jax.ShapeDtypeStruct(share_shape, jnp.float32),
            jax.ShapeDtypeStruct(share_shape, jnp.bfloat16),
            jax.ShapeDtypeStruct(share_shape, jnp.bfloat16),
        ],
        in_specs=[SMEM] + [VMEM] * len(packets),
        out_specs=[VMEM] * 3,
        scratch_shapes=[
            pltpu.VMEM((2 * share_shape[0], column_trades), jnp.bfloat16),
            pltpu.VMEM((share_shape[1], column_trades), jnp.bfloat16),
        ],
        compiler_params=PARAMS,
        cost_estimate=pl.CostEstimate(flops=10**9, bytes_accessed=0, transcendentals=0),
        name="combine",
    )(block_slot, *packets)
    pair_prices = [prices, from_partner(prices, "fac", PRICE_FLIP)]
    parts = []
    for i in range(0, scen_count, 2):
        parts.append(from_partner(narrow, "scen", i) if i else own)
        parts.append(from_both(other, i, SIDE_FLIP))
    shares = pl.pallas_call(
        merge_kernel,
        out_shape=jax.ShapeDtypeStruct((len(parts) // 2 * share_shape[0], share_shape[1]), jnp.bfloat16),
        in_specs=[VMEM] * len(parts),
        out_specs=VMEM,
        compiler_params=PARAMS,
        name="merge",
    )(*parts)
    shares = [shares, from_partner(shares, "scen", 1)]

    parts = pl.pallas_call(
        functools.partial(value_kernel, part, held, scen_count),
        out_shape=[
            jax.ShapeDtypeStruct((SET_DEV, DATES * rows), jnp.bfloat16 if flip else jnp.float32)
            for flip in owner_flips
        ],
        in_specs=[VMEM] * 4,
        out_specs=[VMEM] * len(owner_flips),
        scratch_shapes=[pltpu.VMEM((2 * width, share_shape[1]), jnp.float32)],
        compiler_params=PARAMS,
        name="value",
    )(*shares, *pair_prices)
    sends = list(zip(parts[1:], owner_flips[1:]))
    sends = sends[1:] + sends[:1]
    parts = [parts[0]] + [from_partner(x, "fac", i) for x, i in sends]

    totals = pl.pallas_call(
        functools.partial(totals_kernel, rows),
        out_shape=jax.ShapeDtypeStruct((DATES, SET_DEV), jnp.float32),
        in_specs=[VMEM] * len(parts),
        out_specs=VMEM,
        compiler_params=PARAMS,
        name="totals",
    )(*parts)
    exposure = pl.pallas_call(
        functools.partial(expose_kernel, rows),
        out_shape=jax.ShapeDtypeStruct((DATES, SET_DEV, rows), jnp.float32),
        in_specs=[VMEM] * len(parts),
        out_specs=VMEM,
        compiler_params=PARAMS,
        name="expose",
    )(*parts)
    sums = [totals] + [None] * (scen_count - 1)
    for i in [*range(1, scen_count, 2), *range(2, scen_count, 2)]:
        sums[i] = from_partner(totals, "scen", i)
    while len(sums) > 1:
        sums = [sums[i] + sums[i + 1] for i in range(0, len(sums), 2)]
    return (exposure, sums[0] / (rows * scen_count))


def solution(mesh):
    placed = (
        P(None, "scen", None),
        P(None, "fac"),
        P("fac"),
        P(None, "scen", "fac"),
        P(None, "scen", "fac"),
        P("fac"),
        P("fac"),
        P("fac", None),
        P(),
        P("fac", None, None),
        P("fac"),
    )
    return jax.shard_map(
        body,
        mesh=mesh,
        in_specs=placed,
        out_specs=(P(None, "fac", "scen"), P(None, "fac")),
        check_vma=False,
    )
```

```python
import functools

import jax
import jax.numpy as jnp
from jax import lax
from jax.experimental import pallas as pl
from jax.experimental.pallas import tpu as pltpu
from jax.sharding import PartitionSpec as P

BLOCK = 128
SET_DEV = 64
DATES = 2
SIDE_FLIP = 1
PRICE_FLIP = 6
HALF_FLIP = 4
TAGS = 16
CHUNK = 64

VMEM = pl.BlockSpec(memory_space=pltpu.VMEM)
HBM = pl.BlockSpec(memory_space=pltpu.HBM)
SMEM = pl.BlockSpec(memory_space=pltpu.SMEM)
PARAMS = pltpu.CompilerParams(vmem_limit_bytes=16 * 1024 * 1024)
NT = (((1,), (1,)), ((), ()))


def f32_dot(a, b, dims):
    return lax.dot_general(a, b, dims, preferred_element_type=jnp.float32)


def pick_kernel(part, pick_ref):
    row = lax.broadcasted_iota(jnp.int32, pick_ref.shape, 0)
    column = lax.broadcasted_iota(jnp.int32, pick_ref.shape, 1)
    pick = column == lax.axis_index("scen") * part + row
    pick_ref[...] = pick.astype(jnp.float32).astype(jnp.bfloat16)


def pack_kernel(part, *refs):
    pick_ref, weights_ref, deps_ref, netting_ref = refs[:4]
    factor_refs, packet_ref, factors_ref = refs[4:-2], refs[-2], refs[-1]
    for k in range(2):
        share = f32_dot(pick_ref[...], weights_ref[:, k, :], NT)
        packet_ref[k * part : (k + 1) * part, :] = share[:part].astype(jnp.bfloat16)
    netting = netting_ref[...]
    tags = jnp.concatenate(
        [
            deps_ref[...],
            netting // SET_DEV,
            netting % SET_DEV,
            jnp.zeros((TAGS - 4, netting.shape[1]), jnp.int32),
        ],
        axis=0,
    )
    packet_ref[2 * part :, :] = tags.astype(jnp.float32).astype(jnp.bfloat16)
    for i, ref in enumerate(factor_refs):
        factors_ref[i : i + 1, :] = ref[...]


def price_kernel(shocks_ref, loadings_ref, counts_ref, noise_ref, factors_ref, out_ref):
    rows = shocks_ref.shape[1]
    vol = factors_ref[0:1, :]
    drift = 0.5 * vol * vol
    mean = factors_ref[1:2, :]
    dev = factors_ref[2:3, :]
    loadings = loadings_ref[...]
    for i in range(0, rows, CHUNK):
        at = slice(i, i + CHUNK)
        level = jnp.zeros((CHUNK, vol.shape[1]), jnp.float32)
        for date in range(DATES):
            diffuse = jnp.dot(shocks_ref[date, at, :], loadings, preferred_element_type=jnp.float32)
            counts = counts_ref[date, at, :].astype(jnp.float32)
            noise = noise_ref[date, at, :].astype(jnp.float32)
            level = level + vol * diffuse - drift + counts * mean + jnp.sqrt(counts) * dev * noise
            out_ref[date * rows + i : date * rows + i + CHUNK, :] = (jnp.exp(level) - 1.0).astype(
                jnp.bfloat16
            )


def combine_kernel(part, held, flips, *refs):
    slot_ref, packet_refs = refs[0], refs[1:-5]
    own_ref, narrow_ref, other_ref, chosen_ref, marks_ref = refs[-5:]
    fac = lax.axis_index("fac")
    names = []
    for flip in (0, PRICE_FLIP, SIDE_FLIP, SIDE_FLIP ^ PRICE_FLIP):
        for h in range(held):
            slot = (fac ^ flip) * held + h

            def find(b, name):
                return jnp.where(slot_ref[b] == slot, b, name)

            names.append(lax.fori_loop(0, slot_ref.shape[0], find, 0, unroll=True).astype(jnp.float32))
    trades = packet_refs[0].shape[1]
    place = lax.broadcasted_iota(jnp.int32, (SET_DEV, trades), 0).astype(jnp.float32)
    for source, packet_ref in enumerate(packet_refs):
        at = slice(source * trades, (source + 1) * trades)
        tags = packet_ref[2 * part :, :].astype(jnp.float32)
        weights = [packet_ref[k * part : (k + 1) * part, :].astype(jnp.float32) for k in range(2)]
        for b, name in enumerate(names):
            picked = jnp.where(tags[0:1] == name, weights[0], 0.0)
            picked = jnp.where(tags[1:2] == name, weights[1], picked)
            chosen_ref[b * part : (b + 1) * part, at] = picked.astype(jnp.bfloat16)
        for i, flip in enumerate(flips):
            owner = (fac ^ flip).astype(jnp.float32)
            local = jnp.where(tags[2:3] == owner, tags[3:4], -1.0)
            mark = jnp.where(local == place, 1.0, 0.0)
            marks_ref[i * SET_DEV : (i + 1) * SET_DEV, at] = mark.astype(jnp.bfloat16)
    sums = f32_dot(chosen_ref[...], marks_ref[...], NT)
    half = own_ref.shape[0]
    own_ref[...] = sums[:half]
    narrow_ref[...] = sums[:half].astype(jnp.bfloat16)
    other_ref[...] = sums[half:].astype(jnp.bfloat16)


def merge_kernel(*refs):
    part_refs, shares_ref = refs[:-1], refs[-1]
    rows, columns = part_refs[0].shape
    pair = 2 * SET_DEV
    for i in range(len(part_refs) // 2):
        own_ref, other_ref = part_refs[2 * i : 2 * i + 2]
        for at in range(0, columns, pair):
            own = own_ref[:, at : at + pair].astype(jnp.float32)
            other = pltpu.roll(other_ref[:, at : at + pair].astype(jnp.float32), SET_DEV, 1)
            shares_ref[i * rows : (i + 1) * rows, at : at + pair] = (own + other).astype(jnp.bfloat16)


def value_kernel(part, held, scen_count, *refs):
    cores_refs, price_refs = refs[:2], refs[2:4]
    out_refs, whole_ref = refs[4:-1], refs[-1]
    scen = lax.axis_index("scen")
    for i in range(scen_count):
        column = (scen ^ i) * part
        for b in range(2 * held):
            row = (i // 2 * 2 * held + b) * part
            at = pl.ds(pl.multiple_of(b * BLOCK + column, part), part)
            whole_ref[at, :] = cores_refs[i % 2][row : row + part, :].astype(jnp.float32)
    width = held * BLOCK
    total = None
    for i, price_ref in enumerate(price_refs):
        whole = whole_ref[i * width : (i + 1) * width, :].T.astype(jnp.bfloat16)
        term = f32_dot(whole, price_ref[...], NT)
        total = term if total is None else total + term
    for p, out_ref in enumerate(out_refs):
        out_ref[...] = total[p * SET_DEV : (p + 1) * SET_DEV].astype(out_ref.dtype)


def exposure_of(part_refs, date, rows):
    at = slice(date * rows, (date + 1) * rows)
    nets = part_refs[0][:, at]
    for ref in part_refs[1:]:
        nets = nets + ref[:, at].astype(jnp.float32)
    return jnp.maximum(nets, 0.0)


def totals_kernel(rows, *refs):
    for date in range(DATES):
        refs[-1][date] = jnp.sum(exposure_of(refs[:-1], date, rows), axis=1)


def expose_kernel(rows, *refs):
    for date in range(DATES):
        refs[-1][date] = exposure_of(refs[:-1], date, rows)


def from_partner(x, axis, flip):
    count = lax.axis_size(axis)
    return lax.ppermute(x, axis, [(i, i ^ flip) for i in range(count)])


def from_both(x, scen_flip, fac_flip):
    count = lax.axis_size("fac")
    pairs = [
        (i * count + j, (i ^ scen_flip) * count + (j ^ fac_flip))
        for i in range(lax.axis_size("scen"))
        for j in range(count)
    ]
    return lax.ppermute(x, ("scen", "fac"), pairs)


def body(
    shocks,
    loadings,
    vol,
    jump_counts,
    jump_noise,
    jump_mean,
    jump_vol,
    dependencies,
    block_slot,
    trade_weights,
    netting,
):
    fac_count = lax.axis_size("fac")
    scen_count = lax.axis_size("scen")
    rows = shocks.shape[1]
    width = loadings.shape[1]
    held = width // BLOCK
    trades = trade_weights.shape[0]
    part = BLOCK // scen_count
    column_flips = [i for i in range(fac_count) if not i & SIDE_FLIP]
    owner_flips = [i for i in range(fac_count) if not i & HALF_FLIP]

    pick = pl.pallas_call(
        functools.partial(pick_kernel, part),
        out_shape=jax.ShapeDtypeStruct((max(part, 16), BLOCK), jnp.bfloat16),
        out_specs=VMEM,
        compiler_params=PARAMS,
        cost_estimate=pl.CostEstimate(flops=10**10, bytes_accessed=0, transcendentals=0),
        name="pick",
    )()
    packet, factors = pl.pallas_call(
        functools.partial(pack_kernel, part),
        out_shape=[
            jax.ShapeDtypeStruct((2 * part + TAGS, trades), jnp.bfloat16),
            jax.ShapeDtypeStruct((3, width), jnp.float32),
        ],
        in_specs=[VMEM] * 7,
        out_specs=[VMEM] * 2,
        compiler_params=PARAMS,
        name="pack",
    )(
        pick,
        trade_weights,
        dependencies.T,
        netting[None],
        vol[None],
        jump_mean[None],
        jump_vol[None],
    )
    order = column_flips[1:2] + column_flips[:1:-1]
    packets = [packet] + [from_partner(packet, "fac", i) for i in order]

    packet, shocks = lax.optimization_barrier((packet, shocks))
    prices = pl.pallas_call(
        price_kernel,
        out_shape=jax.ShapeDtypeStruct((DATES * rows, width), jnp.bfloat16),
        in_specs=[VMEM] * 5,
        out_specs=VMEM,
        compiler_params=PARAMS,
        name="price",
    )(shocks, loadings, jump_counts, jump_noise, factors)
    share_shape = (2 * held * part, len(owner_flips) * SET_DEV)
    column_trades = len(column_flips) * trades
    own, narrow, other = pl.pallas_call(
        functools.partial(combine_kernel, part, held, owner_flips),
        out_shape=[
            jax.ShapeDtypeStruct(share_shape, jnp.float32),
            jax.ShapeDtypeStruct(share_shape, jnp.bfloat16),
            jax.ShapeDtypeStruct(share_shape, jnp.bfloat16),
        ],
        in_specs=[SMEM] + [VMEM] * len(packets),
        out_specs=[VMEM] * 3,
        scratch_shapes=[
            pltpu.VMEM((2 * share_shape[0], column_trades), jnp.bfloat16),
            pltpu.VMEM((share_shape[1], column_trades), jnp.bfloat16),
        ],
        compiler_params=PARAMS,
        cost_estimate=pl.CostEstimate(flops=10**9, bytes_accessed=0, transcendentals=0),
        name="combine",
    )(block_slot, *packets)
    pair_prices = [prices, from_partner(prices, "fac", PRICE_FLIP)]
    parts = []
    for i in range(0, scen_count, 2):
        parts.append(from_partner(narrow, "scen", i) if i else own)
        parts.append(from_both(other, i, SIDE_FLIP))
    shares = pl.pallas_call(
        merge_kernel,
        out_shape=jax.ShapeDtypeStruct((len(parts) // 2 * share_shape[0], share_shape[1]), jnp.bfloat16),
        in_specs=[VMEM] * len(parts),
        out_specs=VMEM,
        compiler_params=PARAMS,
        name="merge",
    )(*parts)
    shares = [shares, from_partner(shares, "scen", 1)]

    parts = pl.pallas_call(
        functools.partial(value_kernel, part, held, scen_count),
        out_shape=[
            jax.ShapeDtypeStruct((SET_DEV, DATES * rows), jnp.bfloat16 if flip else jnp.float32)
            for flip in owner_flips
        ],
        in_specs=[VMEM] * 4,
        out_specs=[VMEM] * len(owner_flips),
        scratch_shapes=[pltpu.VMEM((2 * width, share_shape[1]), jnp.float32)],
        compiler_params=PARAMS,
        name="value",
    )(*shares, *pair_prices)
    sends = list(zip(parts[1:], owner_flips[1:]))
    sends = sends[::-1]
    parts = [parts[0]] + [from_partner(x, "fac", i) for x, i in sends]

    totals = pl.pallas_call(
        functools.partial(totals_kernel, rows),
        out_shape=jax.ShapeDtypeStruct((DATES, SET_DEV), jnp.float32),
        in_specs=[VMEM] * len(parts),
        out_specs=VMEM,
        compiler_params=PARAMS,
        name="totals",
    )(*parts)
    exposure = pl.pallas_call(
        functools.partial(expose_kernel, rows),
        out_shape=jax.ShapeDtypeStruct((DATES, SET_DEV, rows), jnp.float32),
        in_specs=[VMEM] * len(parts),
        out_specs=VMEM,
        compiler_params=PARAMS,
        name="expose",
    )(*parts)
    sums = [totals] + [None] * (scen_count - 1)
    for i in [*range(1, scen_count, 2), *range(2, scen_count, 2)]:
        sums[i] = from_partner(totals, "scen", i)
    while len(sums) > 1:
        sums = [sums[i] + sums[i + 1] for i in range(0, len(sums), 2)]
    return (exposure, sums[0] / (rows * scen_count))


def solution(mesh):
    placed = (
        P(None, "scen", None),
        P(None, "fac"),
        P("fac"),
        P(None, "scen", "fac"),
        P(None, "scen", "fac"),
        P("fac"),
        P("fac"),
        P("fac", None),
        P(),
        P("fac", None, None),
        P("fac"),
    )
    return jax.shard_map(
        body,
        mesh=mesh,
        in_specs=placed,
        out_specs=(P(None, "fac", "scen"), P(None, "fac")),
        check_vma=False,
    )
```

```python
import functools

import jax
import jax.numpy as jnp
from jax import lax
from jax.experimental import pallas as pl
from jax.experimental.pallas import tpu as pltpu
from jax.sharding import PartitionSpec as P

BLOCK = 128
SET_DEV = 64
DATES = 2
SIDE_FLIP = 1
PRICE_FLIP = 6
HALF_FLIP = 4
TAGS = 16
CHUNK = 64

VMEM = pl.BlockSpec(memory_space=pltpu.VMEM)
HBM = pl.BlockSpec(memory_space=pltpu.HBM)
SMEM = pl.BlockSpec(memory_space=pltpu.SMEM)
PARAMS = pltpu.CompilerParams(vmem_limit_bytes=16 * 1024 * 1024)
NT = (((1,), (1,)), ((), ()))


def f32_dot(a, b, dims):
    return lax.dot_general(a, b, dims, preferred_element_type=jnp.float32)


def pick_kernel(part, pick_ref):
    row = lax.broadcasted_iota(jnp.int32, pick_ref.shape, 0)
    column = lax.broadcasted_iota(jnp.int32, pick_ref.shape, 1)
    pick = column == lax.axis_index("scen") * part + row
    pick_ref[...] = pick.astype(jnp.float32).astype(jnp.bfloat16)


def pack_kernel(part, *refs):
    pick_ref, weights_ref, deps_ref, netting_ref = refs[:4]
    factor_refs, packet_ref, factors_ref = refs[4:-2], refs[-2], refs[-1]
    for k in range(2):
        share = f32_dot(pick_ref[...], weights_ref[:, k, :], NT)
        packet_ref[k * part : (k + 1) * part, :] = share[:part].astype(jnp.bfloat16)
    netting = netting_ref[...]
    tags = jnp.concatenate(
        [
            deps_ref[...],
            netting // SET_DEV,
            netting % SET_DEV,
            jnp.zeros((TAGS - 4, netting.shape[1]), jnp.int32),
        ],
        axis=0,
    )
    packet_ref[2 * part :, :] = tags.astype(jnp.float32).astype(jnp.bfloat16)
    for i, ref in enumerate(factor_refs):
        factors_ref[i : i + 1, :] = ref[...]


def price_kernel(shocks_ref, loadings_ref, counts_ref, noise_ref, factors_ref, out_ref):
    rows = shocks_ref.shape[1]
    vol = factors_ref[0:1, :]
    drift = 0.5 * vol * vol
    mean = factors_ref[1:2, :]
    dev = factors_ref[2:3, :]
    loadings = loadings_ref[...]
    for i in range(0, rows, CHUNK):
        at = slice(i, i + CHUNK)
        level = jnp.zeros((CHUNK, vol.shape[1]), jnp.float32)
        for date in range(DATES):
            diffuse = jnp.dot(shocks_ref[date, at, :], loadings, preferred_element_type=jnp.float32)
            counts = counts_ref[date, at, :].astype(jnp.float32)
            noise = noise_ref[date, at, :].astype(jnp.float32)
            level = level + vol * diffuse - drift + counts * mean + jnp.sqrt(counts) * dev * noise
            out_ref[date * rows + i : date * rows + i + CHUNK, :] = (jnp.exp(level) - 1.0).astype(
                jnp.bfloat16
            )


def combine_kernel(part, held, flips, *refs):
    slot_ref, packet_refs = refs[0], refs[1:-5]
    own_ref, narrow_ref, other_ref, chosen_ref, marks_ref = refs[-5:]
    fac = lax.axis_index("fac")
    names = []
    for flip in (0, PRICE_FLIP, SIDE_FLIP, SIDE_FLIP ^ PRICE_FLIP):
        for h in range(held):
            slot = (fac ^ flip) * held + h

            def find(b, name):
                return jnp.where(slot_ref[b] == slot, b, name)

            names.append(lax.fori_loop(0, slot_ref.shape[0], find, 0, unroll=True).astype(jnp.float32))
    trades = packet_refs[0].shape[1]
    place = lax.broadcasted_iota(jnp.int32, (SET_DEV, trades), 0).astype(jnp.float32)
    for source, packet_ref in enumerate(packet_refs):
        at = slice(source * trades, (source + 1) * trades)
        tags = packet_ref[2 * part :, :].astype(jnp.float32)
        weights = [packet_ref[k * part : (k + 1) * part, :].astype(jnp.float32) for k in range(2)]
        for b, name in enumerate(names):
            picked = jnp.where(tags[0:1] == name, weights[0], 0.0)
            picked = jnp.where(tags[1:2] == name, weights[1], picked)
            chosen_ref[b * part : (b + 1) * part, at] = picked.astype(jnp.bfloat16)
        for i, flip in enumerate(flips):
            owner = (fac ^ flip).astype(jnp.float32)
            local = jnp.where(tags[2:3] == owner, tags[3:4], -1.0)
            mark = jnp.where(local == place, 1.0, 0.0)
            marks_ref[i * SET_DEV : (i + 1) * SET_DEV, at] = mark.astype(jnp.bfloat16)
    sums = f32_dot(chosen_ref[...], marks_ref[...], NT)
    half = own_ref.shape[0]
    own_ref[...] = sums[:half]
    narrow_ref[...] = sums[:half].astype(jnp.bfloat16)
    other_ref[...] = sums[half:].astype(jnp.bfloat16)


def merge_kernel(*refs):
    part_refs, shares_ref = refs[:-1], refs[-1]
    rows, columns = part_refs[0].shape
    pair = 2 * SET_DEV
    for i in range(len(part_refs) // 2):
        own_ref, other_ref = part_refs[2 * i : 2 * i + 2]
        for at in range(0, columns, pair):
            own = own_ref[:, at : at + pair].astype(jnp.float32)
            other = pltpu.roll(other_ref[:, at : at + pair].astype(jnp.float32), SET_DEV, 1)
            shares_ref[i * rows : (i + 1) * rows, at : at + pair] = (own + other).astype(jnp.bfloat16)


def value_kernel(part, held, scen_count, *refs):
    cores_refs, price_refs = refs[:2], refs[2:4]
    out_refs, whole_ref = refs[4:-1], refs[-1]
    scen = lax.axis_index("scen")
    for i in range(scen_count):
        column = (scen ^ i) * part
        for b in range(2 * held):
            row = (i // 2 * 2 * held + b) * part
            at = pl.ds(pl.multiple_of(b * BLOCK + column, part), part)
            whole_ref[at, :] = cores_refs[i % 2][row : row + part, :].astype(jnp.float32)
    width = held * BLOCK
    total = None
    for i, price_ref in enumerate(price_refs):
        whole = whole_ref[i * width : (i + 1) * width, :].T.astype(jnp.bfloat16)
        term = f32_dot(whole, price_ref[...], NT)
        total = term if total is None else total + term
    for p, out_ref in enumerate(out_refs):
        out_ref[...] = total[p * SET_DEV : (p + 1) * SET_DEV].astype(out_ref.dtype)


def exposure_of(part_refs, date, rows):
    at = slice(date * rows, (date + 1) * rows)
    nets = part_refs[0][:, at]
    for ref in part_refs[1:]:
        nets = nets + ref[:, at].astype(jnp.float32)
    return jnp.maximum(nets, 0.0)


def totals_kernel(rows, *refs):
    for date in range(DATES):
        refs[-1][date] = jnp.sum(exposure_of(refs[:-1], date, rows), axis=1)


def expose_kernel(rows, *refs):
    for date in range(DATES):
        refs[-1][date] = exposure_of(refs[:-1], date, rows)


def from_partner(x, axis, flip):
    count = lax.axis_size(axis)
    return lax.ppermute(x, axis, [(i, i ^ flip) for i in range(count)])


def from_both(x, scen_flip, fac_flip):
    count = lax.axis_size("fac")
    pairs = [
        (i * count + j, (i ^ scen_flip) * count + (j ^ fac_flip))
        for i in range(lax.axis_size("scen"))
        for j in range(count)
    ]
    return lax.ppermute(x, ("scen", "fac"), pairs)


def body(
    shocks,
    loadings,
    vol,
    jump_counts,
    jump_noise,
    jump_mean,
    jump_vol,
    dependencies,
    block_slot,
    trade_weights,
    netting,
):
    fac_count = lax.axis_size("fac")
    scen_count = lax.axis_size("scen")
    rows = shocks.shape[1]
    width = loadings.shape[1]
    held = width // BLOCK
    trades = trade_weights.shape[0]
    part = BLOCK // scen_count
    column_flips = [i for i in range(fac_count) if not i & SIDE_FLIP]
    owner_flips = [i for i in range(fac_count) if not i & HALF_FLIP]

    pick = pl.pallas_call(
        functools.partial(pick_kernel, part),
        out_shape=jax.ShapeDtypeStruct((max(part, 16), BLOCK), jnp.bfloat16),
        out_specs=VMEM,
        compiler_params=PARAMS,
        cost_estimate=pl.CostEstimate(flops=10**10, bytes_accessed=0, transcendentals=0),
        name="pick",
    )()
    packet, factors = pl.pallas_call(
        functools.partial(pack_kernel, part),
        out_shape=[
            jax.ShapeDtypeStruct((2 * part + TAGS, trades), jnp.bfloat16),
            jax.ShapeDtypeStruct((3, width), jnp.float32),
        ],
        in_specs=[VMEM] * 7,
        out_specs=[VMEM] * 2,
        compiler_params=PARAMS,
        name="pack",
    )(
        pick,
        trade_weights,
        dependencies.T,
        netting[None],
        vol[None],
        jump_mean[None],
        jump_vol[None],
    )
    packets = [packet] + [from_partner(packet, "fac", i) for i in column_flips[1:]]

    packet, shocks = lax.optimization_barrier((packet, shocks))
    prices = pl.pallas_call(
        price_kernel,
        out_shape=jax.ShapeDtypeStruct((DATES * rows, width), jnp.bfloat16),
        in_specs=[VMEM] * 5,
        out_specs=VMEM,
        compiler_params=PARAMS,
        name="price",
    )(shocks, loadings, jump_counts, jump_noise, factors)
    share_shape = (2 * held * part, len(owner_flips) * SET_DEV)
    column_trades = len(column_flips) * trades
    own, narrow, other = pl.pallas_call(
        functools.partial(combine_kernel, part, held, owner_flips),
        out_shape=[
            jax.ShapeDtypeStruct(share_shape, jnp.float32),
            jax.ShapeDtypeStruct(share_shape, jnp.bfloat16),
            jax.ShapeDtypeStruct(share_shape, jnp.bfloat16),
        ],
        in_specs=[SMEM] + [VMEM] * len(packets),
        out_specs=[VMEM] * 3,
        scratch_shapes=[
            pltpu.VMEM((2 * share_shape[0], column_trades), jnp.bfloat16),
            pltpu.VMEM((share_shape[1], column_trades), jnp.bfloat16),
        ],
        compiler_params=PARAMS,
        cost_estimate=pl.CostEstimate(flops=10**9, bytes_accessed=0, transcendentals=0),
        name="combine",
    )(block_slot, *packets)
    pair_prices = [prices, from_partner(prices, "fac", PRICE_FLIP)]
    parts = []
    for i in range(0, scen_count, 2):
        parts.append(from_partner(narrow, "scen", i) if i else own)
        parts.append(from_both(other, i, SIDE_FLIP))
    shares = pl.pallas_call(
        merge_kernel,
        out_shape=jax.ShapeDtypeStruct((len(parts) // 2 * share_shape[0], share_shape[1]), jnp.bfloat16),
        in_specs=[VMEM] * len(parts),
        out_specs=VMEM,
        compiler_params=PARAMS,
        name="merge",
    )(*parts)
    shares = [shares, from_partner(shares, "scen", 1)]

    parts = pl.pallas_call(
        functools.partial(value_kernel, part, held, scen_count),
        out_shape=[
            jax.ShapeDtypeStruct((SET_DEV, DATES * rows), jnp.bfloat16 if flip else jnp.float32)
            for flip in owner_flips
        ],
        in_specs=[VMEM] * 4,
        out_specs=[VMEM] * len(owner_flips),
        scratch_shapes=[pltpu.VMEM((2 * width, share_shape[1]), jnp.float32)],
        compiler_params=PARAMS,
        name="value",
    )(*shares, *pair_prices)
    sends = list(zip(parts[1:], owner_flips[1:]))
    sends = sends[::-1]
    parts = [parts[0]] + [from_partner(x, "fac", i) for x, i in sends]

    totals = pl.pallas_call(
        functools.partial(totals_kernel, rows),
        out_shape=jax.ShapeDtypeStruct((DATES, SET_DEV), jnp.float32),
        in_specs=[VMEM] * len(parts),
        out_specs=VMEM,
        compiler_params=PARAMS,
        name="totals",
    )(*parts)
    exposure = pl.pallas_call(
        functools.partial(expose_kernel, rows),
        out_shape=jax.ShapeDtypeStruct((DATES, SET_DEV, rows), jnp.float32),
        in_specs=[VMEM] * len(parts),
        out_specs=VMEM,
        compiler_params=PARAMS,
        name="expose",
    )(*parts)
    sums = [totals] + [None] * (scen_count - 1)
    for i in [*range(1, scen_count, 2), *range(2, scen_count, 2)]:
        sums[i] = from_partner(totals, "scen", i)
    while len(sums) > 1:
        sums = [sums[i] + sums[i + 1] for i in range(0, len(sums), 2)]
    return (exposure, sums[0] / (rows * scen_count))


def solution(mesh):
    placed = (
        P(None, "scen", None),
        P(None, "fac"),
        P("fac"),
        P(None, "scen", "fac"),
        P(None, "scen", "fac"),
        P("fac"),
        P("fac"),
        P("fac", None),
        P(),
        P("fac", None, None),
        P("fac"),
    )
    return jax.shard_map(
        body,
        mesh=mesh,
        in_specs=placed,
        out_specs=(P(None, "fac", "scen"), P(None, "fac")),
        check_vma=False,
    )
```

```python
import functools

import jax
import jax.numpy as jnp
from jax import lax
from jax.experimental import pallas as pl
from jax.experimental.pallas import tpu as pltpu
from jax.sharding import PartitionSpec as P

BLOCK = 128
SET_DEV = 64
DATES = 2
SIDE_FLIP = 1
PRICE_FLIP = 6
HALF_FLIP = 4
TAGS = 16
CHUNK = 64

VMEM = pl.BlockSpec(memory_space=pltpu.VMEM)
HBM = pl.BlockSpec(memory_space=pltpu.HBM)
SMEM = pl.BlockSpec(memory_space=pltpu.SMEM)
PARAMS = pltpu.CompilerParams(vmem_limit_bytes=16 * 1024 * 1024)
NT = (((1,), (1,)), ((), ()))


def f32_dot(a, b, dims):
    return lax.dot_general(a, b, dims, preferred_element_type=jnp.float32)


def pick_kernel(part, pick_ref):
    row = lax.broadcasted_iota(jnp.int32, pick_ref.shape, 0)
    column = lax.broadcasted_iota(jnp.int32, pick_ref.shape, 1)
    pick = column == lax.axis_index("scen") * part + row
    pick_ref[...] = pick.astype(jnp.float32).astype(jnp.bfloat16)


def pack_kernel(part, *refs):
    slot_ref, pick_ref, weights_ref, deps_ref, netting_ref = refs[:5]
    factor_refs, packet_ref, factors_ref = refs[5:-2], refs[-2], refs[-1]
    for k in range(2):
        share = f32_dot(pick_ref[...], weights_ref[:, k, :], NT)
        packet_ref[k * part : (k + 1) * part, :] = share[:part].astype(jnp.bfloat16)
    netting = netting_ref[...]
    slots = jnp.zeros_like(deps_ref[...])
    for b in range(slot_ref.shape[0]):
        slots = jnp.where(deps_ref[...] == b, slot_ref[b], slots)
    tags = jnp.concatenate(
        [
            slots,
            netting // SET_DEV,
            netting % SET_DEV,
            jnp.zeros((TAGS - 4, netting.shape[1]), jnp.int32),
        ],
        axis=0,
    )
    packet_ref[2 * part :, :] = tags.astype(jnp.float32).astype(jnp.bfloat16)
    for i, ref in enumerate(factor_refs):
        factors_ref[i : i + 1, :] = ref[...]


def price_kernel(shocks_ref, loadings_ref, counts_ref, noise_ref, factors_ref, out_ref):
    rows = shocks_ref.shape[1]
    vol = factors_ref[0:1, :]
    drift = 0.5 * vol * vol
    mean = factors_ref[1:2, :]
    dev = factors_ref[2:3, :]
    loadings = loadings_ref[...]
    for i in range(0, rows, CHUNK):
        at = slice(i, i + CHUNK)
        level = jnp.zeros((CHUNK, vol.shape[1]), jnp.float32)
        for date in range(DATES):
            diffuse = jnp.dot(shocks_ref[date, at, :], loadings, preferred_element_type=jnp.float32)
            counts = counts_ref[date, at, :].astype(jnp.float32)
            noise = noise_ref[date, at, :].astype(jnp.float32)
            level = level + vol * diffuse - drift + counts * mean + jnp.sqrt(counts) * dev * noise
            out_ref[date * rows + i : date * rows + i + CHUNK, :] = (jnp.exp(level) - 1.0).astype(
                jnp.bfloat16
            )


def combine_kernel(part, held, flips, *refs):
    packet_refs = refs[:-5]
    own_ref, narrow_ref, other_ref, chosen_ref, marks_ref = refs[-5:]
    fac = lax.axis_index("fac")
    names = []
    for flip in (0, PRICE_FLIP, SIDE_FLIP, SIDE_FLIP ^ PRICE_FLIP):
        for h in range(held):
            names.append(((fac ^ flip) * held + h).astype(jnp.float32))
    trades = packet_refs[0].shape[1]
    place = lax.broadcasted_iota(jnp.int32, (SET_DEV, trades), 0).astype(jnp.float32)
    for source, packet_ref in enumerate(packet_refs):
        at = slice(source * trades, (source + 1) * trades)
        tags = packet_ref[2 * part :, :].astype(jnp.float32)
        weights = [packet_ref[k * part : (k + 1) * part, :].astype(jnp.float32) for k in range(2)]
        for b, name in enumerate(names):
            picked = jnp.where(tags[0:1] == name, weights[0], 0.0)
            picked = jnp.where(tags[1:2] == name, weights[1], picked)
            chosen_ref[b * part : (b + 1) * part, at] = picked.astype(jnp.bfloat16)
        for i, flip in enumerate(flips):
            owner = (fac ^ flip).astype(jnp.float32)
            local = jnp.where(tags[2:3] == owner, tags[3:4], -1.0)
            mark = jnp.where(local == place, 1.0, 0.0)
            marks_ref[i * SET_DEV : (i + 1) * SET_DEV, at] = mark.astype(jnp.bfloat16)
    sums = f32_dot(chosen_ref[...], marks_ref[...], NT)
    half = own_ref.shape[0]
    own_ref[...] = sums[:half]
    narrow_ref[...] = sums[:half].astype(jnp.bfloat16)
    other_ref[...] = sums[half:].astype(jnp.bfloat16)


def merge_kernel(*refs):
    part_refs, shares_ref = refs[:-1], refs[-1]
    rows, columns = part_refs[0].shape
    pair = 2 * SET_DEV
    for i in range(len(part_refs) // 2):
        own_ref, other_ref = part_refs[2 * i : 2 * i + 2]
        for at in range(0, columns, pair):
            own = own_ref[:, at : at + pair].astype(jnp.float32)
            other = pltpu.roll(other_ref[:, at : at + pair].astype(jnp.float32), SET_DEV, 1)
            shares_ref[i * rows : (i + 1) * rows, at : at + pair] = (own + other).astype(jnp.bfloat16)


def value_kernel(part, held, scen_count, *refs):
    cores_refs, price_refs = refs[:2], refs[2:4]
    out_refs, whole_ref = refs[4:-1], refs[-1]
    scen = lax.axis_index("scen")
    for i in range(scen_count):
        column = (scen ^ i) * part
        for b in range(2 * held):
            row = (i // 2 * 2 * held + b) * part
            at = pl.ds(pl.multiple_of(b * BLOCK + column, part), part)
            whole_ref[at, :] = cores_refs[i % 2][row : row + part, :].astype(jnp.float32)
    width = held * BLOCK
    total = None
    for i, price_ref in enumerate(price_refs):
        whole = whole_ref[i * width : (i + 1) * width, :].T.astype(jnp.bfloat16)
        term = f32_dot(whole, price_ref[...], NT)
        total = term if total is None else total + term
    for p, out_ref in enumerate(out_refs):
        out_ref[...] = total[p * SET_DEV : (p + 1) * SET_DEV].astype(out_ref.dtype)


def exposure_of(part_refs, date, rows):
    at = slice(date * rows, (date + 1) * rows)
    nets = part_refs[0][:, at]
    for ref in part_refs[1:]:
        nets = nets + ref[:, at].astype(jnp.float32)
    return jnp.maximum(nets, 0.0)


def totals_kernel(rows, *refs):
    for date in range(DATES):
        refs[-1][date] = jnp.sum(exposure_of(refs[:-1], date, rows), axis=1)


def expose_kernel(rows, *refs):
    for date in range(DATES):
        refs[-1][date] = exposure_of(refs[:-1], date, rows)


def from_partner(x, axis, flip):
    count = lax.axis_size(axis)
    return lax.ppermute(x, axis, [(i, i ^ flip) for i in range(count)])


def from_both(x, scen_flip, fac_flip):
    count = lax.axis_size("fac")
    pairs = [
        (i * count + j, (i ^ scen_flip) * count + (j ^ fac_flip))
        for i in range(lax.axis_size("scen"))
        for j in range(count)
    ]
    return lax.ppermute(x, ("scen", "fac"), pairs)


def body(
    shocks,
    loadings,
    vol,
    jump_counts,
    jump_noise,
    jump_mean,
    jump_vol,
    dependencies,
    block_slot,
    trade_weights,
    netting,
):
    fac_count = lax.axis_size("fac")
    scen_count = lax.axis_size("scen")
    rows = shocks.shape[1]
    width = loadings.shape[1]
    held = width // BLOCK
    trades = trade_weights.shape[0]
    part = BLOCK // scen_count
    column_flips = [i for i in range(fac_count) if not i & SIDE_FLIP]
    owner_flips = [i for i in range(fac_count) if not i & HALF_FLIP]

    pick = pl.pallas_call(
        functools.partial(pick_kernel, part),
        out_shape=jax.ShapeDtypeStruct((max(part, 16), BLOCK), jnp.bfloat16),
        out_specs=VMEM,
        compiler_params=PARAMS,
        cost_estimate=pl.CostEstimate(flops=10**10, bytes_accessed=0, transcendentals=0),
        name="pick",
    )()
    packet, factors = pl.pallas_call(
        functools.partial(pack_kernel, part),
        out_shape=[
            jax.ShapeDtypeStruct((2 * part + TAGS, trades), jnp.bfloat16),
            jax.ShapeDtypeStruct((3, width), jnp.float32),
        ],
        in_specs=[SMEM] + [VMEM] * 7,
        out_specs=[VMEM] * 2,
        compiler_params=PARAMS,
        name="pack",
    )(
        block_slot,
        pick,
        trade_weights,
        dependencies.T,
        netting[None],
        vol[None],
        jump_mean[None],
        jump_vol[None],
    )
    order = column_flips[1:2] + column_flips[:1:-1]
    packets = [packet] + [from_partner(packet, "fac", i) for i in order]

    packet, shocks = lax.optimization_barrier((packet, shocks))
    prices = pl.pallas_call(
        price_kernel,
        out_shape=jax.ShapeDtypeStruct((DATES * rows, width), jnp.bfloat16),
        in_specs=[VMEM] * 5,
        out_specs=VMEM,
        compiler_params=PARAMS,
        name="price",
    )(shocks, loadings, jump_counts, jump_noise, factors)
    share_shape = (2 * held * part, len(owner_flips) * SET_DEV)
    column_trades = len(column_flips) * trades
    own, narrow, other = pl.pallas_call(
        functools.partial(combine_kernel, part, held, owner_flips),
        out_shape=[
            jax.ShapeDtypeStruct(share_shape, jnp.float32),
            jax.ShapeDtypeStruct(share_shape, jnp.bfloat16),
            jax.ShapeDtypeStruct(share_shape, jnp.bfloat16),
        ],
        in_specs=[VMEM] * len(packets),
        out_specs=[VMEM] * 3,
        scratch_shapes=[
            pltpu.VMEM((2 * share_shape[0], column_trades), jnp.bfloat16),
            pltpu.VMEM((share_shape[1], column_trades), jnp.bfloat16),
        ],
        compiler_params=PARAMS,
        cost_estimate=pl.CostEstimate(flops=10**9, bytes_accessed=0, transcendentals=0),
        name="combine",
    )(*packets)
    pair_prices = [prices, from_partner(prices, "fac", PRICE_FLIP)]
    parts = []
    for i in range(0, scen_count, 2):
        parts.append(from_partner(narrow, "scen", i) if i else own)
        parts.append(from_both(other, i, SIDE_FLIP))
    shares = pl.pallas_call(
        merge_kernel,
        out_shape=jax.ShapeDtypeStruct((len(parts) // 2 * share_shape[0], share_shape[1]), jnp.bfloat16),
        in_specs=[VMEM] * len(parts),
        out_specs=VMEM,
        compiler_params=PARAMS,
        name="merge",
    )(*parts)
    shares = [shares, from_partner(shares, "scen", 1)]

    parts = pl.pallas_call(
        functools.partial(value_kernel, part, held, scen_count),
        out_shape=[
            jax.ShapeDtypeStruct((SET_DEV, DATES * rows), jnp.bfloat16 if flip else jnp.float32)
            for flip in owner_flips
        ],
        in_specs=[VMEM] * 4,
        out_specs=[VMEM] * len(owner_flips),
        scratch_shapes=[pltpu.VMEM((2 * width, share_shape[1]), jnp.float32)],
        compiler_params=PARAMS,
        name="value",
    )(*shares, *pair_prices)
    sends = list(zip(parts[1:], owner_flips[1:]))
    sends = sends[::-1]
    parts = [parts[0]] + [from_partner(x, "fac", i) for x, i in sends]

    totals = pl.pallas_call(
        functools.partial(totals_kernel, rows),
        out_shape=jax.ShapeDtypeStruct((DATES, SET_DEV), jnp.float32),
        in_specs=[VMEM] * len(parts),
        out_specs=VMEM,
        compiler_params=PARAMS,
        name="totals",
    )(*parts)
    exposure = pl.pallas_call(
        functools.partial(expose_kernel, rows),
        out_shape=jax.ShapeDtypeStruct((DATES, SET_DEV, rows), jnp.float32),
        in_specs=[VMEM] * len(parts),
        out_specs=VMEM,
        compiler_params=PARAMS,
        name="expose",
    )(*parts)
    sums = [totals] + [None] * (scen_count - 1)
    for i in [*range(1, scen_count, 2), *range(2, scen_count, 2)]:
        sums[i] = from_partner(totals, "scen", i)
    while len(sums) > 1:
        sums = [sums[i] + sums[i + 1] for i in range(0, len(sums), 2)]
    return (exposure, sums[0] / (rows * scen_count))


def solution(mesh):
    placed = (
        P(None, "scen", None),
        P(None, "fac"),
        P("fac"),
        P(None, "scen", "fac"),
        P(None, "scen", "fac"),
        P("fac"),
        P("fac"),
        P("fac", None),
        P(),
        P("fac", None, None),
        P("fac"),
    )
    return jax.shard_map(
        body,
        mesh=mesh,
        in_specs=placed,
        out_specs=(P(None, "fac", "scen"), P(None, "fac")),
        check_vma=False,
    )
```
